32 devices in a mesh: batch: 8 (over z, y), patch: 4 (over x, core).
Axes of the slice: x: 2, y: 2, z: 4, core: 2. Of those that a mesh axis runs over, the one named last changes fastest.
Arguments:
- tokens: bfloat16 [8, 8, 256, 1024], P('batch', None, 'patch'), may hold values from -6 to 6
- cotangent: bfloat16 [8, 8, 256, 1024], P('batch', None, 'patch'), may hold values from -6 to 6
- episode_frames: int32 [8, 4], P('batch'), may hold values from 1 to 4, 8 in all within a row
- kinds: int32 [8, 8, 256], P('batch', None, 'patch'), may hold values from 0 to 2, as said below
- patch_pos: int32 [8, 8, 256], P('batch', None, 'patch'), may hold values from 0 to 255, each once within a row
- ln1_gain: bfloat16 [1024], replicated, may hold values from 0.5 to 1.5
- ln1_shift: bfloat16 [1024], replicated, may hold values from -3 to 3
- w_qkv: bfloat16 [1024, 3072], replicated, may hold values from -0.1875 to 0.1875
- w_out: bfloat16 [1024, 1024], replicated, may hold values from -1.5 to 1.5
- ln2_gain: bfloat16 [1024], replicated, may hold values from 0.5 to 1.5
- ln2_shift: bfloat16 [1024], replicated, may hold values from -3 to 3
- w_up: bfloat16 [1024, 4096], replicated, may hold values from -0.1875 to 0.1875
- w_down: bfloat16 [4096, 1024], replicated, may hold values from -0.09375 to 0.09375
Outputs:
- out: bfloat16 [8, 8, 256, 1024], P('batch', None, 'patch')
- grad_tokens: bfloat16 [8, 8, 256, 1024], P('batch', None, 'patch')
- grad_ln1_gain: float32 [1024], P('patch')
- grad_ln1_shift: float32 [1024], P('patch')
- grad_w_qkv: float32 [1024, 3072], P('patch')
- grad_w_out: float32 [1024, 1024], P('patch')
- grad_ln2_gain: float32 [1024], P('patch')
- grad_ln2_shift: float32 [1024], P('patch')
- grad_w_up: float32 [1024, 4096], P('patch')
- grad_w_down: float32 [4096, 1024], P('patch')
The draws below stay inside these ranges and needn't reach their ends.
Inputs may be any that keep to these rules, and one draw needn't show every extreme that they name: `episode_frames`: each group's 4 episodes have 1 or more frames, sum to 8, and the longest has exactly 4. `kinds`: in every frame exactly one slot holds 1 (action) and one holds 2 (state), both among the frame's first 64 slots; all other slots hold 0. `patch_pos`: each frame's values are a permutation of its slots' cells.
All inputs are finite; a program needn't handle non-finite values.
Results may differ from the reference program's by a relative error of at most 0.035.
Values may be sent and summed in bfloat16 or wider, within the bound.
No kernel may reach another device: no remote copies, remote signals or barrier semaphores. Data moves between devices by JAX's collectives and lax.ppermute only.
A program may use at most 320 MiB of HBM per device.

```python
import math
import jax
import jax.numpy as jnp
import numpy as np
from jax import lax

D = 1024
HEADS = 16
HD = 64
FF = 4096
FRAME_TOK = 256
GRID = 16
EPIS = 4
FRAMES = 8
PPD = 64
BATCHES = 8


def draw_kinds(key, part):
    key = jax.random.fold_in(key, 7)
    first_key, gap_key = jax.random.split(key)
    first = jax.random.randint(first_key, (BATCHES, FRAMES, 1), 0, PPD)
    gap = jax.random.randint(gap_key, (BATCHES, FRAMES, 1), 1, PPD)
    second = (first + gap) % PPD
    slots = jnp.arange(FRAME_TOK, dtype=jnp.int32)[None, None, :]
    marks = jnp.where(slots == first, 1, 0) + jnp.where(slots == second, 2, 0)
    return marks.astype(jnp.int32)


def block_levels(key, shape, cuts, least, high):
    loudness, own = 1.0, jax.random.fold_in(key, 6)
    for dim, shards_of in cuts:
        steps = jnp.exp(jax.random.uniform(jax.random.fold_in(own, dim), (shards_of,), jnp.float32, least / len(cuts), high / len(cuts)))
        loudness = loudness * jnp.repeat(steps, shape[dim] // shards_of).reshape([-1 if axis == dim else 1 for axis in range(len(shape))])
    return loudness


def profile(count, total, most, slope):
    loads = [(1 << 20) // math.isqrt(grade ** slope) + 1 for grade in range(2, count + 1)]
    spare, counts = total - most - (count - 1), [1] * (count - 1)
    while spare > 0:
        candidates = [i for i in range(count - 1) if counts[i] < most]
        whole, budget = sum([loads[i] for i in candidates]), spare
        for i in candidates:
            addition = min(most - counts[i], max(1, budget * loads[i] // whole), spare)
            counts[i] = counts[i] + addition
            spare = spare - addition
    return np.array([most] + counts)


def uneven(rng, number_of, total, limit, skew):
    if number_of == 2:
        one = jax.random.randint(rng, (), max(1, total - limit), min(limit, total - 1) + 1)
        return jnp.stack([one, total - one])
    tallies = jnp.asarray(profile(number_of, total, limit, skew), jnp.int32)
    pairs = (number_of - 1) // 2
    giver, receiver = tallies[1:1 + 2 * pairs:2], tallies[2:2 + 2 * pairs:2]
    room = jnp.minimum(giver - 1, limit - receiver)
    shifted = jax.random.randint(jax.random.fold_in(rng, 1), (pairs,), 0, 1 << 20) % (room + 1)
    tallies = tallies.at[1:1 + 2 * pairs:2].set(giver - shifted).at[2:2 + 2 * pairs:2].set(receiver + shifted)
    return tallies[jax.random.permutation(jax.random.fold_in(rng, 2), number_of)]


def scatter_about(rng, dims, width, limit, cuts=(), kind=jnp.bfloat16):
    factor_of = block_levels(rng, dims, cuts, -0.22, 0.18) if cuts else 1.0
    drawn = jax.random.normal(rng, dims, jnp.float32) * width * factor_of
    return jnp.minimum(jnp.maximum(drawn, -limit), limit).astype(kind)


def setup_inputs(seed: int = 0) -> dict:
    streams_of = jax.random.split(jax.random.key(seed), 14)
    return {
        "tokens": scatter_about(streams_of[0], (BATCHES, FRAMES, FRAME_TOK, D), 1.0, 6.0, ((0, 8), (2, 4))),
        "cotangent": scatter_about(streams_of[1], (BATCHES, FRAMES, FRAME_TOK, D), 1.0, 6.0, ((0, 8), (2, 4))),
        "episode_frames": jax.vmap(lambda own: uneven(own, EPIS, FRAMES, FRAMES // 2, 2))(jax.random.split(streams_of[2], BATCHES)).reshape((BATCHES, EPIS)).astype(jnp.int32),
        "kinds": draw_kinds(jax.random.fold_in(streams_of[13], 71), 0),
        "patch_pos": jax.vmap(lambda own: jax.random.permutation(own, FRAME_TOK))(jax.random.split(streams_of[4], BATCHES * FRAMES)).reshape((BATCHES, FRAMES, FRAME_TOK)).astype(jnp.int32),
        "ln1_gain": jnp.clip(1.0 + 0.1 * jax.random.normal(streams_of[5], (D,), jnp.float32), 0.5, 1.5).astype(jnp.bfloat16),
        "ln1_shift": scatter_about(streams_of[6], (D,), 0.3, 3.0),
        "w_qkv": scatter_about(streams_of[7], (D, 3 * D), D ** -0.5, 0.1875),
        "w_out": scatter_about(streams_of[8], (D, D), (max(D // 64, 1)) ** -0.5, 1.5),
        "ln2_gain": jnp.clip(1.0 + 0.1 * jax.random.normal(streams_of[9], (D,), jnp.float32), 0.5, 1.5).astype(jnp.bfloat16),
        "ln2_shift": scatter_about(streams_of[10], (D,), 0.3, 3.0),
        "w_up": scatter_about(streams_of[11], (D, FF), D ** -0.5, 0.1875),
        "w_down": scatter_about(streams_of[12], (FF, D), FF ** -0.5, 0.09375),
    }


EPS = 1e-06
THETA = 10000.0
MASKED = -1e+30

@jax.custom_vjp
def low(v):
    return lax.optimization_barrier(v.astype(jnp.bfloat16)).astype(jnp.float32)

@jax.custom_vjp
def low_back(v):
    return v

def low_keep(v):
    return (low(v), None)

def low_pass(kept, grad):
    return (grad,)

def back_keep(v):
    return (v, None)

def back_low(kept, grad):
    return (low(grad),)
low.defvjp(low_keep, low_pass)
low_back.defvjp(back_keep, back_low)

def layer_norm(value, gain, shift):
    mean = lax.optimization_barrier(jnp.mean(value, axis=-1, keepdims=True))
    centred = value - mean
    spread = lax.optimization_barrier(jnp.mean(centred * centred, axis=-1, keepdims=True))
    return centred * lax.rsqrt(spread + EPS) * gain + shift

def rotate(value, times, heights, widths):
    head = value.shape[-1]
    band = 2 * (head // 6)
    half = band // 2
    freq = jnp.power(THETA, -2.0 * jnp.arange(half, dtype=jnp.float32) / band)
    pieces = []
    for index, place in enumerate((times, heights, widths)):
        angle = place[:, None] * freq[None, :]
        cosine = jnp.cos(angle)[:, None, :]
        sine = jnp.sin(angle)[:, None, :]
        first = value[..., index * band:index * band + half]
        second = value[..., index * band + half:(index + 1) * band]
        pieces.append(first * cosine - second * sine)
        pieces.append(first * sine + second * cosine)
    pieces.append(value[..., 3 * band:])
    return jnp.concatenate(pieces, axis=-1)

def episode_of(frame_ids, ends):
    return lax.optimization_barrier(jnp.sum((frame_ids[:, None] >= ends[None, :]).astype(jnp.int32), axis=1))

def attention(queries, keys, values, row_frame, row_episode):
    total = queries.shape[0]
    block = math.gcd(total, 512)
    count = total // block
    scale = 1.0 / math.sqrt(HD)
    hp = lax.Precision.HIGHEST

    def one_block(item):
        q_block, f_block, e_block = item
        score = low_back(jnp.einsum('rhd,khd->hrk', q_block, keys, precision=hp) * scale)
        mask = ((e_block[:, None] == row_episode[None, :]) & (row_frame[None, :] <= f_block[:, None]))[None]
        score = jnp.where(mask, score, MASKED)
        top = lax.optimization_barrier(jnp.max(score, axis=-1, keepdims=True))
        lse = top + jnp.log(lax.optimization_barrier(jnp.sum(jnp.exp(score - top), axis=-1, keepdims=True)))
        prob = low(jnp.where(mask, jnp.exp(score - lse), 0.0))
        return jnp.einsum('hrk,khd->rhd', prob, values, precision=hp)
    result = lax.map(jax.checkpoint(one_block), (queries.reshape(count, block, HEADS, HD), row_frame.reshape(count, block), row_episode.reshape(count, block)))
    return result.reshape(total, HEADS * HD)

def group_forward(x, weights, times, heights, widths, row_frame, row_episode):
    ln1_gain, ln1_shift, w_qkv, w_out, ln2_gain, ln2_shift, w_up, w_down = weights
    hp = lax.Precision.HIGHEST
    total = x.shape[0]
    h_one = low(layer_norm(x, ln1_gain, ln1_shift))
    qkv = low_back(jnp.dot(h_one, w_qkv, precision=hp))
    q_raw = qkv[:, :D].reshape(total, HEADS, HD)
    k_raw = qkv[:, D:2 * D].reshape(total, HEADS, HD)
    v_raw = qkv[:, 2 * D:].reshape(total, HEADS, HD)
    queries = low(rotate(q_raw, times, heights, widths))
    keys = low(rotate(k_raw, times, heights, widths))
    values = low(v_raw)
    attended = attention(queries, keys, values, row_frame, row_episode)
    o_low = low(low_back(attended))
    branch = low_back(jnp.dot(o_low, w_out, precision=hp))
    x_one = x + branch
    h_two = low(layer_norm(x_one, ln2_gain, ln2_shift))
    up = low_back(jnp.dot(h_two, w_up, precision=hp))
    g_low = low(jax.nn.gelu(up, approximate=False))
    return x_one + jnp.dot(g_low, w_down, precision=hp)

def reference(tokens, cotangent, episode_frames, kinds, patch_pos, ln1_gain, ln1_shift, w_qkv, w_out, ln2_gain, ln2_shift, w_up, w_down):
    params = tuple((a.astype(jnp.float32) for a in (ln1_gain, ln1_shift, w_qkv, w_out, ln2_gain, ln2_shift, w_up, w_down)))
    total = FRAMES * FRAME_TOK
    frame_ids = jnp.arange(FRAMES, dtype=jnp.int32)
    row_frame = jnp.repeat(frame_ids, FRAME_TOK)
    times = row_frame.astype(jnp.float32)

    def step(sums, item):
        x_group, c_group, lengths, kind_group, pos_group = item
        ends = jnp.cumsum(lengths).astype(jnp.int32)
        row_episode = episode_of(row_frame, ends)
        kind = kind_group.reshape(total)
        place = pos_group.reshape(total)
        heights = jnp.where(kind == 0, place // GRID, 0).astype(jnp.float32)
        widths = jnp.where(kind == 0, place % GRID, 0).astype(jnp.float32)

        def forward(x, *weights):
            return group_forward(x, weights, times, heights, widths, row_frame, row_episode)
        result, pull = jax.vjp(forward, x_group.reshape(total, D).astype(jnp.float32), *params)
        grads = pull(c_group.reshape(total, D).astype(jnp.float32))
        sums = tuple((s + g for s, g in zip(sums, grads[1:])))
        return (sums, (result.astype(jnp.bfloat16), grads[0].astype(jnp.bfloat16)))
    zeros = tuple((jnp.zeros(p.shape, jnp.float32) for p in params))
    sums, (outs, grad_x) = lax.scan(step, zeros, (tokens, cotangent, episode_frames, kinds, patch_pos))
    shape = tokens.shape
    return (outs.reshape(shape), grad_x.reshape(shape), sums[0], sums[1], sums[2], sums[3], sums[4], sums[5], sums[6], sums[7])
```

```python
import functools
import math

import jax
import jax.numpy as jnp
from jax import lax
from jax.experimental import pallas as pl
from jax.experimental.pallas import tpu as pltpu
from jax.sharding import PartitionSpec as P

HEADS = 16
GRID = 16
EPS = 1e-06
THETA = 10000.0
MASKED = -1e30
LIMIT = 48 * 1024 * 1024
BF = jnp.bfloat16
F32 = jnp.float32
AXES = ("batch", "patch")


def nn(a, b):
    return lax.dot_general(a, b, (((1,), (0,)), ((), ())), preferred_element_type=F32)


def nt(a, b):
    return lax.dot_general(a, b, (((1,), (1,)), ((), ())), preferred_element_type=F32)


def tn(a, b):
    return lax.dot_general(a, b, (((0,), (0,)), ((), ())), preferred_element_type=F32)


def params(*semantics):
    return pltpu.CompilerParams(
        dimension_semantics=semantics, vmem_limit_bytes=LIMIT
    )


def cost(flops, nbytes, trans=0):
    return pl.CostEstimate(flops=int(flops), bytes_accessed=int(nbytes), transcendentals=int(trans))


def full(shape, memory=None):
    zeros = (0,) * len(shape)
    return pl.BlockSpec(shape, lambda *_: zeros)


def smem():
    return pl.BlockSpec(memory_space=pltpu.SMEM)


def normalise(x):
    mean = jnp.mean(x, axis=-1, keepdims=True)
    centred = x - mean
    spread = jnp.mean(centred * centred, axis=-1, keepdims=True)
    rstd = lax.rsqrt(spread + EPS)
    return centred * rstd, rstd


def norm_back(d_h, hat, rstd, gain):
    d_hat = d_h * gain
    first = jnp.mean(d_hat, axis=-1, keepdims=True)
    second = jnp.mean(d_hat * hat, axis=-1, keepdims=True)
    return rstd * (d_hat - first - hat * second)


def partner(value):
    head = 64
    half = head // 6
    width = value.shape[1]
    ahead = jnp.concatenate([value[:, half:], value[:, :half]], axis=1)
    behind = jnp.concatenate([value[:, width - half :], value[:, : width - half]], axis=1)
    lane = lax.broadcasted_iota(jnp.int32, value.shape, 1) % head
    return jnp.where(lane % (2 * half) < half, ahead, behind)


def widen(table, width):
    have = table.shape[1]
    if width <= have:
        return table[:, :width]
    return jnp.concatenate([table] * (width // have), axis=1)


def qkv_kernel(count, local, *refs):
    tok = refs[:count]
    cs_ref, w_ref, gain_ref, shift_ref = refs[count : count + 4]
    h_ref, q_ref, k_ref, v_ref = refs[count + 4 :]
    x = jnp.concatenate([t[...] for t in tok], axis=1)
    fb, rows, dim = x.shape
    x = x.reshape(fb * rows, dim).astype(F32)
    hat, _ = normalise(x)
    h = (hat * gain_ref[...] + shift_ref[...]).astype(BF)
    h_ref[...] = h.reshape(fb, rows, dim)
    y = nn(h, w_ref[...])
    cs = cs_ref[...].reshape(fb * rows, 256)
    cos = widen(cs[:, :128], local)
    sin = widen(cs[:, 128:], local)
    q = y[:, :local]
    k = y[:, local : 2 * local]
    q = (q * cos + partner(q) * sin).astype(BF) * BF(0.125)
    k = (k * cos + partner(k) * sin).astype(BF)
    q_ref[...] = q.reshape(fb, rows, local)
    k_ref[...] = k.reshape(fb, rows, local)
    v_ref[...] = y[:, 2 * local :].astype(BF).reshape(fb, rows, local)


def qkv_call(items, cs, w_local, gain, shift):
    count = len(items)
    frames, width, dim = items[0].shape
    local = w_local.shape[1] // 3
    rows = count * width
    fb = max(1, min(frames, 512 // rows))
    while frames % fb:
        fb -= 1
    shapes = [
        jax.ShapeDtypeStruct((frames, rows, dim), BF),
        jax.ShapeDtypeStruct((frames, rows, local), BF),
        jax.ShapeDtypeStruct((frames, rows, local), BF),
        jax.ShapeDtypeStruct((frames, rows, local), BF),
    ]
    return pl.pallas_call(
        functools.partial(qkv_kernel, count, local),
        grid=(frames // fb,),
        in_specs=[pl.BlockSpec((fb, width, dim), lambda i: (i, 0, 0))] * count
        + [
            pl.BlockSpec((fb, rows, 256), lambda i: (i, 0, 0)),
            full(w_local.shape),
            full(gain.shape),
            full(shift.shape),
        ],
        out_specs=[pl.BlockSpec((fb,) + s.shape[1:], lambda i: (i, 0, 0)) for s in shapes],
        out_shape=shapes,
        compiler_params=params("arbitrary"),
        cost_estimate=cost(
            2 * frames * rows * dim * 3 * local,
            frames * rows * (4 * dim + 1024 + 6 * local) + 6 * dim * local,
        ),
        name="qkv",
    )(*items, cs, w_local, gain, shift)


def attend_kernel(groups, heads, head, patches, info_ref, *refs):
    qs = refs[:groups]
    ks = refs[groups : 2 * groups]
    vs = refs[2 * groups : 3 * groups]
    o_ref, of_ref, lse_ref = refs[3 * groups :]
    f = pl.program_id(0)
    begin = info_ref[1 + f]
    me = info_ref[0]
    q = jnp.concatenate([r[0] for r in qs], axis=0)
    rows = q.shape[0]

    def body(g, state):
        k = jnp.concatenate([r[g] for r in ks], axis=0)
        v = jnp.concatenate([r[g] for r in vs], axis=0)
        new = []
        for h in range(heads):
            top, total, acc = state[3 * h : 3 * h + 3]
            sl = slice(h * head, (h + 1) * head)
            s = nt(q[:, sl], k[:, sl])
            new_top = jnp.maximum(top, jnp.max(s, axis=1, keepdims=True))
            p = jnp.exp(s - new_top)
            factor = jnp.exp(top - new_top)
            total = total * factor + jnp.sum(p, axis=1, keepdims=True)
            acc = acc * factor + nn(p.astype(BF), v[:, sl])
            new += [new_top, total, acc]
        return tuple(new)

    state = []
    for h in range(heads):
        state += [
            jnp.full((rows, 1), MASKED, F32),
            jnp.zeros((rows, 1), F32),
            jnp.zeros((rows, head), F32),
        ]
    state = lax.fori_loop(begin, f + 1, body, tuple(state))
    outs, lses = [], []
    for h in range(heads):
        top, total, acc = state[3 * h : 3 * h + 3]
        outs.append(acc / total)
        lses.append(top + jnp.log(total))
    o = jnp.concatenate(outs, axis=1)
    of_ref[0] = o
    lse_ref[0] = jnp.concatenate(lses, axis=1)
    o = o.astype(BF)
    width = rows // patches
    for j in range(patches):
        o_ref[me ^ j, 0] = o[j * width : (j + 1) * width]


def attend_call(info, q, k, v, heads, patches):
    groups = len(q)
    frames, _, local = q[0].shape
    rows = sum(a.shape[1] for a in q)
    width = rows // patches
    head = local // heads
    shapes = [
        jax.ShapeDtypeStruct((patches, frames, width, local), BF),
        jax.ShapeDtypeStruct((frames, rows, local), F32),
        jax.ShapeDtypeStruct((frames, rows, heads), F32),
    ]
    return pl.pallas_call(
        functools.partial(attend_kernel, groups, heads, head, patches),
        grid=(frames,),
        in_specs=[smem()]
        + [pl.BlockSpec((1,) + a.shape[1:], lambda i: (i, 0, 0)) for a in q]
        + [full(a.shape) for a in k]
        + [full(a.shape) for a in v],
        out_specs=[
            pl.BlockSpec((patches, 1, width, local), lambda i: (0, i, 0, 0)),
            pl.BlockSpec((1, rows, local), lambda i: (i, 0, 0)),
            pl.BlockSpec((1, rows, heads), lambda i: (i, 0, 0)),
        ],
        out_shape=shapes,
        compiler_params=params("arbitrary"),
        cost_estimate=cost(
            4 * 2 * frames * rows * rows * 256 * heads, 8 * frames * rows * local, frames * rows * rows
        ),
        name="attend",
    )(info, *q, *k, *v)


def attend_back_kernel(groups, heads, head, patches, info_ref, *refs):
    qs = refs[:groups]
    ks = refs[groups : 2 * groups]
    vs = refs[2 * groups : 3 * groups]
    css = refs[3 * groups : 4 * groups]
    do_ref, of_ref, lse_ref = refs[4 * groups : 4 * groups + 3]
    outs = refs[4 * groups + 3 : 5 * groups + 3]
    dk_ref, dv_ref = refs[5 * groups + 3 :]
    f = pl.program_id(0)
    frames = pl.num_programs(0)
    begin = info_ref[1 + f]
    me = info_ref[0]
    local = heads * head
    q = jnp.concatenate([r[0] for r in qs], axis=0)
    d_o = jnp.concatenate([do_ref[me ^ j, 0] for j in range(patches)], axis=0)
    rows = q.shape[0]
    prod = d_o.astype(F32) * of_ref[0]
    lse = lse_ref[0]
    delta = [
        jnp.sum(prod[:, h * head : (h + 1) * head], axis=1, keepdims=True) for h in range(heads)
    ]
    dk_ref[f] = jnp.zeros((rows, local), F32)
    dv_ref[f] = jnp.zeros((rows, local), F32)

    def body(g, state):
        k = jnp.concatenate([r[g] for r in ks], axis=0)
        v = jnp.concatenate([r[g] for r in vs], axis=0)
        new, dks, dvs = [], [], []
        for h in range(heads):
            sl = slice(h * head, (h + 1) * head)
            p = jnp.exp(nt(q[:, sl], k[:, sl]) - lse[:, h : h + 1])
            dp = nt(d_o[:, sl], v[:, sl])
            ds = (p * (dp - delta[h])).astype(BF)
            new.append(state[h] + nn(ds, k[:, sl]))
            dks.append(tn(ds, q[:, sl]))
            dvs.append(tn(p.astype(BF), d_o[:, sl]))
        dk_ref[g] += jnp.concatenate(dks, axis=1)
        dv_ref[g] += jnp.concatenate(dvs, axis=1)
        return tuple(new)

    dq = lax.fori_loop(
        begin, f + 1, body, tuple(jnp.zeros((rows, head), F32) for _ in range(heads))
    )
    dq = jnp.concatenate(dq, axis=1) * 0.125

    def tables(t):
        cs = jnp.concatenate([r[t] for r in css], axis=0)
        return widen(cs[:, :128], local), widen(cs[:, 128:], local)

    def put(t, at, value):
        start = 0
        for out in outs:
            n = out.shape[1]
            out[t, :, at * local : (at + 1) * local] = value[start : start + n]
            start += n

    cos, sin = tables(f)
    put(f, 0, (dq * cos - partner(dq) * sin).astype(BF))

    @pl.when(f == frames - 1)
    def _():
        @pl.loop(0, frames)
        def _(t):
            cos, sin = tables(t)
            dk = dk_ref[t]
            put(t, 1, (dk * cos - partner(dk) * sin).astype(BF))
            put(t, 2, dv_ref[t].astype(BF))


def attend_back_call(info, q, k, v, cs, d_o, o_full, lse, heads, patches):
    groups = len(q)
    frames, _, local = q[0].shape
    rows = sum(a.shape[1] for a in q)
    width = rows // patches
    head = local // heads
    shapes = [jax.ShapeDtypeStruct((frames, a.shape[1], 3 * local), BF) for a in q]
    return pl.pallas_call(
        functools.partial(attend_back_kernel, groups, heads, head, patches),
        grid=(frames,),
        in_specs=[smem()]
        + [pl.BlockSpec((1,) + a.shape[1:], lambda i: (i, 0, 0)) for a in q]
        + [full(a.shape) for a in k]
        + [full(a.shape) for a in v]
        + [full(a.shape) for a in cs]
        + [
            pl.BlockSpec((patches, 1, width, local), lambda i: (0, i, 0, 0)),
            pl.BlockSpec((1, rows, local), lambda i: (i, 0, 0)),
            pl.BlockSpec((1, rows, heads), lambda i: (i, 0, 0)),
        ],
        out_specs=[full(s.shape) for s in shapes],
        out_shape=shapes,
        scratch_shapes=[
            pltpu.VMEM((frames, rows, local), F32),
            pltpu.VMEM((frames, rows, local), F32),
        ],
        compiler_params=params("arbitrary"),
        cost_estimate=cost(
            10 * 2 * frames * rows * rows * 256 * heads, 16 * frames * rows * local, frames * rows * rows
        ),
        name="attend_back",
    )(info, *q, *k, *v, *cs, d_o, o_full, lse)


def project_kernel(o_ref, x_ref, w_ref, gain_ref, shift_ref, x1_ref, h_ref):
    patches, fb, width, local = o_ref.shape
    rows = fb * width
    acc = x_ref[...].astype(F32).reshape(rows, -1)
    for p in range(patches):
        acc = acc + nn(o_ref[p].reshape(rows, local), w_ref[p * local : (p + 1) * local, :])
    x1_ref[...] = acc
    hat, _ = normalise(acc)
    h_ref[...] = (hat * gain_ref[...] + shift_ref[...]).astype(BF)


def project_call(o_in, tokens, w_out, gain, shift):
    patches, frames, width, local = o_in.shape
    dim = w_out.shape[0]
    fb = frames // 2
    rows = frames * width
    return pl.pallas_call(
        project_kernel,
        grid=(2,),
        in_specs=[
            pl.BlockSpec((patches, fb, width, local), lambda i: (0, i, 0, 0)),
            pl.BlockSpec((fb, width, dim), lambda i: (i, 0, 0)),
            full(w_out.shape),
            full(gain.shape),
            full(shift.shape),
        ],
        out_specs=[
            pl.BlockSpec((rows // 2, dim), lambda i: (i, 0)),
            pl.BlockSpec((rows // 2, dim), lambda i: (i, 0)),
        ],
        out_shape=[
            jax.ShapeDtypeStruct((rows, dim), F32),
            jax.ShapeDtypeStruct((rows, dim), BF),
        ],
        compiler_params=params("arbitrary"),
        cost_estimate=cost(2 * rows * dim * dim, rows * dim * 10 + 2 * dim * dim),
        name="project",
    )(o_in, tokens, w_out, gain, shift)


def ffn_kernel(
    info_ref, h_own, h_mate, dy_own, dy_mate, up_ref, down_ref,
    g_ref, du_ref, dh_own, dh_mate, dw_ref, acc_ref,
):
    step = pl.program_id(0)
    w_up = up_ref[...]
    w_down = down_ref[...]
    half = h_own.shape[0]
    total = None
    for n, (h_ref, dy_ref) in enumerate(((h_own, dy_own), (h_mate, dy_mate))):
        rows = slice(n * half, (n + 1) * half)
        u = nn(h_ref[...], w_up)
        dg = nt(dy_ref[...], w_down)
        cdf = 0.5 + 0.5 * lax.erf(u * math.sqrt(0.5))
        pdf = jnp.exp(u * u * -0.5) * (1.0 / math.sqrt(2.0 * math.pi))
        g = (u * cdf).astype(BF)
        du = (dg * (cdf + u * pdf)).astype(BF)
        g_ref[rows] = g
        du_ref[rows] = du
        part = nt(du, w_up)

        @pl.when(step == 0)
        def _():
            acc_ref[rows] = part

        @pl.when(step > 0)
        def _():
            acc_ref[rows] += part

        dw = tn(g, dy_ref[...])
        total = dw if total is None else total + dw
    dw_ref[...] = total.astype(BF)

    @pl.when(step == pl.num_programs(0) - 1)
    def _():
        dh_own[...] = acc_ref[:half]
        dh_mate[...] = acc_ref[half:].astype(BF)


def ffn_call(info, h_own, h_mate, dy_own, dy_mate, w_up, w_down, patches):
    half, dim = h_own.shape
    hidden = w_up.shape[1]
    tile = min(256, hidden // patches)
    per = hidden // patches // tile
    steps = hidden // 2 // tile

    def at(i, info):
        return ((i // per) * 2 + (info[0] & 1)) * per + i % per

    grid_spec = pltpu.PrefetchScalarGridSpec(
        num_scalar_prefetch=1,
        grid=(steps,),
        in_specs=[full((half, dim))] * 4
        + [
            pl.BlockSpec((dim, tile), lambda i, info: (0, at(i, info))),
            pl.BlockSpec((tile, dim), lambda i, info: (at(i, info), 0)),
        ],
        out_specs=[
            pl.BlockSpec((2 * half, tile), lambda i, info: (0, i)),
            pl.BlockSpec((2 * half, tile), lambda i, info: (0, i)),
            full((half, dim)),
            full((half, dim)),
            pl.BlockSpec((tile, dim), lambda i, info: (i, 0)),
        ],
        scratch_shapes=[pltpu.VMEM((2 * half, dim), F32)],
    )
    return pl.pallas_call(
        ffn_kernel,
        grid_spec=grid_spec,
        out_shape=[
            jax.ShapeDtypeStruct((2 * half, hidden // 2), BF),
            jax.ShapeDtypeStruct((2 * half, hidden // 2), BF),
            jax.ShapeDtypeStruct((half, dim), F32),
            jax.ShapeDtypeStruct((half, dim), BF),
            jax.ShapeDtypeStruct((hidden // 2, dim), BF),
        ],
        compiler_params=params("arbitrary"),
        cost_estimate=cost(8 * 2 * half * dim * hidden // 2, 4 * dim * hidden, half * hidden),
        name="ffn",
    )(info, h_own, h_mate, dy_own, dy_mate, w_up, w_down)


def ffn_rest_kernel(
    info_ref, h_own, h_mate, x1_ref, g_ref, du_ref, down_ref,
    dw_ref, out_own, out_mate, ht_ref, acc_ref,
):
    step = pl.program_id(0)
    half = h_own.shape[0]

    @pl.when(step == 0)
    def _():
        ht_ref[:, :half] = h_own[...].T
        ht_ref[:, half:] = h_mate[...].T
        acc_ref[:half] = x1_ref[...]
        acc_ref[half:] = jnp.zeros_like(x1_ref)

    dw_ref[...] = nn(ht_ref[...], du_ref[...]).astype(BF)
    for n in range(2):
        rows = slice(n * half, (n + 1) * half)
        acc_ref[rows] += nn(g_ref[rows], down_ref[...])

    @pl.when(step == pl.num_programs(0) - 1)
    def _():
        out_own[...] = acc_ref[:half]
        out_mate[...] = acc_ref[half:].astype(BF)


def ffn_rest_call(info, h_own, h_mate, x1, g, du, w_down, patches):
    half, dim = h_own.shape
    hidden = w_down.shape[0]
    tile = min(256, hidden // patches)
    per = hidden // patches // tile
    steps = hidden // 2 // tile

    def at(i, info):
        return ((i // per) * 2 + (info[0] & 1)) * per + i % per

    grid_spec = pltpu.PrefetchScalarGridSpec(
        num_scalar_prefetch=1,
        grid=(steps,),
        in_specs=[full((half, dim))] * 3
        + [
            pl.BlockSpec((2 * half, tile), lambda i, info: (0, i)),
            pl.BlockSpec((2 * half, tile), lambda i, info: (0, i)),
            pl.BlockSpec((tile, dim), lambda i, info: (at(i, info), 0)),
        ],
        out_specs=[
            pl.BlockSpec((dim, tile), lambda i, info: (0, i)),
            full((half, dim)),
            full((half, dim)),
        ],
        scratch_shapes=[pltpu.VMEM((dim, 2 * half), BF), pltpu.VMEM((2 * half, dim), F32)],
    )
    return pl.pallas_call(
        ffn_rest_kernel,
        grid_spec=grid_spec,
        out_shape=[
            jax.ShapeDtypeStruct((dim, hidden // 2), BF),
            jax.ShapeDtypeStruct((half, dim), F32),
            jax.ShapeDtypeStruct((half, dim), BF),
        ],
        compiler_params=params("arbitrary"),
        cost_estimate=cost(4 * 2 * half * dim * hidden // 2, 6 * dim * hidden),
        name="ffn_rest",
    )(info, h_own, h_mate, x1, g, du, w_down)


def mid_kernel(dh_ref, recv_ref, x1_ref, dy_ref, w_ref, gain_ref, dx_ref, da_ref, do_ref, gs_ref):
    step = pl.program_id(0)
    patches, fb, width, local = do_ref.shape
    rows = fb * width
    hat, rstd = normalise(x1_ref[...])
    dh = dh_ref[...] + recv_ref[...].astype(F32)
    dx = dy_ref[...].astype(F32) + norm_back(dh, hat, rstd, gain_ref[...])
    dx_ref[...] = dx
    da = dx.astype(BF)
    da_ref[...] = da
    sums = jnp.concatenate(
        [jnp.sum(dh * hat, axis=0, keepdims=True), jnp.sum(dh, axis=0, keepdims=True)], axis=0
    )

    @pl.when(step == 0)
    def _():
        gs_ref[...] = sums

    @pl.when(step > 0)
    def _():
        gs_ref[...] += sums

    for p in range(patches):
        do_ref[p] = (
            nt(da, w_ref[p * local : (p + 1) * local, :]).astype(BF).reshape(fb, width, local)
        )


def mid_call(dh, recv, x1, dy, w_out, gain, frames, patches):
    rows, dim = x1.shape
    width = rows // frames
    local = dim // patches
    fb = frames // 2
    row = pl.BlockSpec((rows // 2, dim), lambda i: (i, 0))
    return pl.pallas_call(
        mid_kernel,
        grid=(2,),
        in_specs=[row, row, row, row, full(w_out.shape), full(gain.shape)],
        out_specs=[
            row,
            row,
            pl.BlockSpec((patches, fb, width, local), lambda i: (0, i, 0, 0)),
            full((2, dim)),
        ],
        out_shape=[
            jax.ShapeDtypeStruct((rows, dim), F32),
            jax.ShapeDtypeStruct((rows, dim), BF),
            jax.ShapeDtypeStruct((patches, frames, width, local), BF),
            jax.ShapeDtypeStruct((2, dim), F32),
        ],
        compiler_params=params("arbitrary"),
        cost_estimate=cost(2 * rows * dim * dim, rows * dim * 20 + 2 * dim * dim),
        name="mid",
    )(dh, recv, x1, dy, w_out, gain)


def dwo_kernel(o_ref, da_ref, dw_ref):
    _, frames, width, local = o_ref.shape
    dw_ref[...] = tn(o_ref[0].reshape(frames * width, local), da_ref[...]).astype(BF)[None]


def dwo_call(o_in, da):
    patches, frames, width, local = o_in.shape
    dim = da.shape[1]
    return pl.pallas_call(
        dwo_kernel,
        grid=(patches,),
        in_specs=[
            pl.BlockSpec((1, frames, width, local), lambda i: (i, 0, 0, 0)),
            full(da.shape),
        ],
        out_specs=pl.BlockSpec((1, local, dim), lambda i: (i, 0, 0)),
        out_shape=jax.ShapeDtypeStruct((patches, local, dim), BF),
        compiler_params=params("arbitrary"),
        cost_estimate=cost(2 * da.shape[0] * dim * dim, 6 * dim * dim),
        name="dwo",
    )(o_in, da)


def dqkv_kernel(groups, *refs):
    hs = refs[:groups]
    ds = refs[groups : 2 * groups]
    w_ref = refs[2 * groups]
    dh = refs[2 * groups + 1 : 3 * groups + 1]
    dw_ref = refs[3 * groups + 1]
    acc_ref = refs[3 * groups + 2]
    step = pl.program_id(0)
    total = None
    for h_ref, d_ref, out in zip(hs, ds, dh):
        fb, rows, dim = h_ref.shape
        d = d_ref[...].reshape(fb * rows, -1)
        out[...] = nt(d, w_ref[...]).astype(BF).reshape(fb, rows, dim)
        part = tn(h_ref[...].reshape(fb * rows, dim), d)
        total = part if total is None else total + part

    @pl.when(step == 0)
    def _():
        acc_ref[...] = total

    @pl.when(step > 0)
    def _():
        acc_ref[...] += total

    @pl.when(step == pl.num_programs(0) - 1)
    def _():
        dw_ref[...] = acc_ref[...].astype(BF)


def dqkv_call(hs, ds, w_local):
    groups = len(hs)
    frames = hs[0].shape[0]
    dim, cols = w_local.shape
    rows = sum(a.shape[1] for a in hs)
    fb = max(1, min(frames, 512 // rows))

    def blocks(a):
        return pl.BlockSpec((fb,) + a.shape[1:], lambda i: (i, 0, 0))

    shapes = [jax.ShapeDtypeStruct(a.shape, BF) for a in hs]
    shapes.append(jax.ShapeDtypeStruct((dim, cols), BF))
    return pl.pallas_call(
        functools.partial(dqkv_kernel, groups),
        grid=(frames // fb,),
        in_specs=[blocks(a) for a in hs] + [blocks(a) for a in ds] + [full(w_local.shape)],
        out_specs=[blocks(a) for a in hs] + [full((dim, cols))],
        out_shape=shapes,
        scratch_shapes=[pltpu.VMEM((dim, cols), F32)],
        compiler_params=params("arbitrary"),
        cost_estimate=cost(4 * frames * rows * dim * cols, frames * rows * 4 * dim),
        name="dqkv",
    )(*hs, *ds, w_local)


def last_kernel(a_ref, b_ref, x_ref, dx_ref, gain_ref, gt_ref, gs_ref):
    step = pl.program_id(0)
    hat, rstd = normalise(x_ref[...].astype(F32))
    dh = a_ref[...].astype(F32) + b_ref[...].astype(F32)
    gt_ref[...] = (dx_ref[...] + norm_back(dh, hat, rstd, gain_ref[...])).astype(BF)
    sums = jnp.concatenate(
        [jnp.sum(dh * hat, axis=0, keepdims=True), jnp.sum(dh, axis=0, keepdims=True)], axis=0
    )

    @pl.when(step == 0)
    def _():
        gs_ref[...] = sums

    @pl.when(step > 0)
    def _():
        gs_ref[...] += sums


def last_call(a, b, x, dx, gain):
    rows, dim = x.shape
    row = pl.BlockSpec((rows // 2, dim), lambda i: (i, 0))
    return pl.pallas_call(
        last_kernel,
        grid=(2,),
        in_specs=[row, row, row, row, full(gain.shape)],
        out_specs=[row, full((2, dim))],
        out_shape=[
            jax.ShapeDtypeStruct((rows, dim), BF),
            jax.ShapeDtypeStruct((2, dim), F32),
        ],
        compiler_params=params("arbitrary"),
        cost_estimate=cost(40 * rows * dim, rows * dim * 12),
        name="last",
    )(a, b, x, dx, gain)


class Links:
    def __init__(self, batches, patches):
        self.batches, self.patches = batches, patches
        self.patch = lax.axis_index("patch")
        self.batch = lax.axis_index("batch")
        self.rest = batches // 2
        self.groups = [[y + 2 * z for z in range(self.rest)] for y in range(2)]

    def swap_patch(self, a, bit):
        n = self.batches * self.patches
        return lax.ppermute(a, AXES, [(i, i ^ bit) for i in range(n)])

    def swap_y(self, a):
        n = self.batches * self.patches
        return lax.ppermute(a, AXES, [(i, i ^ self.patches) for i in range(n)])

    def halve(self, a, bit, swap):
        keep = lax.dynamic_index_in_dim(a, bit, 0, keepdims=False)
        send = lax.dynamic_index_in_dim(a, 1 - bit, 0, keepdims=False)
        return (keep.astype(F32) + swap(send).astype(F32)).astype(BF)

    def join(self, a, bit, swap):
        other = swap(a)
        return jnp.where(bit == 0, jnp.stack([a, other]), jnp.stack([other, a]))

    def over_x(self, a):
        bit = self.patches // 2
        while bit > 1:
            a = a.reshape((2, a.shape[0] // 2) + a.shape[1:])
            a = self.halve(a, (self.patch // bit) & 1, functools.partial(self.swap_patch, bit=bit))
            bit //= 2
        return a.reshape(a.shape[1:])

    def over_core(self, a):
        return self.halve(a, self.patch & 1, functools.partial(self.swap_patch, bit=1))

    def scatter_y(self, a):
        return self.halve(a, self.batch & 1, self.swap_y)

    def scatter_z(self, a):
        got = lax.all_to_all(a, "batch", 0, 0, tiled=True, axis_index_groups=self.groups)
        return jnp.sum(got.astype(F32), axis=0).astype(BF)

    def gather_z(self, a):
        wide = jnp.broadcast_to(a[None], (self.rest,) + a.shape)
        return lax.all_to_all(wide, "batch", 0, 0, tiled=True, axis_index_groups=self.groups)

    def gather_y(self, a):
        return self.join(a, self.batch & 1, self.swap_y)

    def over_batch(self, a):
        rows = a.shape[0]
        a = a.reshape((2, self.rest, rows // self.batches) + a.shape[1:])
        a = self.scatter_z(self.scatter_y(a))
        a = self.gather_y(self.gather_z(a))
        return a.reshape((rows,) + a.shape[3:])

    def items(self, a):
        got = {0: a}
        bit = self.patches // 2
        while bit > 1:
            for j in sorted(got):
                got[j | bit] = self.swap_patch(got[j], bit)
            bit //= 2
        for j in sorted(got):
            got[j | 1] = self.swap_patch(got[j], 1)
        return got


def tables(code, times):
    head = 64
    half = head // 6
    band = 2 * half
    dims = jnp.arange(head)
    freq = jnp.power(THETA, -2.0 * (dims % half).astype(F32) / band)
    places = jnp.stack([times, (code // GRID).astype(F32), (code % GRID).astype(F32)], axis=-1)
    which = jnp.minimum(dims // band, 2)
    pick = jnp.where(
        which == 0, places[..., 0:1], jnp.where(which == 1, places[..., 1:2], places[..., 2:3])
    )
    angle = pick * freq
    turned = dims < 3 * band
    cos = jnp.where(turned, jnp.cos(angle), 1.0)
    sin = jnp.where(turned, jnp.sin(angle) * jnp.where(dims % band < half, -1.0, 1.0), 0.0)
    return jnp.concatenate([cos, cos, sin, sin], axis=-1)


def per_device(
    batches, patches, tokens, cotangent, episode_frames, kinds, patch_pos,
    ln1_gain, ln1_shift, w_qkv, w_out, ln2_gain, ln2_shift, w_up, w_down,
):
    tokens = tokens[0]
    frames, width, dim = tokens.shape
    rows = frames * width
    heads = HEADS // patches
    local = dim // patches
    links = Links(batches, patches)
    me = links.patch
    core = me & 1
    gain1, shift1, gain2, shift2 = (
        a.astype(F32).reshape(1, dim) for a in (ln1_gain, ln1_shift, ln2_gain, ln2_shift)
    )
    dy = cotangent.reshape(rows, dim)

    items = links.items(tokens)
    dy_mate = links.swap_patch(dy, 1)
    code = jnp.where(kinds[0] == 0, patch_pos[0], 0)
    codes = lax.all_to_all(
        jnp.broadcast_to(code[None], (patches,) + code.shape), "patch", 0, 0, tiled=True
    )
    codes = codes[me ^ jnp.arange(patches)]
    times = jnp.broadcast_to(jnp.arange(frames, dtype=F32)[None, :, None], codes.shape)
    turn = tables(codes, times)
    ends = jnp.cumsum(episode_frames[0])
    frame_ids = jnp.arange(frames, dtype=jnp.int32)
    starts = jnp.max(
        jnp.where(ends[None, :] <= frame_ids[:, None], ends[None, :], 0), axis=1
    )
    info = jnp.concatenate([me[None], starts]).astype(jnp.int32)

    w_local = lax.dynamic_index_in_dim(
        w_qkv.reshape(dim, 3, patches, local), me, 2, keepdims=False
    ).reshape(dim, 3 * local)

    hs, qs, ks, vs, css = [], [], [], [], []
    members = [[0, 1], list(range(2, patches))]
    for group in members:
        cs = turn[group[0] : group[-1] + 1].transpose(1, 0, 2, 3)
        cs = cs.reshape(frames, len(group) * width, 256)
        h, q, k, v = qkv_call([items[j] for j in group], cs, w_local, gain1, shift1)
        hs.append(h)
        qs.append(q)
        ks.append(k)
        vs.append(v)
        css.append(cs)

    o_send, o_full, lse = attend_call(info, qs, ks, vs, heads, patches)
    o_in = lax.all_to_all(o_send, "patch", 0, 0, tiled=True)
    x1, h2 = project_call(o_in, tokens, w_out, gain2, shift2)
    h2_mate = links.swap_patch(h2, 1)
    g, du, dh_own, dh_mate, dw_down = ffn_call(
        info, h2, h2_mate, dy, dy_mate, w_up, w_down, patches
    )
    dh_recv = links.swap_patch(dh_mate, 1)
    dx1, da, d_o, sums2 = mid_call(dh_own, dh_recv, x1, dy, w_out, gain2, frames, patches)
    do_in = lax.all_to_all(d_o, "patch", 0, 0, tiled=True)

    dw_up, out_own, out_mate = ffn_rest_call(info, h2, h2_mate, x1, g, du, w_down, patches)
    out = (out_own + links.swap_patch(out_mate, 1).astype(F32)).astype(BF)
    dw_out = dwo_call(o_in, da)

    dqkv = attend_back_call(info, qs, ks, vs, css, do_in, o_full, lse, heads, patches)
    *dh1, dw_qkv = dqkv_call(hs, dqkv, w_local)

    slots = []
    for group, part in zip(members, dh1):
        part = part.reshape(frames, len(group), width, dim)
        slots += [part[:, n] for n in range(len(group))]
    even = jnp.stack(slots[0::2])
    odd = jnp.stack(slots[1::2])
    slots = (even.astype(F32) + links.swap_patch(odd, 1).astype(F32)).astype(BF)
    bit = patches // 2
    while bit > 1:
        n = slots.shape[0] // 2
        got = links.swap_patch(slots[n:], bit)
        if bit > 2:
            slots = (slots[:n].astype(F32) + got.astype(F32)).astype(BF)
        else:
            slots = (slots[0], got[0])
        bit //= 2
    grad_tokens, sums1 = last_call(
        slots[0].reshape(rows, dim), slots[1].reshape(rows, dim), tokens.reshape(rows, dim), dx1, gain1
    )

    nx = patches // 2
    down = links.over_x(dw_down.reshape(nx, -1, dim))
    down = links.over_batch(down)
    up = links.over_x(dw_up.reshape(nx, dim // nx, -1))
    up = up.reshape(2, local, -1)
    mine = lax.dynamic_index_in_dim(up, core, 0, keepdims=False)
    other = links.swap_patch(lax.dynamic_index_in_dim(up, 1 - core, 0, keepdims=False), 1)
    up = jnp.where(core == 0, jnp.stack([mine, other]), jnp.stack([other, mine]))
    up = up.reshape(2, local, nx, -1).transpose(1, 2, 0, 3).reshape(local, -1)
    up = links.over_batch(up)
    wo = links.over_core(dw_out.reshape(nx, 2, local, dim).transpose(1, 0, 2, 3))
    wo = links.over_batch(links.over_x(wo))
    qkv = dw_qkv.reshape(patches, 2, links.rest, -1, 3 * local).transpose(1, 2, 0, 3, 4)
    qkv = links.scatter_z(links.scatter_y(qkv))
    qkv = lax.all_to_all(qkv, "patch", 0, 0, tiled=True)
    qkv = qkv.reshape(patches, -1, 3, local).transpose(1, 2, 0, 3).reshape(-1, 3 * dim)
    qkv = links.gather_y(links.gather_z(qkv)).reshape(local, 3 * dim)

    sums = jnp.concatenate([sums1, sums2], axis=0)
    sums = sums.reshape(4, patches, local).transpose(1, 0, 2)
    sums = jnp.sum(lax.all_to_all(sums, "patch", 0, 0, tiled=True), axis=0)
    sums = jnp.broadcast_to(sums[None], (batches,) + sums.shape)
    sums = jnp.sum(lax.all_to_all(sums, "batch", 0, 0, tiled=True), axis=0)
    return (
        out.reshape(1, frames, width, dim),
        grad_tokens.reshape(1, frames, width, dim),
        sums[0],
        sums[1],
        qkv.astype(F32),
        wo.astype(F32),
        sums[2],
        sums[3],
        up.astype(F32),
        down.astype(F32),
    )


def solution(mesh):
    placed = (
        P("batch", None, "patch", None),
        P("batch", None, "patch", None),
        P("batch", None),
        P("batch", None, "patch"),
        P("batch", None, "patch"),
    ) + (P(),) * 8
    return jax.shard_map(
        functools.partial(per_device, mesh.shape["batch"], mesh.shape["patch"]),
        mesh=mesh,
        in_specs=placed,
        out_specs=(
            P("batch", None, "patch", None),
            P("batch", None, "patch", None),
            P("patch"),
            P("patch"),
            P("patch", None),
            P("patch", None),
            P("patch"),
            P("patch"),
            P("patch", None),
            P("patch", None),
        ),
        check_vma=False,
    )
```

```python
import functools
import math

import jax
import jax.numpy as jnp
from jax import lax
from jax.experimental import pallas as pl
from jax.experimental.pallas import tpu as pltpu
from jax.sharding import PartitionSpec as P

GRID = 16
EPS = 1e-06
THETA = 10000.0
MASKED = -1e30
LIMIT = 48 * 1024 * 1024
BF = jnp.bfloat16
F32 = jnp.float32
AXES = ("batch", "patch")


def nn(a, b):
    return lax.dot_general(a, b, (((1,), (0,)), ((), ())), preferred_element_type=F32)


def nt(a, b):
    return lax.dot_general(a, b, (((1,), (1,)), ((), ())), preferred_element_type=F32)


def tn(a, b):
    return lax.dot_general(a, b, (((0,), (0,)), ((), ())), preferred_element_type=F32)


def params(*semantics):
    return pltpu.CompilerParams(
        dimension_semantics=semantics, vmem_limit_bytes=LIMIT
    )


def cost(flops, nbytes, trans=0):
    return pl.CostEstimate(flops=int(flops), bytes_accessed=int(nbytes), transcendentals=int(trans))


def full(shape, memory=None):
    zeros = (0,) * len(shape)
    return pl.BlockSpec(shape, lambda *_: zeros)


def blocked(ref, value):
    for n in range(ref.shape[0]):
        ref[n] = value[:, n * 128 : (n + 1) * 128].astype(BF)


def smem():
    return pl.BlockSpec(memory_space=pltpu.SMEM)


def normalise(x):
    mean = jnp.mean(x, axis=-1, keepdims=True)
    centred = x - mean
    spread = jnp.mean(centred * centred, axis=-1, keepdims=True)
    rstd = lax.rsqrt(spread + EPS)
    return centred * rstd, rstd


def norm_back(d_h, hat, rstd, gain):
    d_hat = d_h * gain
    first = jnp.mean(d_hat, axis=-1, keepdims=True)
    second = jnp.mean(d_hat * hat, axis=-1, keepdims=True)
    return rstd * (d_hat - first - hat * second)


def partner(value):
    head = 64
    half = head // 6
    width = value.shape[1]
    ahead = jnp.concatenate([value[:, half:], value[:, :half]], axis=1)
    behind = jnp.concatenate([value[:, width - half :], value[:, : width - half]], axis=1)
    lane = lax.broadcasted_iota(jnp.int32, value.shape, 1) % head
    return jnp.where(lane % (2 * half) < half, ahead, behind)


def widen(table, width):
    have = table.shape[1]
    if width <= have:
        return table[:, :width]
    return jnp.concatenate([table] * (width // have), axis=1)


def qkv_kernel(count, local, *refs):
    tok = refs[:count]
    cs_ref, w_ref, gain_ref, shift_ref = refs[count : count + 4]
    h_ref, qkv_ref = refs[count + 4 :]
    x = jnp.concatenate([t[...] for t in tok], axis=1)
    fb, rows, dim = x.shape
    x = x.reshape(fb * rows, dim).astype(F32)
    hat, _ = normalise(x)
    h = (hat * gain_ref[...] + shift_ref[...]).astype(BF)
    h_ref[...] = h.reshape(fb, rows, dim)
    y = nn(h, w_ref[...])
    cs = cs_ref[...].reshape(fb * rows, 256)
    cos = widen(cs[:, :128], local)
    sin = widen(cs[:, 128:], local)
    q = y[:, :local]
    k = y[:, local : 2 * local]
    q = (q * cos + partner(q) * sin).astype(BF) * BF(0.125)
    k = (k * cos + partner(k) * sin).astype(BF)
    qkv_ref[:, :, :local] = q.reshape(fb, rows, local)
    qkv_ref[:, :, local : 2 * local] = k.reshape(fb, rows, local)
    qkv_ref[:, :, 2 * local :] = y[:, 2 * local :].astype(BF).reshape(fb, rows, local)


def qkv_call(items, cs, w_local, gain, shift):
    count = len(items)
    frames, width, dim = items[0].shape
    local = w_local.shape[1] // 3
    rows = count * width
    fb = max(1, min(frames, 512 // rows))
    while frames % fb:
        fb -= 1
    shapes = [
        jax.ShapeDtypeStruct((frames, rows, dim), BF),
        jax.ShapeDtypeStruct((frames, rows, 3 * local), BF),
    ]
    return pl.pallas_call(
        functools.partial(qkv_kernel, count, local),
        grid=(frames // fb,),
        in_specs=[pl.BlockSpec((fb, width, dim), lambda i: (i, 0, 0))] * count
        + [
            pl.BlockSpec((fb, rows, 256), lambda i: (i, 0, 0)),
            full(w_local.shape),
            full(gain.shape),
            full(shift.shape),
        ],
        out_specs=[pl.BlockSpec((fb,) + s.shape[1:], lambda i: (i, 0, 0)) for s in shapes],
        out_shape=shapes,
        compiler_params=params("arbitrary"),
        cost_estimate=cost(
            2 * frames * rows * dim * 3 * local,
            frames * rows * (4 * dim + 1024 + 6 * local) + 6 * dim * local,
        ),
        name="qkv",
    )(*items, cs, w_local, gain, shift)


def lane_halves(shape):
    lane = lax.broadcasted_iota(jnp.int32, shape, 1)
    return lane < 64


def attend_kernel(groups, local, patches, most, info_ref, *refs):
    ins = refs[:groups]
    o_refs = refs[groups : groups + patches]
    of_ref, lse_ref = refs[groups + patches :]
    f = pl.program_id(0)
    begin = info_ref[1 + f]
    q = jnp.concatenate([r[f, :, :local] for r in ins], axis=0)
    rows = q.shape[0]
    low = lane_halves((rows, 128))
    one = jnp.ones((rows, 128), BF)
    zero = jnp.zeros((rows, 128), BF)
    lane = lax.broadcasted_iota(jnp.int32, (rows, 128), 1)

    def keys(g, at):
        return jnp.concatenate([r[g, :, at : at + 128] for r in ins], axis=0)

    def finish(pair, tops, accs, lses):
        num = jnp.where(low, accs[0], accs[1])
        den = pltpu.roll(jnp.where(low, accs[1], accs[0]), 64, 1)
        of_ref[0, :, pair * 128 : (pair + 1) * 128] = num / den
        logs = jnp.log(jnp.where(low, accs[1], accs[0]))
        lses = jnp.where(lane == 2 * pair + 64, tops[0] + logs, lses)
        return jnp.where(lane == 2 * pair + 1, tops[1] + logs, lses)

    def store(lses):
        even = lane % 2 == 0
        lses = jnp.where(even, pltpu.roll(lses, 64, 1), lses)
        lse_ref[0] = lses.T[:8]

    def whole(count):
        lses = jnp.zeros((rows, 128), F32)
        for pair in range(local // 128):
            at = pair * 128
            tops, accs = [], []
            for h in range(2):
                qm = jnp.where(low == (h == 0), q[:, at : at + 128], zero)
                scores = [nt(qm, keys(begin + n, local + at)) for n in range(count)]
                top = scores[0]
                for s in scores[1:]:
                    top = jnp.maximum(top, s)
                top = jnp.max(top, axis=1, keepdims=True)
                acc = None
                for n, s in enumerate(scores):
                    v = jnp.where(low == (h == 0), keys(begin + n, 2 * local + at), one)
                    part = nn(jnp.exp(s - top).astype(BF), v)
                    acc = part if acc is None else acc + part
                tops.append(top)
                accs.append(acc)
            lses = finish(pair, tops, accs, lses)
        store(lses)

    if most <= 4:
        for count in range(1, most + 1):
            pl.when(f + 1 - begin == count)(functools.partial(whole, count))
    else:
        lses = jnp.zeros((rows, 128), F32)
        for pair in range(local // 128):
            at = pair * 128

            def body(g, state):
                new = []
                for h in range(2):
                    top, acc = state[2 * h : 2 * h + 2]
                    qm = jnp.where(low == (h == 0), q[:, at : at + 128], zero)
                    s = nt(qm, keys(g, local + at))
                    new_top = jnp.maximum(top, jnp.max(s, axis=1, keepdims=True))
                    v = jnp.where(low == (h == 0), keys(g, 2 * local + at), one)
                    p = jnp.exp(s - new_top).astype(BF)
                    new += [new_top, acc * jnp.exp(top - new_top) + nn(p, v)]
                return tuple(new)

            blank = (jnp.full((rows, 1), MASKED, F32), jnp.zeros((rows, 128), F32))
            state = lax.fori_loop(begin, f + 1, body, blank + blank)
            lses = finish(pair, state[0::2], state[1::2], lses)
        store(lses)

    o = of_ref[0].astype(BF)
    width = rows // patches
    for j in range(patches):
        o_refs[j][0] = o[j * width : (j + 1) * width]


def attend_call(info, qkv, patches):
    groups = len(qkv)
    frames = qkv[0].shape[0]
    local = qkv[0].shape[2] // 3
    rows = sum(a.shape[1] for a in qkv)
    width = rows // patches
    shapes = [jax.ShapeDtypeStruct((frames, width, local), BF)] * patches
    shapes += [
        jax.ShapeDtypeStruct((frames, rows, local), F32),
        jax.ShapeDtypeStruct((frames, 8, rows), F32),
    ]
    return pl.pallas_call(
        functools.partial(attend_kernel, groups, local, patches, frames // 2),
        grid=(frames,),
        in_specs=[smem()] + [full(a.shape) for a in qkv],
        out_specs=[pl.BlockSpec((1,) + s.shape[1:], lambda i: (i, 0, 0)) for s in shapes],
        out_shape=shapes,
        compiler_params=params("arbitrary"),
        cost_estimate=cost(
            2 * 2 * 2 * frames * rows * rows * 2 * local, 14 * frames * rows * local
        ),
        name="attend",
    )(info, *qkv)


def attend_back_kernel(groups, local, patches, after, info_ref, *refs):
    refs = refs[after:]
    ins = refs[:groups]
    css = refs[groups : 2 * groups]
    do_refs = refs[2 * groups : 2 * groups + patches]
    refs = refs[2 * groups + patches :]
    of_ref, lse_ref = refs[:2]
    outs = refs[2 : groups + 2]
    dk_ref, dv_ref, dq_ref, kt_ref = refs[groups + 2 :]
    f = pl.program_id(0)
    frames = pl.num_programs(0)
    begin = info_ref[1 + f]
    q = jnp.concatenate([r[f, :, :local] for r in ins], axis=0)
    d_o = jnp.concatenate([r[0] for r in do_refs], axis=0)
    rows = q.shape[0]
    low = lane_halves((rows, 128))
    zero = jnp.zeros((rows, 128), BF)
    turned = (d_o.astype(F32) * of_ref[0]).T
    delta = [
        jnp.sum(turned[h * 64 : (h + 1) * 64], axis=0, keepdims=True) for h in range(local // 64)
    ]
    lse = lse_ref[0]
    dk_ref[f] = jnp.zeros((rows, local), F32)
    dv_ref[f] = jnp.zeros((rows, local), F32)
    dq_ref[...] = jnp.zeros((local, rows), F32)
    kt_ref[f] = jnp.concatenate([r[f, :, local : 2 * local] for r in ins], axis=0).T

    def masked(a):
        return [
            [jnp.where(low == (h == 0), a[:, at : at + 128], zero) for h in range(2)]
            for at in range(0, local, 128)
        ]

    qm = masked(q)
    dom = masked(d_o)

    @pl.loop(begin, f + 1)
    def _(g):
        for pair in range(local // 128):
            at = pair * 128
            k = jnp.concatenate([r[g, :, local + at : local + at + 128] for r in ins], axis=0)
            v = jnp.concatenate(
                [r[g, :, 2 * local + at : 2 * local + at + 128] for r in ins], axis=0
            )
            dk = dv = None
            for h in range(2):
                head = 2 * pair + h
                p = jnp.exp(nt(k, qm[pair][h]) - lse[head : head + 1])
                dp = nt(v, dom[pair][h])
                ds = (p * (dp - delta[head])).astype(BF)
                dq_ref[head * 64 : (head + 1) * 64] += nn(
                    kt_ref[g, head * 64 : (head + 1) * 64], ds
                )
                part_k = nn(ds, qm[pair][h])
                part_v = nn(p.astype(BF), dom[pair][h])
                dk = part_k if dk is None else dk + part_k
                dv = part_v if dv is None else dv + part_v
            dk_ref[g, :, at : at + 128] += dk
            dv_ref[g, :, at : at + 128] += dv

    def tables(t):
        cs = jnp.concatenate([r[t] for r in css], axis=0)
        return widen(cs[:, :128], local), widen(cs[:, 128:], local)

    def put(t, at, value):
        start = 0
        for out in outs:
            n = out.shape[1]
            out[t, :, at * local : (at + 1) * local] = value[start : start + n]
            start += n

    cos, sin = tables(f)
    dq = dq_ref[...].T * 0.125
    put(f, 0, (dq * cos - partner(dq) * sin).astype(BF))

    @pl.when(f == frames - 1)
    def _():
        @pl.loop(0, frames)
        def _(t):
            cos, sin = tables(t)
            dk = dk_ref[t]
            put(t, 1, (dk * cos - partner(dk) * sin).astype(BF))
            put(t, 2, dv_ref[t].astype(BF))


def attend_back_call(info, qkv, cs, d_o, o_full, lse, patches, after=()):
    groups = len(qkv)
    frames = qkv[0].shape[0]
    local = qkv[0].shape[2] // 3
    rows = sum(a.shape[1] for a in qkv)
    width = rows // patches
    shapes = [jax.ShapeDtypeStruct((frames, a.shape[1], 3 * local), BF) for a in qkv]
    return pl.pallas_call(
        functools.partial(attend_back_kernel, groups, local, patches, len(after)),
        grid=(frames,),
        in_specs=[smem()]
        + [pl.BlockSpec(memory_space=pl.ANY)] * len(after)
        + [full(a.shape) for a in qkv]
        + [full(a.shape) for a in cs]
        + [pl.BlockSpec((1, width, local), lambda i: (i, 0, 0))] * patches
        + [
            pl.BlockSpec((1, rows, local), lambda i: (i, 0, 0)),
            pl.BlockSpec((1, 8, rows), lambda i: (i, 0, 0)),
        ],
        out_specs=[full(s.shape) for s in shapes],
        out_shape=shapes,
        scratch_shapes=[
            pltpu.VMEM((frames, rows, local), F32),
            pltpu.VMEM((frames, rows, local), F32),
            pltpu.VMEM((local, rows), F32),
            pltpu.VMEM((frames, local, rows), BF),
        ],
        compiler_params=params("arbitrary"),
        cost_estimate=cost(
            5 * 2 * 2 * frames * rows * rows * 2 * local, 20 * frames * rows * local
        ),
        name="attend_back",
    )(info, *after, *qkv, *cs, *d_o, o_full, lse)


def heads_rows(info_ref, j, local):
    return pl.ds(pl.multiple_of((info_ref[0] ^ j) * local, local), local)


def project_kernel(patches, info_ref, *refs):
    o_refs = refs[:patches]
    x_ref, w_ref, gain_ref, shift_ref, x1_ref, h_ref = refs[patches:]
    fb, width, local = o_refs[0].shape
    rows = fb * width
    acc = x_ref[...].astype(F32).reshape(rows, -1)
    for j, o_ref in enumerate(o_refs):
        acc = acc + nn(o_ref[...].reshape(rows, local), w_ref[heads_rows(info_ref, j, local), :])
    x1_ref[...] = acc
    hat, _ = normalise(acc)
    h_ref[...] = (hat * gain_ref[...] + shift_ref[...]).astype(BF)


def project_call(info, o_in, tokens, w_out, gain, shift):
    patches = len(o_in)
    frames, width, local = o_in[0].shape
    dim = w_out.shape[0]
    fb = frames // 2
    rows = frames * width
    return pl.pallas_call(
        functools.partial(project_kernel, patches),
        grid=(2,),
        in_specs=[smem()]
        + [pl.BlockSpec((fb, width, local), lambda i: (i, 0, 0))] * patches
        + [
            pl.BlockSpec((fb, width, dim), lambda i: (i, 0, 0)),
            full(w_out.shape),
            full(gain.shape),
            full(shift.shape),
        ],
        out_specs=[
            pl.BlockSpec((rows // 2, dim), lambda i: (i, 0)),
            pl.BlockSpec((rows // 2, dim), lambda i: (i, 0)),
        ],
        out_shape=[
            jax.ShapeDtypeStruct((rows, dim), F32),
            jax.ShapeDtypeStruct((rows, dim), BF),
        ],
        compiler_params=params("arbitrary"),
        cost_estimate=cost(2 * rows * dim * dim, rows * dim * 10 + 2 * dim * dim),
        name="project",
    )(info, *o_in, tokens, w_out, gain, shift)


def hidden_block(hidden, patches):
    tile = min(256, hidden // patches)
    per = hidden // patches // tile

    def at(i, info):
        return ((i // per) * 2 + (info[0] & 1)) * per + i % per

    return tile, per, hidden // 2 // tile, at


def pre_kernel(info_ref, dy_own, dy_mate, down_ref, dg_ref):
    half = dy_own.shape[0]
    dg_ref[:half] = nt(dy_own[...], down_ref[...]).astype(BF)
    dg_ref[half:] = nt(dy_mate[...], down_ref[...]).astype(BF)


def pre_call(info, dy_own, dy_mate, w_down, patches):
    half, dim = dy_own.shape
    hidden = w_down.shape[0]
    tile, _, steps, at = hidden_block(hidden, patches)
    return pl.pallas_call(
        pre_kernel,
        grid_spec=pltpu.PrefetchScalarGridSpec(
            num_scalar_prefetch=1,
            grid=(steps,),
            in_specs=[full((half, dim))] * 2
            + [pl.BlockSpec((tile, dim), lambda i, info: (at(i, info), 0))],
            out_specs=pl.BlockSpec((2 * half, tile), lambda i, info: (0, i)),
        ),
        out_shape=jax.ShapeDtypeStruct((2 * half, hidden // 2), BF),
        compiler_params=params("arbitrary"),
        cost_estimate=cost(2 * half * dim * hidden, 6 * dim * hidden // 2),
        name="pre",
    )(info, dy_own, dy_mate, w_down)


def ffn_kernel(
    info_ref, h_own, h_mate, dy_own, dy_mate, dg_ref, up_ref,
    g_ref, du_ref, dh_own, dh_mate, dw_ref, acc_ref,
):
    step = pl.program_id(0)
    w_up = up_ref[...]
    half = h_own.shape[0]
    total = None
    for n, (h_ref, dy_ref) in enumerate(((h_own, dy_own), (h_mate, dy_mate))):
        rows = slice(n * half, (n + 1) * half)
        u = nn(h_ref[...], w_up)
        cdf = 0.5 + 0.5 * lax.erf(u * math.sqrt(0.5))
        pdf = jnp.exp(u * u * -0.5) * (1.0 / math.sqrt(2.0 * math.pi))
        g = (u * cdf).astype(BF)
        du = (dg_ref[rows].astype(F32) * (cdf + u * pdf)).astype(BF)
        g_ref[rows] = g
        du_ref[rows] = du
        part = nt(du, w_up)

        @pl.when(step == 0)
        def _():
            acc_ref[rows] = part

        @pl.when(step > 0)
        def _():
            acc_ref[rows] += part

        dw = tn(g, dy_ref[...])
        total = dw if total is None else total + dw
    blocked(dw_ref, total)

    @pl.when(step == pl.num_programs(0) - 1)
    def _():
        dh_own[...] = acc_ref[:half]
        dh_mate[...] = acc_ref[half:].astype(BF)


def ffn_call(info, h_own, h_mate, dy_own, dy_mate, dg, w_up, patches):
    half, dim = h_own.shape
    hidden = w_up.shape[1]
    tile, _, steps, at = hidden_block(hidden, patches)
    column = pl.BlockSpec((2 * half, tile), lambda i, info: (0, i))
    grid_spec = pltpu.PrefetchScalarGridSpec(
        num_scalar_prefetch=1,
        grid=(steps,),
        in_specs=[full((half, dim))] * 4
        + [column, pl.BlockSpec((dim, tile), lambda i, info: (0, at(i, info)))],
        out_specs=[
            column,
            column,
            full((half, dim)),
            full((half, dim)),
            pl.BlockSpec((dim // 128, tile, 128), lambda i, info: (0, i, 0)),
        ],
        scratch_shapes=[pltpu.VMEM((2 * half, dim), F32)],
    )
    return pl.pallas_call(
        ffn_kernel,
        grid_spec=grid_spec,
        out_shape=[
            jax.ShapeDtypeStruct((2 * half, hidden // 2), BF),
            jax.ShapeDtypeStruct((2 * half, hidden // 2), BF),
            jax.ShapeDtypeStruct((half, dim), F32),
            jax.ShapeDtypeStruct((half, dim), BF),
            jax.ShapeDtypeStruct((dim // 128, hidden // 2, 128), BF),
        ],
        compiler_params=params("arbitrary"),
        cost_estimate=cost(6 * 2 * half * dim * hidden // 2, 4 * dim * hidden),
        name="ffn",
    )(info, h_own, h_mate, dy_own, dy_mate, dg, w_up)


def ffn_rest_kernel(
    info_ref, h_own, h_mate, x1_ref, g_ref, du_ref, down_ref,
    dw_ref, out_own, out_mate, ht_ref, acc_ref,
):
    step = pl.program_id(0)
    half = h_own.shape[0]

    @pl.when(step == 0)
    def _():
        ht_ref[:, :half] = h_own[...].T
        ht_ref[:, half:] = h_mate[...].T
        acc_ref[:half] = x1_ref[...]
        acc_ref[half:] = jnp.zeros_like(x1_ref)

    blocked(dw_ref, nn(ht_ref[...], du_ref[...]))
    for n in range(2):
        rows = slice(n * half, (n + 1) * half)
        acc_ref[rows] += nn(g_ref[rows], down_ref[...])

    @pl.when(step == pl.num_programs(0) - 1)
    def _():
        out_own[...] = acc_ref[:half]
        out_mate[...] = acc_ref[half:].astype(BF)


def ffn_rest_call(info, h_own, h_mate, x1, g, du, w_down, patches):
    half, dim = h_own.shape
    hidden = w_down.shape[0]
    tile, per, steps, at = hidden_block(hidden, patches)
    grid_spec = pltpu.PrefetchScalarGridSpec(
        num_scalar_prefetch=1,
        grid=(steps,),
        in_specs=[full((half, dim))] * 3
        + [
            pl.BlockSpec((2 * half, tile), lambda i, info: (0, i)),
            pl.BlockSpec((2 * half, tile), lambda i, info: (0, i)),
            pl.BlockSpec((tile, dim), lambda i, info: (at(i, info), 0)),
        ],
        out_specs=[
            pl.BlockSpec((tile // 128, dim, 128), lambda i, info: (i, 0, 0)),
            full((half, dim)),
            full((half, dim)),
        ],
        scratch_shapes=[pltpu.VMEM((dim, 2 * half), BF), pltpu.VMEM((2 * half, dim), F32)],
    )
    return pl.pallas_call(
        ffn_rest_kernel,
        grid_spec=grid_spec,
        out_shape=[
            jax.ShapeDtypeStruct((hidden // 256, dim, 128), BF),
            jax.ShapeDtypeStruct((half, dim), F32),
            jax.ShapeDtypeStruct((half, dim), BF),
        ],
        compiler_params=params("arbitrary"),
        cost_estimate=cost(4 * 2 * half * dim * hidden // 2, 6 * dim * hidden),
        name="ffn_rest",
    )(info, h_own, h_mate, x1, g, du, w_down)


def mid_kernel(
    patches, info_ref, dh_ref, recv_ref, x1_ref, dy_ref, w_ref, gain_ref, dx_ref, da_ref, gs_ref,
    *do_refs,
):
    step = pl.program_id(0)
    fb, width, local = do_refs[0].shape
    hat, rstd = normalise(x1_ref[...])
    dh = dh_ref[...] + recv_ref[...].astype(F32)
    dx = dy_ref[...].astype(F32) + norm_back(dh, hat, rstd, gain_ref[...])
    dx_ref[...] = dx
    da = dx.astype(BF)
    da_ref[...] = da
    sums = jnp.concatenate(
        [jnp.sum(dh * hat, axis=0, keepdims=True), jnp.sum(dh, axis=0, keepdims=True)], axis=0
    )

    @pl.when(step == 0)
    def _():
        gs_ref[...] = sums

    @pl.when(step > 0)
    def _():
        gs_ref[...] += sums

    for j, do_ref in enumerate(do_refs):
        part = nt(da, w_ref[heads_rows(info_ref, j, local), :])
        do_ref[...] = part.astype(BF).reshape(fb, width, local)


def mid_call(info, dh, recv, x1, dy, w_out, gain, frames, patches):
    rows, dim = x1.shape
    width = rows // frames
    local = dim // patches
    fb = frames // 2
    row = pl.BlockSpec((rows // 2, dim), lambda i: (i, 0))
    return pl.pallas_call(
        functools.partial(mid_kernel, patches),
        grid=(2,),
        in_specs=[smem(), row, row, row, row, full(w_out.shape), full(gain.shape)],
        out_specs=[row, row, full((2, dim))]
        + [pl.BlockSpec((fb, width, local), lambda i: (i, 0, 0))] * patches,
        out_shape=[
            jax.ShapeDtypeStruct((rows, dim), F32),
            jax.ShapeDtypeStruct((rows, dim), BF),
            jax.ShapeDtypeStruct((2, dim), F32),
        ]
        + [jax.ShapeDtypeStruct((frames, width, local), BF)] * patches,
        compiler_params=params("arbitrary"),
        cost_estimate=cost(2 * rows * dim * dim, rows * dim * 20 + 2 * dim * dim),
        name="mid",
    )(info, dh, recv, x1, dy, w_out, gain)


def dwo_kernel(patches, info_ref, *refs):
    o_refs, da_ref, dw_ref = refs[:patches], refs[patches], refs[patches + 1]
    frames, width, local = o_refs[0].shape
    for j, o_ref in enumerate(o_refs):
        part = tn(o_ref[...].reshape(frames * width, local), da_ref[...]).astype(BF)
        at = heads_rows(info_ref, j, local)
        for n in range(dw_ref.shape[0]):
            dw_ref[n, at, :] = part[:, n * 128 : (n + 1) * 128]


def dwo_call(info, o_in, da):
    patches = len(o_in)
    dim = da.shape[1]
    shape = (dim // 128, dim, 128)
    return pl.pallas_call(
        functools.partial(dwo_kernel, patches),
        grid=(1,),
        in_specs=[smem()] + [full(a.shape) for a in o_in] + [full(da.shape)],
        out_specs=full(shape),
        out_shape=jax.ShapeDtypeStruct(shape, BF),
        compiler_params=params("arbitrary"),
        cost_estimate=cost(2 * da.shape[0] * dim * dim, 6 * dim * dim),
        name="dwo",
    )(info, *o_in, da)


def dqkv_kernel(groups, *refs):
    hs = refs[:groups]
    ds = refs[groups : 2 * groups]
    w_ref = refs[2 * groups]
    dh = refs[2 * groups + 1 : 3 * groups + 1]
    dw_ref = refs[3 * groups + 1]
    acc_ref = refs[3 * groups + 2]
    step = pl.program_id(0)
    total = None
    for h_ref, d_ref, out in zip(hs, ds, dh):
        fb, rows, dim = h_ref.shape
        d = d_ref[...].reshape(fb * rows, -1)
        out[...] = nt(d, w_ref[...]).astype(BF).reshape(fb, rows, dim)
        part = tn(h_ref[...].reshape(fb * rows, dim), d)
        total = part if total is None else total + part

    @pl.when(step == 0)
    def _():
        acc_ref[...] = total

    @pl.when(step > 0)
    def _():
        acc_ref[...] += total

    @pl.when(step == pl.num_programs(0) - 1)
    def _():
        blocked(dw_ref, acc_ref)


def dqkv_call(hs, ds, w_local):
    groups = len(hs)
    frames = hs[0].shape[0]
    dim, cols = w_local.shape
    rows = sum(a.shape[1] for a in hs)
    fb = max(1, min(frames, 512 // rows))

    def blocks(a):
        return pl.BlockSpec((fb,) + a.shape[1:], lambda i: (i, 0, 0))

    shapes = [jax.ShapeDtypeStruct(a.shape, BF) for a in hs]
    shapes.append(jax.ShapeDtypeStruct((cols // 128, dim, 128), BF))
    return pl.pallas_call(
        functools.partial(dqkv_kernel, groups),
        grid=(frames // fb,),
        in_specs=[blocks(a) for a in hs] + [blocks(a) for a in ds] + [full(w_local.shape)],
        out_specs=[blocks(a) for a in hs] + [full((cols // 128, dim, 128))],
        out_shape=shapes,
        scratch_shapes=[pltpu.VMEM((dim, cols), F32)],
        compiler_params=params("arbitrary"),
        cost_estimate=cost(4 * frames * rows * dim * cols, frames * rows * 4 * dim),
        name="dqkv",
    )(*hs, *ds, w_local)


def last_kernel(a_ref, b_ref, x_ref, dx_ref, gain_ref, gt_ref, gs_ref):
    step = pl.program_id(0)
    hat, rstd = normalise(x_ref[...].astype(F32))
    dh = a_ref[...].astype(F32) + b_ref[...].astype(F32)
    gt_ref[...] = (dx_ref[...] + norm_back(dh, hat, rstd, gain_ref[...])).astype(BF)
    sums = jnp.concatenate(
        [jnp.sum(dh * hat, axis=0, keepdims=True), jnp.sum(dh, axis=0, keepdims=True)], axis=0
    )

    @pl.when(step == 0)
    def _():
        gs_ref[...] = sums

    @pl.when(step > 0)
    def _():
        gs_ref[...] += sums


def last_call(a, b, x, dx, gain):
    rows, dim = x.shape
    row = pl.BlockSpec((rows // 2, dim), lambda i: (i, 0))
    return pl.pallas_call(
        last_kernel,
        grid=(2,),
        in_specs=[row, row, row, row, full(gain.shape)],
        out_specs=[row, full((2, dim))],
        out_shape=[
            jax.ShapeDtypeStruct((rows, dim), BF),
            jax.ShapeDtypeStruct((2, dim), F32),
        ],
        compiler_params=params("arbitrary"),
        cost_estimate=cost(40 * rows * dim, rows * dim * 12),
        name="last",
    )(a, b, x, dx, gain)


class Chain:
    def __init__(self, hops):
        self.hops, self.value, self.got, self.begun, self.done = hops, None, None, False, False

    def request(self):
        try:
            return self.hops.send(self.got) if self.begun else next(self.hops)
        except StopIteration as stop:
            self.value, self.done = stop.value, True
            return None
        finally:
            self.begun = True


class Stage:
    def __init__(self, links):
        self.links, self.moves = links, []

    def step(self, *chains):
        wanted = {}
        for chain in chains:
            if chain.done:
                continue
            request = chain.request()
            if request is not None:
                wanted.setdefault(request[0], []).append((chain, request[1]))
        for bit, members in wanted.items():
            arrays = [a for _, a in members]
            if bit == "patch":
                sent = arrays[0] if len(arrays) == 1 else jnp.concatenate(arrays, axis=0)
                got = lax.all_to_all(sent, "patch", 1, 1, tiled=True)
            elif len(arrays) == 1:
                got = self.links.swap(arrays[0], bit)
            else:
                sent = jnp.concatenate([a.reshape(-1, 128) for a in arrays], axis=0)
                got = self.links.swap(sent, bit)
            self.moves.append((bit, members, got))

    def close(self, values):
        held, values = lax.optimization_barrier(([m[2] for m in self.moves], values))
        for (bit, members, _), got in zip(self.moves, held):
            start = 0
            for chain, a in members:
                if len(members) == 1:
                    chain.got = got
                elif bit == "patch":
                    chain.got = got[start : start + a.shape[0]]
                    start += a.shape[0]
                else:
                    n = a.size // 128
                    chain.got = got[start : start + n].reshape(a.shape)
                    start += n
        self.moves = []
        return values


class Links:
    def __init__(self, batches, patches):
        self.batches, self.patches = batches, patches
        self.patch = lax.axis_index("patch")
        self.batch = lax.axis_index("batch")
        self.bits = {"c": [("p", 1)], "y": [("b", 1)], "x": [], "z": []}
        bit = 2
        while bit < patches:
            self.bits["x"].append(("p", bit))
            bit *= 2
        bit = 2
        while bit < batches:
            self.bits["z"].append(("b", bit))
            bit *= 2

    def swap(self, a, bit):
        axis, step = bit
        step = step if axis == "p" else step * self.patches
        n = self.batches * self.patches
        return lax.ppermute(a, AXES, [(i, i ^ step) for i in range(n)])

    def swap_patch(self, a, bit):
        return self.swap(a, ("p", bit))

    def mine(self, bit):
        axis, step = bit
        return ((self.patch if axis == "p" else self.batch) // step) & 1

    def expand(self, order):
        bits = []
        for axis in order:
            one = self.bits[axis.lower()]
            bits += one if axis.islower() else one[::-1]
        return bits

    def hops(self, a, axes, order, back, trade):
        names = self.expand(axes)
        blocks, rows, _ = a.shape
        a = a.reshape((blocks,) + (2,) * len(names) + (rows // 2 ** len(names), 128))
        layout = [bit for bit in names if bit[0] == "b"]
        for bit in self.expand(order):
            at = names.index(bit) + 1
            names.pop(at - 1)
            got = yield bit, lax.dynamic_index_in_dim(a, 1 - self.mine(bit), at, keepdims=False)
            keep = lax.dynamic_index_in_dim(a, self.mine(bit), at, keepdims=False)
            a = (keep.astype(F32) + got.astype(F32)).astype(BF)
        if trade == "core":
            bit = ("p", 1)
            got = yield bit, lax.dynamic_index_in_dim(a, 1 - self.mine(bit), 1, keepdims=False)
            own = lax.dynamic_index_in_dim(a, self.mine(bit), 1, keepdims=False)
            a = self.join(own, got, bit, 0)
            a = a.reshape((2 * blocks,) + a.shape[2:])
        if trade == "patch":
            a = a.reshape((blocks, self.patches) + a.shape[-2:])
            a = yield "patch", a
            a = a.reshape((blocks * self.patches,) + a.shape[-2:])
        have = []
        for bit in self.expand(back):
            got = yield bit, a
            at = 1 + sum(layout.index(other) < layout.index(bit) for other in have)
            have.append(bit)
            a = self.join(a, got, bit, at)
        return a.reshape(a.shape[0], -1, 128)

    def join(self, a, got, bit, at):
        return jnp.where(
            self.mine(bit) == 0, jnp.stack([a, got], axis=at), jnp.stack([got, a], axis=at)
        )

    def chain(self, a, axes, order, back, trade=None):
        return Chain(self.hops(a, axes, order, back, trade))

    def apart(self, a):
        got = {0: a}
        bit = self.patches // 2
        while bit > 1:
            for j in sorted(got):
                got[j | bit] = self.swap_patch(got[j], bit)
            bit //= 2
        return got

    def items(self, a):
        got = self.apart(a)
        for j in sorted(got):
            got[j | 1] = self.swap_patch(got[j], 1)
        return got

    def deal(self, parts):
        return [parts[0]] + [self.swap_patch(parts[j], j) for j in range(1, self.patches)]


def assemble_kernel(count, order, valid, *refs):
    out = refs[count]
    pieces = [refs[n][b][:, :valid].astype(F32) for n, b in order]
    out[...] = jnp.concatenate(pieces, axis=1)


def assemble(parts, order, valid=128):
    rows = parts[0].shape[1]
    step = min(rows, 128)
    return pl.pallas_call(
        functools.partial(assemble_kernel, len(parts), order, valid),
        grid=(rows // step,),
        in_specs=[pl.BlockSpec((a.shape[0], step, 128), lambda i: (0, i, 0)) for a in parts],
        out_specs=pl.BlockSpec((step, len(order) * valid), lambda i: (i, 0)),
        out_shape=jax.ShapeDtypeStruct((rows, len(order) * valid), F32),
        compiler_params=params("arbitrary"),
        cost_estimate=cost(0, 6 * rows * len(order) * 128),
        name="assemble",
    )(*parts)


def tables(code, times):
    head = 64
    half = head // 6
    band = 2 * half
    dims = jnp.arange(head)
    freq = jnp.power(THETA, -2.0 * (dims % half).astype(F32) / band)
    places = jnp.stack([times, (code // GRID).astype(F32), (code % GRID).astype(F32)], axis=-1)
    which = jnp.minimum(dims // band, 2)
    pick = jnp.where(
        which == 0, places[..., 0:1], jnp.where(which == 1, places[..., 1:2], places[..., 2:3])
    )
    angle = pick * freq
    turned = dims < 3 * band
    cos = jnp.where(turned, jnp.cos(angle), 1.0)
    sin = jnp.where(turned, jnp.sin(angle) * jnp.where(dims % band < half, -1.0, 1.0), 0.0)
    return jnp.concatenate([cos, cos, sin, sin], axis=-1)


def per_device(
    batches, patches, tokens, cotangent, episode_frames, kinds, patch_pos,
    ln1_gain, ln1_shift, w_qkv, w_out, ln2_gain, ln2_shift, w_up, w_down,
):
    tokens = tokens[0]
    frames, width, dim = tokens.shape
    rows = frames * width
    local = dim // patches
    links = Links(batches, patches)
    me = links.patch
    core = me & 1
    gain1, shift1, gain2, shift2 = (
        a.astype(F32).reshape(1, dim) for a in (ln1_gain, ln1_shift, ln2_gain, ln2_shift)
    )
    dy = cotangent.reshape(rows, dim)

    code = jnp.where(kinds[0] == 0, patch_pos[0], 0)
    codes = links.items(code)
    codes, tokens, dy = lax.optimization_barrier((codes, tokens, dy))
    mate = links.swap_patch(tokens, 1)
    dy_mate = links.swap_patch(dy, 1)
    apart = links.apart(tokens)
    ends = jnp.cumsum(episode_frames[0])
    frame_ids = jnp.arange(frames, dtype=jnp.int32)
    starts = jnp.max(
        jnp.where(ends[None, :] <= frame_ids[:, None], ends[None, :], 0), axis=1
    )
    info = jnp.concatenate([me[None], starts]).astype(jnp.int32)
    pad = max(128, local)
    columns = []
    for n in range(3):
        columns.append(
            lax.dynamic_slice(w_qkv, (jnp.int32(0), n * dim + me * local), (dim, local))
        )
        if pad > local:
            columns.append(jnp.zeros((dim, pad - local), BF))
    w_local = jnp.concatenate(columns, axis=1)

    members = [[0, 1], list(range(2, patches))]
    css = []
    for group in members:
        place = jnp.concatenate([codes[j] for j in group], axis=1)
        times = jnp.broadcast_to(frame_ids.astype(F32)[:, None], place.shape)
        css.append(tables(place, times))
    near = qkv_call([tokens, mate], css[0], w_local, gain1, shift1)
    dg = pre_call(info, dy, dy_mate, w_down, patches)
    near, dg, apart, css = lax.optimization_barrier((near, dg, apart, css))
    far_items = []
    for j in range(2, patches, 2):
        far_items += [apart[j], links.swap_patch(apart[j], 1)]
    far = qkv_call(far_items, css[1], w_local, gain1, shift1)
    hs, qkvs = [near[0], far[0]], [near[1], far[1]]

    *o_send, o_full, lse = attend_call(info, qkvs, patches)
    o_in = links.deal([a[..., :local] for a in o_send])
    x1, h2 = project_call(info, o_in, tokens, w_out, gain2, shift2)
    h2_mate = links.swap_patch(h2, 1)
    g, du, dh_own, dh_mate, dw_down = ffn_call(
        info, h2, h2_mate, dy, dy_mate, dg, w_up, patches
    )
    dh_recv = links.swap_patch(dh_mate, 1)

    stage = Stage(links)
    half = dim // 256
    d1 = links.chain(dw_down[:half], "Xyz", "yzx", "Zy")
    d2 = links.chain(dw_down[half:], "Xyz", "zxy", "yZ")
    stage.step(d1, d2)
    dx1, da, sums2, *d_o = mid_call(
        info, dh_own, dh_recv, x1, dy, w_out, gain2, frames, patches
    )
    d_o, g, da = lax.optimization_barrier((d_o, g, da))
    do_in = links.deal(d_o)
    dw_up, out_own, out_mate = ffn_rest_call(info, h2, h2_mate, x1, g, du, w_down, patches)
    out_recv = links.swap_patch(out_mate, 1)
    dw_out = dwo_call(info, o_in, da)
    do_in, dw_up, dw_out, out_own, out_recv = stage.close(
        (do_in, dw_up, dw_out, out_own, out_recv)
    )
    out = (out_own + out_recv.astype(F32)).astype(BF)

    half = dw_up.shape[0] // 2
    u1 = links.chain(dw_up[:half], "Xcyz", "xyz", "Zy", "core")
    u2 = links.chain(dw_up[half:], "Xcyz", "yzx", "yZ", "core")
    wo = links.chain(dw_out, "Xcyz", "cxyz", "Zy")
    stage.step(d1, d2, u1, u2, wo)
    if pad > local:
        do_in = [jnp.pad(a, ((0, 0), (0, 0), (0, pad - local))) for a in do_in]
    dqkv = attend_back_call(info, qkvs, css, do_in, o_full, lse, patches)
    dqkv = stage.close(dqkv)

    stage.step(d1, d2, u1, u2)
    *dh1, dw_qkv = dqkv_call(hs, dqkv, w_local)
    dh1, dw_qkv = stage.close((dh1, dw_qkv))

    slots = []
    for group, part in zip(members, dh1):
        part = part.reshape(frames, len(group), width, dim)
        slots += [part[:, n] for n in range(len(group))]
    even = jnp.stack(slots[0::2])
    odd = links.swap_patch(jnp.stack(slots[1::2]), 1)
    half = dw_qkv.shape[0] // 2
    q1 = links.chain(dw_qkv[:half], "Xcyz", "yz", "Zy", "patch")
    q2 = links.chain(dw_qkv[half:], "Xcyz", "zy", "yZ", "patch")
    stage.step(q1, q2, d1, d2, u1, u2, wo)
    odd, even = stage.close((odd, even))
    slots = (even.astype(F32) + odd.astype(F32)).astype(BF)
    bit = patches // 2
    while bit > 2:
        n = slots.shape[0] // 2
        slots = (slots[:n].astype(F32) + links.swap_patch(slots[n:], bit).astype(F32)).astype(BF)
        bit //= 2
    got = links.swap_patch(slots[1], 2)
    stage.step(q1, q2, d1, d2, u1, wo)
    slots, got = stage.close((slots, got))
    stage.step(q1, q2, d1, d2, u1, u2, wo)
    grad_tokens, sums1 = last_call(
        slots[0].reshape(rows, dim), got.reshape(rows, dim), tokens.reshape(rows, dim), dx1, gain1
    )
    sums = jnp.concatenate([sums1, sums2], axis=0)
    sums = sums.reshape(4, patches, local).transpose(1, 0, 2)
    grad_tokens, sums = stage.close((grad_tokens, sums))
    stage.step(q1, q2, d1, d2, u1, u2, wo)
    sums = lax.all_to_all(sums, "patch", 0, 0, tiled=True)
    sums = stage.close(sums)
    stage.step(q1, q2, d1, d2, u1, u2, wo)
    sums = jnp.sum(sums, axis=0)
    sums = jnp.broadcast_to(sums[None], (batches,) + sums.shape)
    sums = lax.all_to_all(sums, "batch", 0, 0, tiled=True)
    sums = stage.close(sums)
    sums = jnp.sum(sums, axis=0)
    chains = (q1, q2, d1, d2, u1, u2, wo)
    while not all(c.done for c in chains):
        stage.step(*chains)
        sums = stage.close(sums)

    nx = patches // 2
    half = dim // 256
    down = assemble(
        [d1.value, d2.value], [(n, b) for n in range(2) for b in range(half)]
    )
    per = w_up.shape[1] // patches // 128
    half = u1.value.shape[0] // 2
    order = []
    for i in range(nx):
        for owner in range(2):
            for t in range(per):
                b = i * per + t
                order.append((0, owner * half + b) if b < half else (1, owner * half + b - half))
    up = assemble([u1.value, u2.value], order)
    grad_wo = assemble([wo.value], [(0, b) for b in range(dim // 128)])
    order = []
    half = dw_qkv.shape[0] // 2
    for n in range(3):
        for p in range(patches):
            for t in range(pad // 128):
                b = n * (pad // 128) + t
                order.append((0, b * patches + p) if b < half else (1, (b - half) * patches + p))
    qkv = assemble([q1.value, q2.value], order, min(128, local))

    return (
        out.reshape(1, frames, width, dim),
        grad_tokens.reshape(1, frames, width, dim),
        sums[0],
        sums[1],
        qkv,
        grad_wo,
        sums[2],
        sums[3],
        up,
        down,
    )


def solution(mesh):
    placed = (
        P("batch", None, "patch", None),
        P("batch", None, "patch", None),
        P("batch", None),
        P("batch", None, "patch"),
        P("batch", None, "patch"),
    ) + (P(),) * 8
    return jax.shard_map(
        functools.partial(per_device, mesh.shape["batch"], mesh.shape["patch"]),
        mesh=mesh,
        in_specs=placed,
        out_specs=(
            P("batch", None, "patch", None),
            P("batch", None, "patch", None),
            P("patch"),
            P("patch"),
            P("patch", None),
            P("patch", None),
            P("patch"),
            P("patch"),
            P("patch", None),
            P("patch", None),
        ),
        check_vma=False,
    )
```

```python
import functools
import math

import jax
import jax.numpy as jnp
from jax import lax
from jax.experimental import pallas as pl
from jax.experimental.pallas import tpu as pltpu
from jax.sharding import PartitionSpec as P

GRID = 16
EPS = 1e-06
THETA = 10000.0
MASKED = -1e30
LIMIT = 40 * 1024 * 1024
BF = jnp.bfloat16
F32 = jnp.float32
AXES = ("batch", "patch")


def nn(a, b):
    return lax.dot_general(a, b, (((1,), (0,)), ((), ())), preferred_element_type=F32)


def nt(a, b):
    return lax.dot_general(a, b, (((1,), (1,)), ((), ())), preferred_element_type=F32)


def tn(a, b):
    return lax.dot_general(a, b, (((0,), (0,)), ((), ())), preferred_element_type=F32)


def params(*semantics):
    return pltpu.CompilerParams(
        dimension_semantics=semantics, vmem_limit_bytes=LIMIT
    )


def cost(micros):
    return pl.CostEstimate(flops=int(micros * 2.875e+08), bytes_accessed=1, transcendentals=0)


def full(shape, memory=None):
    zeros = (0,) * len(shape)
    return pl.BlockSpec(shape, lambda *_: zeros)


def blocked(ref, value):
    for n in range(ref.shape[0]):
        ref[n] = value[:, n * 128 : (n + 1) * 128].astype(BF)


def hbm(a):
    return pltpu.with_memory_space_constraint(a, pltpu.HBM)


def smem():
    return pl.BlockSpec(memory_space=pltpu.SMEM)


def normalise(x):
    mean = jnp.mean(x, axis=-1, keepdims=True)
    centred = x - mean
    spread = jnp.mean(centred * centred, axis=-1, keepdims=True)
    rstd = lax.rsqrt(spread + EPS)
    return centred * rstd, rstd


def norm_back(d_h, hat, rstd, gain):
    d_hat = d_h * gain
    first = jnp.mean(d_hat, axis=-1, keepdims=True)
    second = jnp.mean(d_hat * hat, axis=-1, keepdims=True)
    return rstd * (d_hat - first - hat * second)


def partner(value):
    head = 64
    half = head // 6
    width = value.shape[1]
    ahead = jnp.concatenate([value[:, half:], value[:, :half]], axis=1)
    behind = jnp.concatenate([value[:, width - half :], value[:, : width - half]], axis=1)
    lane = lax.broadcasted_iota(jnp.int32, value.shape, 1) % head
    return jnp.where(lane % (2 * half) < half, ahead, behind)


def qkv_kernel(count, local, *refs):
    tok = refs[:count]
    cs_ref, w_ref, gain_ref, shift_ref = refs[count : count + 4]
    h_ref, qkv_ref = refs[count + 4 :]
    x = jnp.concatenate([t[...] for t in tok], axis=1)
    fb, rows, dim = x.shape
    x = x.reshape(fb * rows, dim).astype(F32)
    hat, _ = normalise(x)
    h = (hat * gain_ref[...] + shift_ref[...]).astype(BF)
    h_ref[...] = h.reshape(fb, rows, dim)
    y = nn(h, w_ref[...])
    cs = cs_ref[...].reshape(fb * rows, 256)
    cos = cs[:, :128]
    sin = cs[:, 128:]
    for at in range(0, 3 * local, 384):
        q = y[:, at : at + 128]
        k = y[:, at + 128 : at + 256]
        q = (q * cos + partner(q) * sin).astype(BF) * BF(0.125)
        k = (k * cos + partner(k) * sin).astype(BF)
        v = y[:, at + 256 : at + 384].astype(BF)
        qkv_ref[:, :, at : at + 128] = q.reshape(fb, rows, 128)
        qkv_ref[:, :, at + 128 : at + 256] = k.reshape(fb, rows, 128)
        qkv_ref[:, :, at + 256 : at + 384] = v.reshape(fb, rows, 128)


def qkv_call(items, cs, w_local, gain, shift):
    count = len(items)
    frames, width, dim = items[0].shape
    local = w_local.shape[1] // 3
    rows = count * width
    fb = max(1, min(frames, 512 // rows))
    while frames % fb:
        fb -= 1
    shapes = [
        pltpu.HBM((frames, rows, dim), BF),
        pltpu.HBM((frames, rows, 3 * local), BF),
    ]
    return pl.pallas_call(
        functools.partial(qkv_kernel, count, local),
        grid=(frames // fb,),
        in_specs=[pl.BlockSpec((fb, width, dim), lambda i: (i, 0, 0))] * count
        + [
            pl.BlockSpec((fb, rows, 256), lambda i: (i, 0, 0)),
            full(w_local.shape),
            full(gain.shape),
            full(shift.shape),
        ],
        out_specs=[
            pl.BlockSpec((fb, rows, dim), lambda i: (i, 0, 0)),
            pl.BlockSpec((fb, rows, 3 * local), lambda i: (i, 0, 0)),
        ],
        out_shape=shapes,
        compiler_params=params("arbitrary"),
        cost_estimate=cost(5.5),
        name="qkv",
    )(*items, cs, w_local, gain, shift)


def lane_halves(shape):
    lane = lax.broadcasted_iota(jnp.int32, shape, 1)
    return lane < 64


def attend_kernel(groups, local, patches, most, info_ref, *refs):
    ins = refs[:groups]
    o_refs = refs[groups : groups + patches]
    of_ref, lse_ref = refs[groups + patches :]
    f = pl.program_id(0)
    begin = info_ref[1 + f]
    rows = sum(r.shape[1] for r in ins)
    low = lane_halves((rows, 128))
    one = jnp.ones((rows, 128), BF)
    zero = jnp.zeros((rows, 128), BF)
    lane = lax.broadcasted_iota(jnp.int32, (rows, 128), 1)

    def part_of(g, pair, n):
        at = pair * 384 + n * 128
        return jnp.concatenate([r[g, :, at : at + 128] for r in ins], axis=0)

    def finish(pair, tops, accs, lses):
        num = jnp.where(low, accs[0], accs[1])
        den = pltpu.roll(jnp.where(low, accs[1], accs[0]), 64, 1)
        of_ref[0, :, pair * 128 : (pair + 1) * 128] = num / den
        logs = jnp.log(jnp.where(low, accs[1], accs[0]))
        lses = jnp.where(lane == 2 * pair + 64, tops[0] + logs, lses)
        return jnp.where(lane == 2 * pair + 1, tops[1] + logs, lses)

    def store(lses):
        even = lane % 2 == 0
        lses = jnp.where(even, pltpu.roll(lses, 64, 1), lses)
        lse_ref[0] = lses.T[:8]

    def whole(count):
        lses = jnp.zeros((rows, 128), F32)
        for pair in range(local // 128):
            q = part_of(f, pair, 0)
            tops, accs = [], []
            for h in range(2):
                qm = jnp.where(low == (h == 0), q, zero)
                scores = [nt(qm, part_of(begin + n, pair, 1)) for n in range(count)]
                top = scores[0]
                for s in scores[1:]:
                    top = jnp.maximum(top, s)
                top = jnp.max(top, axis=1, keepdims=True)
                acc = None
                for n, s in enumerate(scores):
                    v = jnp.where(low == (h == 0), part_of(begin + n, pair, 2), one)
                    part = nn(jnp.exp(s - top).astype(BF), v)
                    acc = part if acc is None else acc + part
                tops.append(top)
                accs.append(acc)
            lses = finish(pair, tops, accs, lses)
        store(lses)

    if most <= 4:
        for count in range(1, most + 1):
            pl.when(f + 1 - begin == count)(functools.partial(whole, count))
    else:
        lses = jnp.zeros((rows, 128), F32)
        for pair in range(local // 128):
            q = part_of(f, pair, 0)

            def body(g, state, pair=pair, q=q):
                new = []
                for h in range(2):
                    top, acc = state[2 * h : 2 * h + 2]
                    qm = jnp.where(low == (h == 0), q, zero)
                    s = nt(qm, part_of(g, pair, 1))
                    new_top = jnp.maximum(top, jnp.max(s, axis=1, keepdims=True))
                    v = jnp.where(low == (h == 0), part_of(g, pair, 2), one)
                    p = jnp.exp(s - new_top).astype(BF)
                    new += [new_top, acc * jnp.exp(top - new_top) + nn(p, v)]
                return tuple(new)

            blank = (jnp.full((rows, 1), MASKED, F32), jnp.zeros((rows, 128), F32))
            state = lax.fori_loop(begin, f + 1, body, blank + blank)
            lses = finish(pair, state[0::2], state[1::2], lses)
        store(lses)

    o = of_ref[0].astype(BF)
    width = rows // patches
    for j in range(patches):
        o_refs[j][0] = o[j * width : (j + 1) * width]


def attend_call(info, qkv, patches):
    groups = len(qkv)
    frames = qkv[0].shape[0]
    local = qkv[0].shape[2] // 3
    rows = sum(a.shape[1] for a in qkv)
    width = rows // patches
    shapes = [jax.ShapeDtypeStruct((frames, width, local), BF)] * patches
    sizes = [(frames, width, local)] * patches + [(frames, rows, local), (frames, 8, rows)]
    shapes += [pltpu.HBM((frames, rows, local), F32), pltpu.HBM((frames, 8, rows), F32)]
    return pl.pallas_call(
        functools.partial(attend_kernel, groups, local, patches, frames // 2),
        grid=(frames,),
        in_specs=[smem()] + [full(a.shape) for a in qkv],
        out_specs=[pl.BlockSpec((1,) + s[1:], lambda i: (i, 0, 0)) for s in sizes],
        out_shape=shapes,
        compiler_params=params("arbitrary"),
        cost_estimate=cost(12.5),
        name="attend",
    )(info, *[hbm(a) for a in qkv])


def attend_back_kernel(groups, pair, patches, info_ref, *refs):
    ins = refs[:groups]
    css = refs[groups : 2 * groups]
    do_refs = refs[2 * groups : 2 * groups + patches]
    refs = refs[2 * groups + patches :]
    of_ref, lse_ref = refs[:2]
    outs = refs[2 : groups + 2]
    dk_ref, dv_ref, dq_ref, kt_ref = refs[groups + 2 :]
    f = pl.program_id(0)
    frames = pl.num_programs(0)
    begin = info_ref[1 + f]

    def part_of(g, n):
        return jnp.concatenate([r[g, :, n * 128 : (n + 1) * 128] for r in ins], axis=0)

    q = part_of(f, 0)
    d_o = jnp.concatenate([r[0] for r in do_refs], axis=0)
    rows = q.shape[0]
    low = lane_halves((rows, 128))
    zero = jnp.zeros((rows, 128), BF)
    turned = (d_o.astype(F32) * of_ref[0]).T
    delta = [jnp.sum(turned[h * 64 : (h + 1) * 64], axis=0, keepdims=True) for h in range(2)]
    lse = lse_ref[0, 2 * pair : 2 * pair + 2]
    dk_ref[f] = jnp.zeros((rows, 128), F32)
    dv_ref[f] = jnp.zeros((rows, 128), F32)
    dq_ref[...] = jnp.zeros((128, rows), F32)
    kt_ref[f] = part_of(f, 1).T
    qm = [jnp.where(low == (h == 0), q, zero) for h in range(2)]
    dom = [jnp.where(low == (h == 0), d_o, zero) for h in range(2)]

    @pl.loop(begin, f + 1)
    def _(g):
        k = part_of(g, 1)
        v = part_of(g, 2)
        scores = [nt(k, qm[h]) for h in range(2)]
        dps = [nt(v, dom[h]) for h in range(2)]
        dk = dv = None
        for h in range(2):
            p = jnp.exp(scores[h] - lse[h : h + 1])
            ds = (p * (dps[h] - delta[h])).astype(BF)
            dq_ref[h * 64 : (h + 1) * 64] += nn(kt_ref[g, h * 64 : (h + 1) * 64], ds)
            part_k = nn(ds, qm[h])
            part_v = nn(p.astype(BF), dom[h])
            dk = part_k if dk is None else dk + part_k
            dv = part_v if dv is None else dv + part_v
        dk_ref[g] += dk
        dv_ref[g] += dv

    def turn_back(t, value):
        cs = jnp.concatenate([r[t] for r in css], axis=0)
        return (value * cs[:, :128] - partner(value) * cs[:, 128:]).astype(BF)

    def put(t, n, value):
        start = 0
        for out in outs:
            count = out.shape[1]
            out[t, :, n * 128 : (n + 1) * 128] = value[start : start + count]
            start += count

    put(f, 0, turn_back(f, dq_ref[...].T * 0.125))

    @pl.when(f == frames - 1)
    def _():
        @pl.loop(0, frames)
        def _(t):
            put(t, 1, turn_back(t, dk_ref[t]))
            put(t, 2, dv_ref[t].astype(BF))


def attend_back_call(info, qkv, cs, d_o, o_full, lse, patches, pair):
    groups = len(qkv)
    frames = qkv[0].shape[0]
    rows = sum(a.shape[1] for a in qkv)
    width = rows // patches
    shapes = [jax.ShapeDtypeStruct((frames, a.shape[1], 384), BF) for a in qkv]
    return pl.pallas_call(
        functools.partial(attend_back_kernel, groups, pair, patches),
        grid=(frames,),
        in_specs=[smem()]
        + [pl.BlockSpec(a.shape[:2] + (384,), lambda i: (0, 0, pair)) for a in qkv]
        + [full(a.shape) for a in cs]
        + [pl.BlockSpec((1, width, 128), lambda i: (i, 0, pair))] * patches
        + [
            pl.BlockSpec((1, rows, 128), lambda i: (i, 0, pair)),
            pl.BlockSpec((1, 8, rows), lambda i: (i, 0, 0)),
        ],
        out_specs=[full(s.shape) for s in shapes],
        out_shape=shapes,
        scratch_shapes=[
            pltpu.VMEM((frames, rows, 128), F32),
            pltpu.VMEM((frames, rows, 128), F32),
            pltpu.VMEM((128, rows), F32),
            pltpu.VMEM((frames, 128, rows), BF),
        ],
        compiler_params=params("arbitrary"),
        cost_estimate=cost(15),
        name="attend_back",
    )(info, *[hbm(a) for a in (*qkv, *cs)], *d_o, hbm(o_full), hbm(lse))


def heads_rows(info_ref, j, local):
    return pl.ds(pl.multiple_of((info_ref[0] ^ j) * local, local), local)


def project_kernel(patches, info_ref, *refs):
    o_refs = refs[:patches]
    x_ref, w_ref, gain_ref, shift_ref, x1_ref, h_ref, o_ref, kept_ref = refs[patches:]
    fb, width, local = o_refs[0].shape
    rows = fb * width
    for j, ref in enumerate(o_refs):
        kept_ref[j] = ref[...].reshape(rows, local)
    o = jnp.concatenate([kept_ref[info_ref[0] ^ p] for p in range(patches)], axis=1)
    o_ref[...] = o
    acc = x_ref[...].astype(F32).reshape(rows, -1) + nn(o, w_ref[...])
    x1_ref[...] = acc
    hat, _ = normalise(acc)
    h_ref[...] = (hat * gain_ref[...] + shift_ref[...]).astype(BF)


def project_call(info, o_in, tokens, w_out, gain, shift):
    patches = len(o_in)
    frames, width, local = o_in[0].shape
    dim = w_out.shape[0]
    fb = frames // 2
    rows = frames * width
    return pl.pallas_call(
        functools.partial(project_kernel, patches),
        grid=(2,),
        in_specs=[smem()]
        + [pl.BlockSpec((fb, width, local), lambda i: (i, 0, 0))] * patches
        + [
            pl.BlockSpec((fb, width, dim), lambda i: (i, 0, 0)),
            full(w_out.shape),
            full(gain.shape),
            full(shift.shape),
        ],
        out_specs=[
            pl.BlockSpec((rows // 2, dim), lambda i: (i, 0)),
            pl.BlockSpec((rows // 2, dim), lambda i: (i, 0)),
            pl.BlockSpec((rows // 2, dim), lambda i: (i, 0)),
        ],
        out_shape=[
            pltpu.HBM((rows, dim), F32),
            jax.ShapeDtypeStruct((rows, dim), BF),
            jax.ShapeDtypeStruct((rows, dim), BF),
        ],
        scratch_shapes=[pltpu.VMEM((patches, rows // 2, local), BF)],
        compiler_params=params("arbitrary"),
        cost_estimate=cost(3.7),
        name="project",
    )(info, *o_in, tokens, w_out, gain, shift)


def tile_at(piece, steps):
    return lambda i, info: ((i % steps) * 2 + (info[0] & 1)) * 2 + (
        i // steps if piece is None else piece
    )


def pre_kernel(info_ref, dy_own, dy_mate, down_ref, dg_ref):
    half = dy_own.shape[0]
    dg_ref[:half] = nt(dy_own[...], down_ref[...]).astype(BF)
    dg_ref[half:] = nt(dy_mate[...], down_ref[...]).astype(BF)


def pre_call(info, dy_own, dy_mate, w_down, patches):
    half, dim = dy_own.shape
    hidden = w_down.shape[0]
    tile, steps = hidden // patches // 2, patches // 2
    at = tile_at(None, steps)
    return pl.pallas_call(
        pre_kernel,
        grid_spec=pltpu.PrefetchScalarGridSpec(
            num_scalar_prefetch=1,
            grid=(2 * steps,),
            in_specs=[full((half, dim))] * 2
            + [pl.BlockSpec((tile, dim), lambda i, info: (at(i, info), 0))],
            out_specs=pl.BlockSpec((2 * half, tile), lambda i, info: (0, i)),
        ),
        out_shape=pltpu.HBM((2 * half, hidden // 2), BF),
        compiler_params=params("arbitrary"),
        cost_estimate=cost(8.5),
        name="pre",
    )(info, dy_own, dy_mate, w_down)


def ffn_kernel(
    info_ref, h_own, h_mate, dy_own, dy_mate, dg_ref, up_ref,
    g_ref, du_ref, dw0_ref, dw1_ref, dh_own, dh_mate, acc_ref,
):
    step = pl.program_id(0)
    half = h_own.shape[0]

    @pl.when(step == 0)
    def _():
        acc_ref[...] = jnp.zeros(acc_ref.shape, F32)

    w_up = up_ref[...]
    total = None
    chunk = half // 2
    for n in range(4):
        h_ref, dy_ref = ((h_own, dy_own), (h_mate, dy_mate))[n // 2]
        here = slice((n % 2) * chunk, (n % 2 + 1) * chunk)
        rows = slice(n * chunk, (n + 1) * chunk)
        u = nn(h_ref[here], w_up)
        cdf = 0.5 + 0.5 * lax.erf(u * math.sqrt(0.5))
        pdf = jnp.exp(u * u * -0.5) * (1.0 / math.sqrt(2.0 * math.pi))
        g = (u * cdf).astype(BF)
        du = (dg_ref[rows].astype(F32) * (cdf + u * pdf)).astype(BF)
        g_ref[rows] = g
        du_ref[rows] = du
        acc_ref[rows] += nt(du, w_up)
        dw = tn(g, dy_ref[here])
        total = dw if total is None else total + dw
    middle = total.shape[1] // 2
    blocked(dw0_ref, total[:, :middle])
    blocked(dw1_ref, total[:, middle:])

    @pl.when(step == pl.num_programs(0) - 1)
    def _():
        dh_own[...] = acc_ref[:half]
        dh_mate[...] = acc_ref[half:].astype(BF)


def ffn_call(info, h_own, h_mate, dy_own, dy_mate, dg, w_up, patches):
    half, dim = h_own.shape
    hidden = w_up.shape[1]
    tile, steps = hidden // patches // 2, patches // 2
    at = tile_at(None, steps)
    column = pl.BlockSpec((2 * half, tile), lambda i, info: (0, i))
    return pl.pallas_call(
        ffn_kernel,
        grid_spec=pltpu.PrefetchScalarGridSpec(
            num_scalar_prefetch=1,
            grid=(2 * steps,),
            in_specs=[full((half, dim))] * 4
            + [column, pl.BlockSpec((dim, tile), lambda i, info: (0, at(i, info)))],
            out_specs=[
                column,
                column,
                pl.BlockSpec((dim // 256, tile, 128), lambda i, info: (0, i, 0)),
                pl.BlockSpec((dim // 256, tile, 128), lambda i, info: (0, i, 0)),
                full((half, dim)),
                full((half, dim)),
            ],
            scratch_shapes=[pltpu.VMEM((2 * half, dim), F32)],
        ),
        out_shape=[
            pltpu.HBM((2 * half, hidden // 2), BF),
            pltpu.HBM((2 * half, hidden // 2), BF),
            pltpu.HBM((dim // 256, hidden // 2, 128), BF),
            pltpu.HBM((dim // 256, hidden // 2, 128), BF),
            pltpu.HBM((half, dim), F32),
            jax.ShapeDtypeStruct((half, dim), BF),
        ],
        compiler_params=params("arbitrary"),
        cost_estimate=cost(25),
        name="ffn",
    )(info, h_own, h_mate, hbm(dy_own), hbm(dy_mate), hbm(dg), hbm(w_up))


def up_kernel(steps, tile, h_own, h_mate, du_ref, o_own, o_mate, da_own, da_mate, dw_ref):
    half = h_own.shape[0]
    step = pl.program_id(0)
    count = tile // 128

    def put(at, value):
        for n in range(value.shape[1] // 128):
            dw_ref[at + n] = value[:, n * 128 : (n + 1) * 128].astype(BF)

    @pl.when(step < steps)
    def _():
        value = tn(h_own[...], du_ref[:half]) + tn(h_mate[...], du_ref[half:])
        put(step * count, value)

    @pl.when(step == steps)
    def _():
        put(steps * count, tn(o_own[...], da_own[...]) + tn(o_mate[...], da_mate[...]))


def up_call(info, h_own, h_mate, du, o_own, o_mate, da_own, da_mate, patches, piece):
    half, dim = h_own.shape
    columns = du.shape[1] // 2
    steps = patches // 2
    tile = columns // steps
    shape = (columns // 128 + dim // 512, dim, 128)
    quarter = pl.BlockSpec((half, dim // 4), lambda i, info: (0, (info[0] & 1) * 2 + piece))

    def kernel(info_ref, *refs):
        up_kernel(steps, tile, *refs)

    return pl.pallas_call(
        kernel,
        grid_spec=pltpu.PrefetchScalarGridSpec(
            num_scalar_prefetch=1,
            grid=(steps + 1,),
            in_specs=[full((half, dim))] * 2
            + [
                pl.BlockSpec(
                    (2 * half, tile),
                    lambda i, info: (0, piece * steps + jnp.minimum(i, steps - 1)),
                )
            ]
            + [full((half, dim))] * 2
            + [quarter] * 2,
            out_specs=full(shape),
        ),
        out_shape=jax.ShapeDtypeStruct(shape, BF),
        compiler_params=params("arbitrary"),
        cost_estimate=cost(6),
        name="up",
    )(info, hbm(h_own), hbm(h_mate), hbm(du), hbm(o_own), hbm(o_mate), hbm(da_own), hbm(da_mate))


def down_kernel(info_ref, x1_ref, g0_ref, g1_ref, down0_ref, down1_ref, own_ref, mate_ref, acc_ref):
    step = pl.program_id(0)
    half = x1_ref.shape[0]

    @pl.when(step == 0)
    def _():
        acc_ref[:half] = x1_ref[...]
        acc_ref[half:] = jnp.zeros_like(x1_ref)

    for n in range(2):
        rows = slice(n * half, (n + 1) * half)
        acc_ref[rows] += nn(g0_ref[rows], down0_ref[...]) + nn(g1_ref[rows], down1_ref[...])

    @pl.when(step == pl.num_programs(0) - 1)
    def _():
        own_ref[...] = acc_ref[:half]
        mate_ref[...] = acc_ref[half:].astype(BF)


def down_call(info, x1, g, w_down, patches):
    half, dim = x1.shape
    hidden = w_down.shape[0]
    tile, steps = hidden // patches // 2, patches // 2
    first, second = tile_at(0, steps), tile_at(1, steps)
    return pl.pallas_call(
        down_kernel,
        grid_spec=pltpu.PrefetchScalarGridSpec(
            num_scalar_prefetch=1,
            grid=(steps,),
            in_specs=[
                full((half, dim)),
                pl.BlockSpec((2 * half, tile), lambda i, info: (0, i)),
                pl.BlockSpec((2 * half, tile), lambda i, info: (0, steps + i)),
                pl.BlockSpec((tile, dim), lambda i, info: (first(i, info), 0)),
                pl.BlockSpec((tile, dim), lambda i, info: (second(i, info), 0)),
            ],
            out_specs=[full((half, dim)), full((half, dim))],
            scratch_shapes=[pltpu.VMEM((2 * half, dim), F32)],
        ),
        out_shape=[
            jax.ShapeDtypeStruct((half, dim), F32),
            jax.ShapeDtypeStruct((half, dim), BF),
        ],
        compiler_params=params("arbitrary"),
        cost_estimate=cost(8.5),
        name="down",
    )(info, hbm(x1), hbm(g), hbm(g), hbm(w_down), hbm(w_down))


def mid_kernel(
    patches, info_ref, dh_ref, recv_ref, x1_ref, dy_ref, w_ref, gain_ref, dx_ref, da_ref, gs_ref,
    *do_refs,
):
    step = pl.program_id(0)
    fb, width, local = do_refs[0].shape
    hat, rstd = normalise(x1_ref[...])
    dh = dh_ref[...] + recv_ref[...].astype(F32)
    dx = dy_ref[...].astype(F32) + norm_back(dh, hat, rstd, gain_ref[...])
    dx_ref[...] = dx
    da = dx.astype(BF)
    da_ref[...] = da
    sums = jnp.concatenate(
        [jnp.sum(dh * hat, axis=0, keepdims=True), jnp.sum(dh, axis=0, keepdims=True)], axis=0
    )

    @pl.when(step == 0)
    def _():
        gs_ref[...] = sums

    @pl.when(step > 0)
    def _():
        gs_ref[...] += sums

    for j, do_ref in enumerate(do_refs):
        part = nt(da, w_ref[heads_rows(info_ref, j, local), :])
        do_ref[...] = part.astype(BF).reshape(fb, width, local)


def mid_call(info, dh, recv, x1, dy, w_out, gain, frames, patches):
    rows, dim = x1.shape
    width = rows // frames
    local = dim // patches
    fb = frames // 2
    row = pl.BlockSpec((rows // 2, dim), lambda i: (i, 0))
    return pl.pallas_call(
        functools.partial(mid_kernel, patches),
        grid=(2,),
        in_specs=[smem(), row, row, row, row, full(w_out.shape), full(gain.shape)],
        out_specs=[row, row, full((2, dim))]
        + [pl.BlockSpec((fb, width, local), lambda i: (i, 0, 0))] * patches,
        out_shape=[
            pltpu.HBM((rows, dim), F32),
            jax.ShapeDtypeStruct((rows, dim), BF),
            jax.ShapeDtypeStruct((2, dim), F32),
        ]
        + [jax.ShapeDtypeStruct((frames, width, local), BF)] * patches,
        compiler_params=params("arbitrary"),
        cost_estimate=cost(6),
        name="mid",
    )(info, hbm(dh), recv, hbm(x1), hbm(dy), hbm(w_out), gain)


def dwq_kernel(groups, *refs):
    hs, ds = refs[:groups], refs[groups : 2 * groups]
    dw_ref, acc_ref = refs[2 * groups :]
    step = pl.program_id(0)

    @pl.when(step == 0)
    def _():
        acc_ref[...] = jnp.zeros(acc_ref.shape, F32)

    total = None
    for h_ref, d_ref in zip(hs, ds):
        fb, rows, dim = h_ref.shape
        part = tn(h_ref[...].reshape(fb * rows, dim), d_ref[...].reshape(fb * rows, -1))
        total = part if total is None else total + part
    acc_ref[...] += total

    @pl.when(step == pl.num_programs(0) - 1)
    def _():
        blocked(dw_ref, acc_ref)


def frame_blocks(a, fb):
    return pl.BlockSpec((fb,) + a.shape[1:], lambda i: (i, 0, 0))


def dwq_call(hs, ds):
    groups = len(hs)
    frames, _, dim = hs[0].shape
    fb = max(1, frames // 2 if frames <= 8 else frames // 8)
    return pl.pallas_call(
        functools.partial(dwq_kernel, groups),
        grid=(frames // fb,),
        in_specs=[frame_blocks(a, fb) for a in (*hs, *ds)],
        out_specs=full((3, dim, 128)),
        out_shape=jax.ShapeDtypeStruct((3, dim, 128), BF),
        scratch_shapes=[pltpu.VMEM((dim, 384), F32)],
        compiler_params=params("arbitrary"),
        cost_estimate=cost(4.3),
        name="dwq",
    )(*[hbm(a) for a in hs], *ds)


def dh_kernel(groups, pairs, width, *refs):
    ds = [refs[n * groups : (n + 1) * groups] for n in range(pairs)]
    w_ref, even_ref, odd_ref = refs[pairs * groups :]
    j = 0
    for n in range(groups):
        fb, rows, _ = ds[0][n].shape
        d = jnp.concatenate([ds[p][n][...] for p in range(pairs)], axis=2)
        dh = nt(d.reshape(fb * rows, -1), w_ref[...]).astype(BF).reshape(fb, rows, -1)
        for at in range(0, rows, width):
            out = odd_ref if j % 2 else even_ref
            out[j // 2] = dh[:, at : at + width]
            j += 1


def dh_call(ds, w_local, patches):
    pairs, groups = len(ds), len(ds[0])
    frames = ds[0][0].shape[0]
    rows = sum(a.shape[1] for a in ds[0])
    width = rows // patches
    dim = w_local.shape[0]
    fb = max(1, frames // 4 if frames <= 8 else frames // 16)
    shape = (patches // 2, frames, width, dim)
    block = pl.BlockSpec((patches // 2, fb, width, dim), lambda i: (0, i, 0, 0))
    return pl.pallas_call(
        functools.partial(dh_kernel, groups, pairs, width),
        grid=(frames // fb,),
        in_specs=[frame_blocks(a, fb) for d in ds for a in d] + [full(w_local.shape)],
        out_specs=[block, block],
        out_shape=[jax.ShapeDtypeStruct(shape, BF)] * 2,
        compiler_params=params("arbitrary"),
        cost_estimate=cost(5),
        name="dh",
    )(*[a for d in ds for a in d], w_local)


def last_kernel(a_ref, b_ref, x_ref, dx_ref, gain_ref, gt_ref, gs_ref):
    step = pl.program_id(0)
    hat, rstd = normalise(x_ref[...].astype(F32))
    dh = a_ref[...].astype(F32) + b_ref[...].astype(F32)
    gt_ref[...] = (dx_ref[...] + norm_back(dh, hat, rstd, gain_ref[...])).astype(BF)
    sums = jnp.concatenate(
        [jnp.sum(dh * hat, axis=0, keepdims=True), jnp.sum(dh, axis=0, keepdims=True)], axis=0
    )

    @pl.when(step == 0)
    def _():
        gs_ref[...] = sums

    @pl.when(step > 0)
    def _():
        gs_ref[...] += sums


def last_call(a, b, x, dx, gain):
    rows, dim = x.shape
    row = pl.BlockSpec((rows // 2, dim), lambda i: (i, 0))
    return pl.pallas_call(
        last_kernel,
        grid=(2,),
        in_specs=[row, row, row, row, full(gain.shape)],
        out_specs=[row, full((2, dim))],
        out_shape=[
            jax.ShapeDtypeStruct((rows, dim), BF),
            jax.ShapeDtypeStruct((2, dim), F32),
        ],
        compiler_params=params("arbitrary"),
        cost_estimate=cost(3),
        name="last",
    )(a, b, hbm(x), hbm(dx), gain)


class Chain:
    def __init__(self, hops):
        self.hops, self.value, self.got, self.begun, self.done = hops, None, None, False, False
        self.move = None

    def request(self):
        try:
            return self.hops.send(self.got) if self.begun else next(self.hops)
        except StopIteration as stop:
            self.value, self.done = stop.value, True
            return None
        finally:
            self.begun = True


class Move:
    def __init__(self, bit, members, got):
        self.bit, self.members, self.got = bit, members, got

    def settle(self, got):
        start = 0
        for chain, a in self.members:
            chain.move = None
            if len(self.members) == 1:
                chain.got = got
            elif self.bit == "patch":
                chain.got = got[start : start + a.shape[0]]
                start += a.shape[0]
            else:
                n = a.size // 128
                chain.got = got[start : start + n].reshape(a.shape)
                start += n


class Stage:
    def __init__(self, links):
        self.links = links

    def start(self, *chains):
        wanted = {}
        for chain in chains:
            if chain.done or chain.move is not None:
                continue
            request = chain.request()
            if request is not None:
                wanted.setdefault(request[0], []).append((chain, request[1]))
        for bit, members in wanted.items():
            arrays = [a for _, a in members]
            if bit == "patch":
                sent = arrays[0] if len(arrays) == 1 else jnp.concatenate(arrays, axis=0)
                got = lax.all_to_all(sent, "patch", 1, 1, tiled=True)
            elif len(arrays) == 1:
                got = self.links.swap(arrays[0], bit)
            else:
                sent = jnp.concatenate([a.reshape(-1, 128) for a in arrays], axis=0)
                got = self.links.swap(sent, bit)
            move = Move(bit, members, got)
            for chain, _ in members:
                chain.move = move

    def join(self, values, *chains):
        moves = []
        for chain in chains:
            if chain.move is not None and chain.move not in moves:
                moves.append(chain.move)
        held, values = lax.optimization_barrier(([m.got for m in moves], values))
        for move, got in zip(moves, held):
            move.settle(got)
        return values


class Links:
    def __init__(self, batches, patches):
        self.batches, self.patches = batches, patches
        self.patch = lax.axis_index("patch")
        self.batch = lax.axis_index("batch")
        self.bits = {"c": [("p", 1)], "y": [("b", 1)], "x": [], "z": []}
        bit = 2
        while bit < patches:
            self.bits["x"].append(("p", bit))
            bit *= 2
        bit = 2
        while bit < batches:
            self.bits["z"].append(("b", bit))
            bit *= 2

    def swap(self, a, bit):
        axis, step = bit
        step = step if axis == "p" else step * self.patches
        n = self.batches * self.patches
        return lax.ppermute(a, AXES, [(i, i ^ step) for i in range(n)])

    def swap_patch(self, a, bit):
        return self.swap(a, ("p", bit))

    def mine(self, bit):
        axis, step = bit
        return ((self.patch if axis == "p" else self.batch) // step) & 1

    def expand(self, order):
        if not isinstance(order, str):
            return order
        bits = []
        for axis in order:
            one = self.bits[axis.lower()]
            bits += one if axis.islower() else one[::-1]
        return bits

    def hops(self, a, axes, order, back, trade, layout):
        names = list(self.expand(axes))
        blocks, rows, _ = a.shape
        a = a.reshape((blocks,) + (2,) * len(names) + (rows // 2 ** len(names), 128))
        layout = self.expand(layout)
        for bit in self.expand(order):
            at = names.index(bit) + 1
            names.pop(at - 1)
            got = yield bit, lax.dynamic_index_in_dim(a, 1 - self.mine(bit), at, keepdims=False)
            keep = lax.dynamic_index_in_dim(a, self.mine(bit), at, keepdims=False)
            a = (keep.astype(F32) + got.astype(F32)).astype(BF)
        if trade is not None and trade != "patch":
            bit = ("p", 1)
            size = a.shape[1:]
            pairs = a[:trade].reshape((trade // 2, 2) + size)
            got = yield bit, lax.dynamic_index_in_dim(pairs, 1 - self.mine(bit), 1, keepdims=False)
            own = lax.dynamic_index_in_dim(pairs, self.mine(bit), 1, keepdims=False)
            a = jnp.concatenate([self.join(own, got, bit, 0).reshape((trade,) + size), a[trade:]])
        if trade == "patch":
            a = a.reshape((blocks, self.patches) + a.shape[-2:])
            a = yield "patch", a
            a = a.reshape((blocks * self.patches,) + a.shape[-2:])
        have = []
        for bit in self.expand(back):
            got = yield bit, a
            at = 1 + sum(layout.index(other) < layout.index(bit) for other in have)
            have.append(bit)
            a = self.join(a, got, bit, at)
        return a.reshape(a.shape[0], -1, 128)

    def join(self, a, got, bit, at):
        return jnp.where(
            self.mine(bit) == 0, jnp.stack([a, got], axis=at), jnp.stack([got, a], axis=at)
        )

    def chain(self, a, axes, order, back, trade=None, layout="yz"):
        return Chain(self.hops(a, axes, order, back, trade, layout))

    def apart(self, a):
        got = {0: a}
        bit = self.patches // 2
        while bit > 1:
            for j in sorted(got):
                got[j | bit] = self.swap_patch(got[j], bit)
            bit //= 2
        return got

    def items(self, a):
        got = self.apart(a)
        for j in sorted(got):
            got[j | 1] = self.swap_patch(got[j], 1)
        return got

    def deal(self, parts):
        return [parts[0]] + [self.swap_patch(parts[j], j) for j in range(1, self.patches)]


def assemble_kernel(count, order, valid, *refs):
    out = refs[count]
    pieces = [refs[n][b][:, :valid].astype(F32) for n, b in order]
    out[...] = jnp.concatenate(pieces, axis=1)


def assemble(parts, order, valid=128):
    rows = parts[0].shape[1]
    step = min(rows, 128)
    return pl.pallas_call(
        functools.partial(assemble_kernel, len(parts), order, valid),
        grid=(rows // step,),
        in_specs=[pl.BlockSpec((a.shape[0], step, 128), lambda i: (0, i, 0)) for a in parts],
        out_specs=pl.BlockSpec((step, len(order) * valid), lambda i: (i, 0)),
        out_shape=jax.ShapeDtypeStruct((rows, len(order) * valid), F32),
        compiler_params=params("arbitrary"),
        cost_estimate=cost(2),
        name="assemble",
    )(*parts)


def pieces_kernel(steps, a_ref, out):
    piece = pl.program_id(0) // steps
    blocks = a_ref.shape[0] // 2

    def put(n):
        for b in range(blocks):
            out[:, b * 128 : (b + 1) * 128] = a_ref[2 * b + n].astype(F32)

    for n in range(2):
        pl.when(piece == n)(functools.partial(put, n))


def pieces_call(a):
    blocks, rows, _ = a.shape
    step = min(rows, 128)
    steps = rows // step
    return pl.pallas_call(
        functools.partial(pieces_kernel, steps),
        grid=(2 * steps,),
        in_specs=[pl.BlockSpec((blocks, step, 128), lambda i: (0, i % steps, 0))],
        out_specs=pl.BlockSpec((step, blocks * 64), lambda i: (i, 0)),
        out_shape=jax.ShapeDtypeStruct((2 * rows, blocks * 64), F32),
        compiler_params=params("arbitrary"),
        cost_estimate=cost(4),
        name="pieces",
    )(a)


def tables(code, times):
    head = 64
    half = head // 6
    band = 2 * half
    dims = jnp.arange(head)
    freq = jnp.power(THETA, -2.0 * (dims % half).astype(F32) / band)
    places = jnp.stack([times, (code // GRID).astype(F32), (code % GRID).astype(F32)], axis=-1)
    which = jnp.minimum(dims // band, 2)
    pick = jnp.where(
        which == 0, places[..., 0:1], jnp.where(which == 1, places[..., 1:2], places[..., 2:3])
    )
    angle = pick * freq
    turned = dims < 3 * band
    cos = jnp.where(turned, jnp.cos(angle), 1.0)
    sin = jnp.where(turned, jnp.sin(angle) * jnp.where(dims % band < half, -1.0, 1.0), 0.0)
    return jnp.concatenate([cos, cos, sin, sin], axis=-1)


def per_device(
    batches, patches, tokens, cotangent, episode_frames, kinds, patch_pos,
    ln1_gain, ln1_shift, w_qkv, w_out, ln2_gain, ln2_shift, w_up, w_down,
):
    tokens = tokens[0]
    frames, width, dim = tokens.shape
    rows = frames * width
    local = dim // patches
    links = Links(batches, patches)
    me = links.patch
    core = me & 1
    gain1, shift1, gain2, shift2 = (
        a.astype(F32).reshape(1, dim) for a in (ln1_gain, ln1_shift, ln2_gain, ln2_shift)
    )
    dy = cotangent.reshape(rows, dim)

    code = jnp.where(kinds[0] == 0, patch_pos[0], 0)
    codes = links.items(code)
    codes, tokens, dy = lax.optimization_barrier((codes, tokens, dy))
    mate = links.swap_patch(tokens, 1)
    dy_mate = links.swap_patch(dy, 1)
    apart = links.apart(tokens)
    ends = jnp.cumsum(episode_frames[0])
    frame_ids = jnp.arange(frames, dtype=jnp.int32)
    starts = jnp.max(
        jnp.where(ends[None, :] <= frame_ids[:, None], ends[None, :], 0), axis=1
    )
    info = jnp.concatenate([me[None], starts]).astype(jnp.int32)
    pad = max(128, local)
    pairs = pad // 128
    valid = min(128, local)
    columns = []
    for p in range(pairs):
        for n in range(3):
            at = n * dim + me * local + p * 128
            columns.append(lax.dynamic_slice(w_qkv, (jnp.int32(0), at), (dim, valid)))
            if valid < 128:
                columns.append(jnp.zeros((dim, 128 - valid), BF))
    w_local = jnp.concatenate(columns, axis=1)

    members = [[0, 1], list(range(2, patches))]
    css = []
    for group in members:
        place = jnp.concatenate([codes[j] for j in group], axis=1)
        times = jnp.broadcast_to(frame_ids.astype(F32)[:, None], place.shape)
        css.append(tables(place, times))
    near = qkv_call([tokens, mate], css[0], w_local, gain1, shift1)
    dg = pre_call(info, dy, dy_mate, w_down, patches)
    near, dg, apart, css = lax.optimization_barrier((near, dg, apart, css))
    far_items = []
    for j in range(2, patches, 2):
        far_items += [apart[j], links.swap_patch(apart[j], 1)]
    far = qkv_call(far_items, css[1], w_local, gain1, shift1)
    hs, qkvs = [near[0], far[0]], [near[1], far[1]]

    *o_send, o_full, lse = attend_call(info, qkvs, patches)
    o_in = links.deal([a[..., :local] for a in o_send])
    x1, h2, o_own = project_call(info, o_in, tokens, w_out, gain2, shift2)
    h2_mate = links.swap_patch(h2, 1)
    o_mate = links.swap_patch(o_own, 1)
    stage = Stage(links)
    g, du, dw0, dw1, dh_own, dh_mate = ffn_call(
        info, h2, h2_mate, dy, dy_mate, dg, w_up, patches
    )
    inner, outer = links.bits["z"][:1], links.bits["z"][1:]
    ys, xs = links.bits["y"], links.bits["x"]

    def two_pieces(a):
        return a.reshape(a.shape[0] * 2, a.shape[1] // 2, 128)

    def step(held, *chains):
        held = stage.join(held, *chains)
        for chain in chains:
            stage.start(chain)
        return held

    def finish(held, *chains):
        while not all(c.done for c in chains):
            held = step(held, *chains)
        return held

    d1 = links.chain(two_pieces(dw0), "Xyz", ys + inner, "")
    d2 = links.chain(two_pieces(dw1), "Xyz", inner + ys, "")
    stage.start(d1)
    stage.start(d2)
    dh_recv = links.swap_patch(dh_mate, 1)
    dx1, da, sums2, *d_o = mid_call(
        info, dh_own, dh_recv, x1, dy, w_out, gain2, frames, patches
    )
    d_o, du, da, o_mate = lax.optimization_barrier((d_o, du, da, o_mate))
    da_mate = links.swap_patch(da, 1)
    do_in = links.deal(d_o)
    sides = (o_own, o_mate, da, da_mate)
    dw1 = up_call(info, h2, h2_mate, du, *sides, patches, 0)
    dw2 = up_call(info, h2, h2_mate, du, *sides, patches, 1)
    do_in, dw1, dw2 = step((do_in, dw1, dw2), d1, d2)
    u1 = links.chain(dw1, "Xcyz", xs + inner + ys, "")
    u2 = links.chain(dw2, "Xcyz", ys + xs + inner, "")
    stage.start(u1)
    if pad > local:
        do_in = [jnp.pad(a, ((0, 0), (0, 0), (0, pad - local))) for a in do_in]
    dqkv = attend_back_call(info, qkvs, css, do_in, o_full, lse, patches, 0)
    dwq = [dwq_call(hs, dqkv)]
    dqkv, dwq, do_in = step((dqkv, dwq, do_in), d1, d2)
    dqkv = finish(dqkv, d1, d2)
    dqkvs = [dqkv]
    d = links.chain(
        jnp.concatenate([d1.value, d2.value], axis=0),
        xs[::-1] + outer,
        outer + xs,
        outer[::-1] + inner + ys,
    )
    stage.start(d)
    stage.start(u2)
    for pair in range(1, pairs):
        dqkvs.append(attend_back_call(info, qkvs, css, do_in, o_full, lse, patches, pair))
    for one in dqkvs[1:]:
        dwq.append(dwq_call(hs, one))
    even, odd = dh_call(dqkvs, w_local, patches)
    odd, even, dwq, g = step((odd, even, dwq, g), u1, d, u2)
    odd = links.swap_patch(odd, 1)
    q = links.chain(jnp.concatenate(dwq, axis=0), "Xcyz", "yz", "zy", "patch")
    stage.start(q)
    slots = (even.astype(F32) + odd.astype(F32)).astype(BF)
    bit = patches // 2
    while bit > 2:
        n = slots.shape[0] // 2
        slots = (slots[:n].astype(F32) + links.swap_patch(slots[n:], bit).astype(F32)).astype(BF)
        bit //= 2
    got = links.swap_patch(slots[1], 2)
    out_own, out_mate = down_call(info, x1, g, w_down, patches)
    out_own, out_mate, sums2 = step((out_own, out_mate, sums2), d)
    out_recv = links.swap_patch(out_mate, 1)
    sums2 = step(sums2, u1)
    sums2 = step(sums2, d)
    sums2 = step(sums2, u2)
    sums2, out_own, out_recv = step((sums2, out_own, out_recv), q)
    out = (out_own + out_recv.astype(F32)).astype(BF)
    sums2 = step(sums2, u1, u2)
    sums2 = finish(sums2, u1, u2)
    w = jnp.concatenate([u1.value, u2.value], axis=0)
    w = w.reshape(2 * w.shape[0], -1, 128)
    w = links.chain(w, outer, outer, outer[::-1] + ys + inner, w.shape[0])
    stage.start(w)
    sums2 = step(sums2, q)
    sums2 = step(sums2, d)
    slots, got, sums2 = lax.optimization_barrier((slots, got, sums2))
    grad_tokens, sums1 = last_call(
        slots[0].reshape(rows, dim), got.reshape(rows, dim), tokens.reshape(rows, dim), dx1, gain1
    )
    sums = jnp.concatenate([sums1, sums2], axis=0)
    sums = step(sums, w)
    sums = sums.reshape(4, patches, local).transpose(1, 0, 2)
    sums = jnp.broadcast_to(sums[None], (batches,) + sums.shape)
    sums = lax.all_to_all(sums.reshape((-1,) + sums.shape[2:]), AXES, 0, 0, tiled=True)
    grad_tokens, sums = step((grad_tokens, sums), q)
    sums = jnp.sum(sums, axis=0)
    grad_tokens = step(grad_tokens, w)
    grad_tokens = step(grad_tokens, d)
    grad_tokens = step(grad_tokens, q)
    grad_tokens = step(grad_tokens, q)
    grad_tokens = step(grad_tokens, w)
    grad_tokens = step(grad_tokens, q)
    grad_tokens = step(grad_tokens, w)
    grad_tokens = step(grad_tokens, q)
    grad_tokens = finish(grad_tokens, q)
    grad_tokens = finish(grad_tokens, w)
    grad_tokens = finish(grad_tokens, d)
    down = pieces_call(d.value)

    nx = patches // 2
    each = dw1.shape[0]
    per = (each - dim // 512) // nx
    ups, wos = [], []
    for owner in range(2):
        for n in range(2):
            at = (owner * 2 + n) * each
            wos += [(0, at + nx * per + t) for t in range(dim // 512)]
    for i in range(nx):
        for owner in range(2):
            for n in range(2):
                ups += [(0, (owner * 2 + n) * each + i * per + t) for t in range(per)]
    up = assemble([w.value], ups)
    grad_wo = assemble([w.value], wos)
    order = []
    for n in range(3):
        for p in range(patches):
            order += [(0, (pair * 3 + n) * patches + p) for pair in range(pairs)]
    qkv = assemble([q.value], order, valid)

    return (
        out.reshape(1, frames, width, dim),
        grad_tokens.reshape(1, frames, width, dim),
        sums[0],
        sums[1],
        qkv,
        grad_wo,
        sums[2],
        sums[3],
        up,
        down,
    )


def solution(mesh):
    placed = (
        P("batch", None, "patch", None),
        P("batch", None, "patch", None),
        P("batch", None),
        P("batch", None, "patch"),
        P("batch", None, "patch"),
    ) + (P(),) * 8
    return jax.shard_map(
        functools.partial(per_device, mesh.shape["batch"], mesh.shape["patch"]),
        mesh=mesh,
        in_specs=placed,
        out_specs=(
            P("batch", None, "patch", None),
            P("batch", None, "patch", None),
            P("patch"),
            P("patch"),
            P("patch", None),
            P("patch", None),
            P("patch"),
            P("patch"),
            P("patch", None),
            P("patch", None),
        ),
        check_vma=False,
    )
```

```python
import functools
import math

import jax
import jax.numpy as jnp
from jax import lax
from jax.experimental import pallas as pl
from jax.experimental.pallas import tpu as pltpu
from jax.sharding import PartitionSpec as P

GRID = 16
EPS = 1e-06
THETA = 10000.0
MASKED = -1e30
LIMIT = 40 * 1024 * 1024
BF = jnp.bfloat16
F32 = jnp.float32
AXES = ("batch", "patch")


def nn(a, b):
    return lax.dot_general(a, b, (((1,), (0,)), ((), ())), preferred_element_type=F32)


def nt(a, b):
    return lax.dot_general(a, b, (((1,), (1,)), ((), ())), preferred_element_type=F32)


def tn(a, b):
    return lax.dot_general(a, b, (((0,), (0,)), ((), ())), preferred_element_type=F32)


def params(*semantics):
    return pltpu.CompilerParams(
        dimension_semantics=semantics, vmem_limit_bytes=LIMIT
    )


def cost(micros):
    return pl.CostEstimate(flops=int(micros * 2.875e+08), bytes_accessed=1, transcendentals=0)


def full(shape, memory=None):
    zeros = (0,) * len(shape)
    return pl.BlockSpec(shape, lambda *_: zeros)


def blocked(ref, value):
    for n in range(ref.shape[0]):
        ref[n] = value[:, n * 128 : (n + 1) * 128].astype(BF)


def hbm(a):
    return pltpu.with_memory_space_constraint(a, pltpu.HBM)


def smem():
    return pl.BlockSpec(memory_space=pltpu.SMEM)


def normalise(x):
    mean = jnp.mean(x, axis=-1, keepdims=True)
    centred = x - mean
    spread = jnp.mean(centred * centred, axis=-1, keepdims=True)
    rstd = lax.rsqrt(spread + EPS)
    return centred * rstd, rstd


def norm_back(d_h, hat, rstd, gain):
    d_hat = d_h * gain
    first = jnp.mean(d_hat, axis=-1, keepdims=True)
    second = jnp.mean(d_hat * hat, axis=-1, keepdims=True)
    return rstd * (d_hat - first - hat * second)


def partner(value):
    head = 64
    half = head // 6
    width = value.shape[1]
    ahead = jnp.concatenate([value[:, half:], value[:, :half]], axis=1)
    behind = jnp.concatenate([value[:, width - half :], value[:, : width - half]], axis=1)
    lane = lax.broadcasted_iota(jnp.int32, value.shape, 1) % head
    return jnp.where(lane % (2 * half) < half, ahead, behind)


def columns_kernel(info_ref, w_ref, out_ref):
    out_ref[...] = w_ref[...]


def columns_call(info, w_qkv, pairs):
    dim = w_qkv.shape[0]
    blocks = dim // 128

    def at(i, info):
        return (0, (i % 3) * blocks + info[0] * pairs + i // 3)

    return pl.pallas_call(
        columns_kernel,
        grid_spec=pltpu.PrefetchScalarGridSpec(
            num_scalar_prefetch=1,
            grid=(3 * pairs,),
            in_specs=[pl.BlockSpec((dim, 128), at)],
            out_specs=pl.BlockSpec((dim, 128), lambda i, info: (0, i)),
        ),
        out_shape=jax.ShapeDtypeStruct((dim, 384 * pairs), BF),
        compiler_params=params("arbitrary"),
        cost_estimate=cost(2),
        name="columns",
    )(info, hbm(w_qkv))


def qkv_kernel(count, local, *refs):
    tok = refs[:count]
    cs_ref, w_ref, gain_ref, shift_ref = refs[count : count + 4]
    h_ref, qkv_ref = refs[count + 4 :]
    x = jnp.concatenate([t[...] for t in tok], axis=1)
    fb, rows, dim = x.shape
    x = x.reshape(fb * rows, dim).astype(F32)
    hat, _ = normalise(x)
    h = (hat * gain_ref[...] + shift_ref[...]).astype(BF)
    h_ref[...] = h.reshape(fb, rows, dim)
    y = nn(h, w_ref[...])
    cs = cs_ref[...].reshape(fb * rows, 256)
    cos = cs[:, :128]
    sin = cs[:, 128:]
    for at in range(0, 3 * local, 384):
        q = y[:, at : at + 128]
        k = y[:, at + 128 : at + 256]
        q = (q * cos + partner(q) * sin).astype(BF) * BF(0.125)
        k = (k * cos + partner(k) * sin).astype(BF)
        v = y[:, at + 256 : at + 384].astype(BF)
        qkv_ref[:, :, at : at + 128] = q.reshape(fb, rows, 128)
        qkv_ref[:, :, at + 128 : at + 256] = k.reshape(fb, rows, 128)
        qkv_ref[:, :, at + 256 : at + 384] = v.reshape(fb, rows, 128)


def qkv_call(items, cs, w_local, gain, shift):
    count = len(items)
    frames, width, dim = items[0].shape
    local = w_local.shape[1] // 3
    rows = count * width
    fb = max(1, min(frames, 512 // rows))
    while frames % fb:
        fb -= 1
    shapes = [
        pltpu.HBM((frames, rows, dim), BF),
        pltpu.HBM((frames, rows, 3 * local), BF),
    ]
    return pl.pallas_call(
        functools.partial(qkv_kernel, count, local),
        grid=(frames // fb,),
        in_specs=[pl.BlockSpec((fb, width, dim), lambda i: (i, 0, 0))] * count
        + [
            pl.BlockSpec((fb, rows, 256), lambda i: (i, 0, 0)),
            full(w_local.shape),
            full(gain.shape),
            full(shift.shape),
        ],
        out_specs=[
            pl.BlockSpec((fb, rows, dim), lambda i: (i, 0, 0)),
            pl.BlockSpec((fb, rows, 3 * local), lambda i: (i, 0, 0)),
        ],
        out_shape=shapes,
        compiler_params=params("arbitrary"),
        cost_estimate=cost(5.5),
        name="qkv",
    )(*items, cs, w_local, gain, shift)


def lane_halves(shape):
    lane = lax.broadcasted_iota(jnp.int32, shape, 1)
    return lane < 64


def attend_kernel(groups, local, patches, most, info_ref, *refs):
    ins = refs[:groups]
    o_refs = refs[groups : groups + patches]
    of_ref, lse_ref = refs[groups + patches :]
    f = pl.program_id(0)
    begin = info_ref[1 + f]
    rows = sum(r.shape[1] for r in ins)
    low = lane_halves((rows, 128))
    one = jnp.ones((rows, 128), BF)
    zero = jnp.zeros((rows, 128), BF)
    lane = lax.broadcasted_iota(jnp.int32, (rows, 128), 1)

    def part_of(g, pair, n):
        at = pair * 384 + n * 128
        return jnp.concatenate([r[g, :, at : at + 128] for r in ins], axis=0)

    def finish(pair, tops, accs, lses):
        num = jnp.where(low, accs[0], accs[1])
        den = pltpu.roll(jnp.where(low, accs[1], accs[0]), 64, 1)
        of_ref[0, :, pair * 128 : (pair + 1) * 128] = num / den
        logs = jnp.log(jnp.where(low, accs[1], accs[0]))
        lses = jnp.where(lane == 2 * pair + 64, tops[0] + logs, lses)
        return jnp.where(lane == 2 * pair + 1, tops[1] + logs, lses)

    def store(lses):
        even = lane % 2 == 0
        lses = jnp.where(even, pltpu.roll(lses, 64, 1), lses)
        lse_ref[0] = lses.T[:8]

    def whole(count):
        lses = jnp.zeros((rows, 128), F32)
        for pair in range(local // 128):
            q = part_of(f, pair, 0)
            tops, accs = [], []
            for h in range(2):
                qm = jnp.where(low == (h == 0), q, zero)
                scores = [nt(qm, part_of(begin + n, pair, 1)) for n in range(count)]
                top = scores[0]
                for s in scores[1:]:
                    top = jnp.maximum(top, s)
                top = jnp.max(top, axis=1, keepdims=True)
                acc = None
                for n, s in enumerate(scores):
                    v = jnp.where(low == (h == 0), part_of(begin + n, pair, 2), one)
                    part = nn(jnp.exp(s - top).astype(BF), v)
                    acc = part if acc is None else acc + part
                tops.append(top)
                accs.append(acc)
            lses = finish(pair, tops, accs, lses)
        store(lses)

    if most <= 4:
        for count in range(1, most + 1):
            pl.when(f + 1 - begin == count)(functools.partial(whole, count))
    else:
        lses = jnp.zeros((rows, 128), F32)
        for pair in range(local // 128):
            q = part_of(f, pair, 0)

            def body(g, state, pair=pair, q=q):
                new = []
                for h in range(2):
                    top, acc = state[2 * h : 2 * h + 2]
                    qm = jnp.where(low == (h == 0), q, zero)
                    s = nt(qm, part_of(g, pair, 1))
                    new_top = jnp.maximum(top, jnp.max(s, axis=1, keepdims=True))
                    v = jnp.where(low == (h == 0), part_of(g, pair, 2), one)
                    p = jnp.exp(s - new_top).astype(BF)
                    new += [new_top, acc * jnp.exp(top - new_top) + nn(p, v)]
                return tuple(new)

            blank = (jnp.full((rows, 1), MASKED, F32), jnp.zeros((rows, 128), F32))
            state = lax.fori_loop(begin, f + 1, body, blank + blank)
            lses = finish(pair, state[0::2], state[1::2], lses)
        store(lses)

    o = of_ref[0].astype(BF)
    width = rows // patches
    for j in range(patches):
        o_refs[j][0] = o[j * width : (j + 1) * width]


def attend_call(info, qkv, patches):
    groups = len(qkv)
    frames = qkv[0].shape[0]
    local = qkv[0].shape[2] // 3
    rows = sum(a.shape[1] for a in qkv)
    width = rows // patches
    shapes = [jax.ShapeDtypeStruct((frames, width, local), BF)] * patches
    sizes = [(frames, width, local)] * patches + [(frames, rows, local), (frames, 8, rows)]
    shapes += [pltpu.HBM((frames, rows, local), F32), pltpu.HBM((frames, 8, rows), F32)]
    return pl.pallas_call(
        functools.partial(attend_kernel, groups, local, patches, frames // 2),
        grid=(frames,),
        in_specs=[smem()] + [full(a.shape) for a in qkv],
        out_specs=[pl.BlockSpec((1,) + s[1:], lambda i: (i, 0, 0)) for s in sizes],
        out_shape=shapes,
        compiler_params=params("arbitrary"),
        cost_estimate=cost(12.5),
        name="attend",
    )(info, *[hbm(a) for a in qkv])


def attend_back_kernel(groups, pair, patches, info_ref, *refs):
    ins = refs[:groups]
    css = refs[groups : 2 * groups]
    do_refs = refs[2 * groups : 2 * groups + patches]
    refs = refs[2 * groups + patches :]
    of_ref, lse_ref = refs[:2]
    outs = refs[2 : groups + 2]
    dk_ref, dv_ref, dq_ref, kt_ref = refs[groups + 2 :]
    f = pl.program_id(0)
    frames = pl.num_programs(0)
    begin = info_ref[1 + f]

    def part_of(g, n):
        return jnp.concatenate([r[g, :, n * 128 : (n + 1) * 128] for r in ins], axis=0)

    q = part_of(f, 0)
    d_o = jnp.concatenate([r[0] for r in do_refs], axis=0)
    rows = q.shape[0]
    low = lane_halves((rows, 128))
    zero = jnp.zeros((rows, 128), BF)
    turned = (d_o.astype(F32) * of_ref[0]).T
    delta = [jnp.sum(turned[h * 64 : (h + 1) * 64], axis=0, keepdims=True) for h in range(2)]
    lse = lse_ref[0, 2 * pair : 2 * pair + 2]
    dk_ref[f] = jnp.zeros((rows, 128), F32)
    dv_ref[f] = jnp.zeros((rows, 128), F32)
    dq_ref[...] = jnp.zeros((128, rows), F32)
    kt_ref[f] = part_of(f, 1).T
    qm = [jnp.where(low == (h == 0), q, zero) for h in range(2)]
    dom = [jnp.where(low == (h == 0), d_o, zero) for h in range(2)]

    @pl.loop(begin, f + 1)
    def _(g):
        k = part_of(g, 1)
        v = part_of(g, 2)
        scores = [nt(k, qm[h]) for h in range(2)]
        dps = [nt(v, dom[h]) for h in range(2)]
        dk = dv = None
        for h in range(2):
            p = jnp.exp(scores[h] - lse[h : h + 1])
            ds = (p * (dps[h] - delta[h])).astype(BF)
            dq_ref[h * 64 : (h + 1) * 64] += nn(kt_ref[g, h * 64 : (h + 1) * 64], ds)
            part_k = nn(ds, qm[h])
            part_v = nn(p.astype(BF), dom[h])
            dk = part_k if dk is None else dk + part_k
            dv = part_v if dv is None else dv + part_v
        dk_ref[g] += dk
        dv_ref[g] += dv

    def turn_back(t, value):
        cs = jnp.concatenate([r[t] for r in css], axis=0)
        return (value * cs[:, :128] - partner(value) * cs[:, 128:]).astype(BF)

    def put(t, n, value):
        start = 0
        for out in outs:
            count = out.shape[1]
            out[t, :, n * 128 : (n + 1) * 128] = value[start : start + count]
            start += count

    put(f, 0, turn_back(f, dq_ref[...].T * 0.125))

    @pl.when(f == frames - 1)
    def _():
        @pl.loop(0, frames)
        def _(t):
            put(t, 1, turn_back(t, dk_ref[t]))
            put(t, 2, dv_ref[t].astype(BF))


def attend_back_call(info, qkv, cs, d_o, o_full, lse, patches, pair):
    groups = len(qkv)
    frames = qkv[0].shape[0]
    rows = sum(a.shape[1] for a in qkv)
    width = rows // patches
    shapes = [jax.ShapeDtypeStruct((frames, a.shape[1], 384), BF) for a in qkv]
    return pl.pallas_call(
        functools.partial(attend_back_kernel, groups, pair, patches),
        grid=(frames,),
        in_specs=[smem()]
        + [pl.BlockSpec(a.shape[:2] + (384,), lambda i: (0, 0, pair)) for a in qkv]
        + [full(a.shape) for a in cs]
        + [pl.BlockSpec((1, width, 128), lambda i: (i, 0, pair))] * patches
        + [
            pl.BlockSpec((1, rows, 128), lambda i: (i, 0, pair)),
            pl.BlockSpec((1, 8, rows), lambda i: (i, 0, 0)),
        ],
        out_specs=[full(s.shape) for s in shapes],
        out_shape=shapes,
        scratch_shapes=[
            pltpu.VMEM((frames, rows, 128), F32),
            pltpu.VMEM((frames, rows, 128), F32),
            pltpu.VMEM((128, rows), F32),
            pltpu.VMEM((frames, 128, rows), BF),
        ],
        compiler_params=params("arbitrary"),
        cost_estimate=cost(15),
        name="attend_back",
    )(info, *[hbm(a) for a in (*qkv, *cs)], *d_o, hbm(o_full), hbm(lse))


def heads_rows(info_ref, j, local):
    return pl.ds(pl.multiple_of((info_ref[0] ^ j) * local, local), local)


def project_kernel(patches, info_ref, *refs):
    o_refs = refs[:patches]
    x_ref, w_ref, gain_ref, shift_ref, x1_ref, h_ref, o_ref, kept_ref = refs[patches:]
    fb, width, local = o_refs[0].shape
    rows = fb * width
    for j, ref in enumerate(o_refs):
        kept_ref[j] = ref[...].reshape(rows, local)
    o = jnp.concatenate([kept_ref[info_ref[0] ^ p] for p in range(patches)], axis=1)
    o_ref[...] = o
    acc = x_ref[...].astype(F32).reshape(rows, -1) + nn(o, w_ref[...])
    x1_ref[...] = acc
    hat, _ = normalise(acc)
    h_ref[...] = (hat * gain_ref[...] + shift_ref[...]).astype(BF)


def project_call(info, o_in, tokens, w_out, gain, shift):
    patches = len(o_in)
    frames, width, local = o_in[0].shape
    dim = w_out.shape[0]
    fb = frames
    rows = frames * width
    return pl.pallas_call(
        functools.partial(project_kernel, patches),
        grid=(1,),
        in_specs=[smem()]
        + [pl.BlockSpec((fb, width, local), lambda i: (i, 0, 0))] * patches
        + [
            pl.BlockSpec((fb, width, dim), lambda i: (i, 0, 0)),
            full(w_out.shape),
            full(gain.shape),
            full(shift.shape),
        ],
        out_specs=[
            pl.BlockSpec((rows, dim), lambda i: (i, 0)),
            pl.BlockSpec((rows, dim), lambda i: (i, 0)),
            pl.BlockSpec((rows, dim), lambda i: (i, 0)),
        ],
        out_shape=[
            pltpu.HBM((rows, dim), F32),
            jax.ShapeDtypeStruct((rows, dim), BF),
            jax.ShapeDtypeStruct((rows, dim), BF),
        ],
        scratch_shapes=[pltpu.VMEM((patches, rows, local), BF)],
        compiler_params=params("arbitrary"),
        cost_estimate=cost(3.7),
        name="project",
    )(info, *o_in, tokens, w_out, gain, shift)


def tile_at(piece, steps):
    return lambda i, info: ((i % steps) * 2 + (info[0] & 1)) * 2 + (
        i // steps if piece is None else piece
    )


def pre_kernel(info_ref, dy_own, dy_mate, down_ref, dg_ref):
    half = dy_own.shape[0]
    dg_ref[:half] = nt(dy_own[...], down_ref[...]).astype(BF)
    dg_ref[half:] = nt(dy_mate[...], down_ref[...]).astype(BF)


def pre_call(info, dy_own, dy_mate, w_down, patches):
    half, dim = dy_own.shape
    hidden = w_down.shape[0]
    tile, steps = hidden // patches // 2, patches // 2
    at = tile_at(None, steps)
    return pl.pallas_call(
        pre_kernel,
        grid_spec=pltpu.PrefetchScalarGridSpec(
            num_scalar_prefetch=1,
            grid=(2 * steps,),
            in_specs=[full((half, dim))] * 2
            + [pl.BlockSpec((tile, dim), lambda i, info: (at(i, info), 0))],
            out_specs=pl.BlockSpec((2 * half, tile), lambda i, info: (0, i)),
        ),
        out_shape=pltpu.HBM((2 * half, hidden // 2), BF),
        compiler_params=params("arbitrary"),
        cost_estimate=cost(8.5),
        name="pre",
    )(info, dy_own, dy_mate, w_down)


def ffn_kernel(
    info_ref, h_own, h_mate, dy_own, dy_mate, dg_ref, up_ref,
    g_ref, du_ref, keep0, send0, keep1, send1, dh_own, dh_mate, acc_ref,
):
    step = pl.program_id(0)
    half = h_own.shape[0]

    @pl.when(step == 0)
    def _():
        acc_ref[...] = jnp.zeros(acc_ref.shape, F32)

    w_up = up_ref[...]
    chunk = half // 2
    for n in range(4):
        h_ref = (h_own, h_mate)[n // 2]
        here = slice((n % 2) * chunk, (n % 2 + 1) * chunk)
        rows = slice(n * chunk, (n + 1) * chunk)
        u = nn(h_ref[here], w_up)
        cdf = 0.5 + 0.5 * lax.erf(u * math.sqrt(0.5))
        pdf = jnp.exp(u * u * -0.5) * (1.0 / math.sqrt(2.0 * math.pi))
        g = (u * cdf).astype(BF)
        du = (dg_ref[rows].astype(F32) * (cdf + u * pdf)).astype(BF)
        g_ref[rows] = g
        du_ref[rows] = du
        acc_ref[rows] += nt(du, w_up)
    total = tn(g_ref[:half], dy_own[...]) + tn(g_ref[half:], dy_mate[...])
    middle = total.shape[1] // 2
    part = total.shape[0] // 2
    for n, (keep_ref, send_ref) in enumerate(((keep0, send0), (keep1, send1))):
        value = total[:, n * middle : (n + 1) * middle]
        if n == 0:
            low, high = value[:part], value[part:]
        else:
            some = part // 2
            low = jnp.concatenate([value[:some], value[part : part + some]], axis=0)
            high = jnp.concatenate([value[some:part], value[part + some :]], axis=0)
        first = info_ref[info_ref.shape[0] - 2 + n] == 0
        blocked(keep_ref, jnp.where(first, low, high))
        blocked(send_ref, jnp.where(first, high, low))

    @pl.when(step == pl.num_programs(0) - 1)
    def _():
        dh_own[...] = acc_ref[:half]
        dh_mate[...] = acc_ref[half:].astype(BF)


def ffn_call(info, h_own, h_mate, dy_own, dy_mate, dg, w_up, patches):
    half, dim = h_own.shape
    hidden = w_up.shape[1]
    tile, steps = hidden // patches // 2, patches // 2
    at = tile_at(None, steps)
    column = pl.BlockSpec((2 * half, tile), lambda i, info: (0, i))
    return pl.pallas_call(
        ffn_kernel,
        grid_spec=pltpu.PrefetchScalarGridSpec(
            num_scalar_prefetch=1,
            grid=(2 * steps,),
            in_specs=[full((half, dim))] * 4
            + [column, pl.BlockSpec((dim, tile), lambda i, info: (0, at(i, info)))],
            out_specs=[
                column,
                column,
            ]
            + [pl.BlockSpec((dim // 256, tile // 2, 128), lambda i, info: (0, i, 0))] * 4
            + [
                full((half, dim)),
                full((half, dim)),
            ],
            scratch_shapes=[pltpu.VMEM((2 * half, dim), F32)],
        ),
        out_shape=[
            pltpu.HBM((2 * half, hidden // 2), BF),
            pltpu.HBM((2 * half, hidden // 2), BF),
        ]
        + [pltpu.HBM((dim // 256, hidden // 4, 128), BF)] * 4
        + [
            pltpu.HBM((half, dim), F32),
            jax.ShapeDtypeStruct((half, dim), BF),
        ],
        compiler_params=params("arbitrary"),
        cost_estimate=cost(25),
        name="ffn",
    )(info, h_own, h_mate, hbm(dy_own), hbm(dy_mate), hbm(dg), hbm(w_up))


def up_kernel(steps, tile, h_own, h_mate, du_ref, o_own, o_mate, da_own, da_mate, dw_ref):
    half = h_own.shape[0]
    step = pl.program_id(0)
    count = tile // 128

    def put(at, value):
        for n in range(value.shape[1] // 128):
            dw_ref[at + n] = value[:, n * 128 : (n + 1) * 128].astype(BF)

    @pl.when(step < steps)
    def _():
        value = tn(h_own[...], du_ref[:half]) + tn(h_mate[...], du_ref[half:])
        put(step * count, value)

    @pl.when(step == steps)
    def _():
        put(steps * count, tn(o_own[...], da_own[...]) + tn(o_mate[...], da_mate[...]))


def up_call(info, h_own, h_mate, du, o_own, o_mate, da_own, da_mate, patches, piece):
    half, dim = h_own.shape
    columns = du.shape[1] // 2
    steps = patches // 2
    tile = columns // steps
    shape = (columns // 128 + dim // 512, dim, 128)
    quarter = pl.BlockSpec((half, dim // 4), lambda i, info: (0, (info[0] & 1) * 2 + piece))

    def kernel(info_ref, *refs):
        up_kernel(steps, tile, *refs)

    return pl.pallas_call(
        kernel,
        grid_spec=pltpu.PrefetchScalarGridSpec(
            num_scalar_prefetch=1,
            grid=(steps + 1,),
            in_specs=[full((half, dim))] * 2
            + [
                pl.BlockSpec(
                    (2 * half, tile),
                    lambda i, info: (0, piece * steps + jnp.minimum(i, steps - 1)),
                )
            ]
            + [full((half, dim))] * 2
            + [quarter] * 2,
            out_specs=full(shape),
        ),
        out_shape=jax.ShapeDtypeStruct(shape, BF),
        compiler_params=params("arbitrary"),
        cost_estimate=cost(6),
        name="up",
    )(info, hbm(h_own), hbm(h_mate), hbm(du), hbm(o_own), hbm(o_mate), hbm(da_own), hbm(da_mate))


def down_kernel(info_ref, x1_ref, g0_ref, g1_ref, down0_ref, down1_ref, own_ref, mate_ref, acc_ref):
    step = pl.program_id(0)
    half = x1_ref.shape[0]

    @pl.when(step == 0)
    def _():
        acc_ref[:half] = x1_ref[...]
        acc_ref[half:] = jnp.zeros_like(x1_ref)

    for n in range(2):
        rows = slice(n * half, (n + 1) * half)
        acc_ref[rows] += nn(g0_ref[rows], down0_ref[...]) + nn(g1_ref[rows], down1_ref[...])

    @pl.when(step == pl.num_programs(0) - 1)
    def _():
        own_ref[...] = acc_ref[:half]
        mate_ref[...] = acc_ref[half:].astype(BF)


def down_call(info, x1, g, w_down, patches):
    half, dim = x1.shape
    hidden = w_down.shape[0]
    tile, steps = hidden // patches // 2, patches // 2
    first, second = tile_at(0, steps), tile_at(1, steps)
    return pl.pallas_call(
        down_kernel,
        grid_spec=pltpu.PrefetchScalarGridSpec(
            num_scalar_prefetch=1,
            grid=(steps,),
            in_specs=[
                full((half, dim)),
                pl.BlockSpec((2 * half, tile), lambda i, info: (0, i)),
                pl.BlockSpec((2 * half, tile), lambda i, info: (0, steps + i)),
                pl.BlockSpec((tile, dim), lambda i, info: (first(i, info), 0)),
                pl.BlockSpec((tile, dim), lambda i, info: (second(i, info), 0)),
            ],
            out_specs=[full((half, dim)), full((half, dim))],
            scratch_shapes=[pltpu.VMEM((2 * half, dim), F32)],
        ),
        out_shape=[
            jax.ShapeDtypeStruct((half, dim), F32),
            jax.ShapeDtypeStruct((half, dim), BF),
        ],
        compiler_params=params("arbitrary"),
        cost_estimate=cost(8.5),
        name="down",
    )(info, hbm(x1), hbm(g), hbm(g), hbm(w_down), hbm(w_down))


def mid_kernel(
    patches, info_ref, dh_ref, recv_ref, x1_ref, dy_ref, w_ref, gain_ref, dx_ref, da_ref, gs_ref,
    *do_refs,
):
    step = pl.program_id(0)
    fb, width, local = do_refs[0].shape
    hat, rstd = normalise(x1_ref[...])
    dh = dh_ref[...] + recv_ref[...].astype(F32)
    dx = dy_ref[...].astype(F32) + norm_back(dh, hat, rstd, gain_ref[...])
    dx_ref[...] = dx
    da = dx.astype(BF)
    da_ref[...] = da
    sums = jnp.concatenate(
        [jnp.sum(dh * hat, axis=0, keepdims=True), jnp.sum(dh, axis=0, keepdims=True)], axis=0
    )

    @pl.when(step == 0)
    def _():
        gs_ref[...] = sums

    @pl.when(step > 0)
    def _():
        gs_ref[...] += sums

    for j, do_ref in enumerate(do_refs):
        part = nt(da, w_ref[heads_rows(info_ref, j, local), :])
        do_ref[...] = part.astype(BF).reshape(fb, width, local)


def mid_call(info, dh, recv, x1, dy, w_out, gain, frames, patches):
    rows, dim = x1.shape
    width = rows // frames
    local = dim // patches
    fb = frames
    row = pl.BlockSpec((rows, dim), lambda i: (i, 0))
    return pl.pallas_call(
        functools.partial(mid_kernel, patches),
        grid=(1,),
        in_specs=[smem(), row, row, row, row, full(w_out.shape), full(gain.shape)],
        out_specs=[row, row, full((2, dim))]
        + [pl.BlockSpec((fb, width, local), lambda i: (i, 0, 0))] * patches,
        out_shape=[
            pltpu.HBM((rows, dim), F32),
            jax.ShapeDtypeStruct((rows, dim), BF),
            jax.ShapeDtypeStruct((2, dim), F32),
        ]
        + [jax.ShapeDtypeStruct((frames, width, local), BF)] * patches,
        compiler_params=params("arbitrary"),
        cost_estimate=cost(6),
        name="mid",
    )(info, hbm(dh), recv, hbm(x1), hbm(dy), hbm(w_out), gain)


def dwq_kernel(groups, *refs):
    hs, ds = refs[:groups], refs[groups : 2 * groups]
    dw_ref, acc_ref = refs[2 * groups :]
    step = pl.program_id(0)

    @pl.when(step == 0)
    def _():
        acc_ref[...] = jnp.zeros(acc_ref.shape, F32)

    total = None
    for h_ref, d_ref in zip(hs, ds):
        fb, rows, dim = h_ref.shape
        part = tn(h_ref[...].reshape(fb * rows, dim), d_ref[...].reshape(fb * rows, -1))
        total = part if total is None else total + part
    acc_ref[...] += total

    @pl.when(step == pl.num_programs(0) - 1)
    def _():
        blocked(dw_ref, acc_ref)


def frame_blocks(a, fb):
    return pl.BlockSpec((fb,) + a.shape[1:], lambda i: (i, 0, 0))


def dwq_call(hs, ds):
    groups = len(hs)
    frames, _, dim = hs[0].shape
    fb = max(1, frames // 2 if frames <= 8 else frames // 8)
    return pl.pallas_call(
        functools.partial(dwq_kernel, groups),
        grid=(frames // fb,),
        in_specs=[frame_blocks(a, fb) for a in (*hs, *ds)],
        out_specs=full((3, dim, 128)),
        out_shape=jax.ShapeDtypeStruct((3, dim, 128), BF),
        scratch_shapes=[pltpu.VMEM((dim, 384), F32)],
        compiler_params=params("arbitrary"),
        cost_estimate=cost(4.3),
        name="dwq",
    )(*[hbm(a) for a in hs], *ds)


def dh_kernel(groups, pairs, width, *refs):
    ds = [refs[n * groups : (n + 1) * groups] for n in range(pairs)]
    w_ref, even_ref, odd_ref = refs[pairs * groups :]
    j = 0
    for n in range(groups):
        fb, rows, _ = ds[0][n].shape
        d = jnp.concatenate([ds[p][n][...] for p in range(pairs)], axis=2)
        dh = nt(d.reshape(fb * rows, -1), w_ref[...]).astype(BF).reshape(fb, rows, -1)
        for at in range(0, rows, width):
            out = odd_ref if j % 2 else even_ref
            out[j // 2] = dh[:, at : at + width]
            j += 1


def dh_call(ds, w_local, patches):
    pairs, groups = len(ds), len(ds[0])
    frames = ds[0][0].shape[0]
    rows = sum(a.shape[1] for a in ds[0])
    width = rows // patches
    dim = w_local.shape[0]
    fb = max(1, frames // 4 if frames <= 8 else frames // 16)
    shape = (patches // 2, frames, width, dim)
    block = pl.BlockSpec((patches // 2, fb, width, dim), lambda i: (0, i, 0, 0))
    return pl.pallas_call(
        functools.partial(dh_kernel, groups, pairs, width),
        grid=(frames // fb,),
        in_specs=[frame_blocks(a, fb) for d in ds for a in d] + [full(w_local.shape)],
        out_specs=[block, block],
        out_shape=[jax.ShapeDtypeStruct(shape, BF)] * 2,
        compiler_params=params("arbitrary"),
        cost_estimate=cost(5),
        name="dh",
    )(*[a for d in ds for a in d], w_local)


def last_kernel(a_ref, b_ref, x_ref, dx_ref, gain_ref, gt_ref, gs_ref):
    step = pl.program_id(0)
    hat, rstd = normalise(x_ref[...].astype(F32))
    dh = a_ref[...].astype(F32) + b_ref[...].astype(F32)
    gt_ref[...] = (dx_ref[...] + norm_back(dh, hat, rstd, gain_ref[...])).astype(BF)
    sums = jnp.concatenate(
        [jnp.sum(dh * hat, axis=0, keepdims=True), jnp.sum(dh, axis=0, keepdims=True)], axis=0
    )

    @pl.when(step == 0)
    def _():
        gs_ref[...] = sums

    @pl.when(step > 0)
    def _():
        gs_ref[...] += sums


def last_call(a, b, x, dx, gain):
    rows, dim = x.shape
    row = pl.BlockSpec((rows // 2, dim), lambda i: (i, 0))
    return pl.pallas_call(
        last_kernel,
        grid=(2,),
        in_specs=[row, row, row, row, full(gain.shape)],
        out_specs=[row, full((2, dim))],
        out_shape=[
            jax.ShapeDtypeStruct((rows, dim), BF),
            jax.ShapeDtypeStruct((2, dim), F32),
        ],
        compiler_params=params("arbitrary"),
        cost_estimate=cost(3),
        name="last",
    )(a, b, hbm(x), hbm(dx), gain)


class Chain:
    def __init__(self, hops):
        self.hops, self.value, self.got, self.begun, self.done = hops, None, None, False, False
        self.move = None

    def request(self):
        try:
            return self.hops.send(self.got) if self.begun else next(self.hops)
        except StopIteration as stop:
            self.value, self.done = stop.value, True
            return None
        finally:
            self.begun = True


class Move:
    def __init__(self, bit, members, got):
        self.bit, self.members, self.got = bit, members, got

    def settle(self, got):
        start = 0
        for chain, a in self.members:
            chain.move = None
            if len(self.members) == 1:
                chain.got = got
            elif self.bit == "patch":
                chain.got = got[start : start + a.shape[0]]
                start += a.shape[0]
            else:
                n = a.size // 128
                chain.got = got[start : start + n].reshape(a.shape)
                start += n


class Stage:
    def __init__(self, links):
        self.links = links

    def start(self, *chains):
        wanted = {}
        for chain in chains:
            if chain.done or chain.move is not None:
                continue
            request = chain.request()
            if request is not None:
                wanted.setdefault(request[0], []).append((chain, request[1]))
        for bit, members in wanted.items():
            arrays = [a for _, a in members]
            if bit == "patch":
                sent = arrays[0] if len(arrays) == 1 else jnp.concatenate(arrays, axis=0)
                got = lax.all_to_all(sent, "patch", 1, 1, tiled=True)
            elif len(arrays) == 1:
                got = self.links.swap(arrays[0], bit)
            else:
                sent = jnp.concatenate([a.reshape(-1, 128) for a in arrays], axis=0)
                got = self.links.swap(sent, bit)
            move = Move(bit, members, got)
            for chain, _ in members:
                chain.move = move

    def join(self, values, *chains):
        moves = []
        for chain in chains:
            if chain.move is not None and chain.move not in moves:
                moves.append(chain.move)
        held, values = lax.optimization_barrier(([m.got for m in moves], values))
        for move, got in zip(moves, held):
            move.settle(got)
        return values


class Links:
    def __init__(self, batches, patches):
        self.batches, self.patches = batches, patches
        self.patch = lax.axis_index("patch")
        self.batch = lax.axis_index("batch")
        self.bits = {"c": [("p", 1)], "y": [("b", 1)], "x": [], "z": []}
        bit = 2
        while bit < patches:
            self.bits["x"].append(("p", bit))
            bit *= 2
        bit = 2
        while bit < batches:
            self.bits["z"].append(("b", bit))
            bit *= 2

    def swap(self, a, bit):
        axis, step = bit
        step = step if axis == "p" else step * self.patches
        n = self.batches * self.patches
        return lax.ppermute(a, AXES, [(i, i ^ step) for i in range(n)])

    def swap_patch(self, a, bit):
        return self.swap(a, ("p", bit))

    def mine(self, bit):
        axis, step = bit
        return ((self.patch if axis == "p" else self.batch) // step) & 1

    def expand(self, order):
        if not isinstance(order, str):
            return order
        bits = []
        for axis in order:
            one = self.bits[axis.lower()]
            bits += one if axis.islower() else one[::-1]
        return bits

    def hops(self, a, axes, order, back, trade, layout, first):
        if first is not None:
            got = yield first
            a = (a.astype(F32) + got.astype(F32)).astype(BF)
        names = list(self.expand(axes))
        blocks, rows, _ = a.shape
        a = a.reshape((blocks,) + (2,) * len(names) + (rows // 2 ** len(names), 128))
        layout = self.expand(layout)
        for bit in self.expand(order):
            at = names.index(bit) + 1
            names.pop(at - 1)
            got = yield bit, lax.dynamic_index_in_dim(a, 1 - self.mine(bit), at, keepdims=False)
            keep = lax.dynamic_index_in_dim(a, self.mine(bit), at, keepdims=False)
            a = (keep.astype(F32) + got.astype(F32)).astype(BF)
        if trade is not None and trade != "patch":
            bit = ("p", 1)
            size = a.shape[1:]
            pairs = a[:trade].reshape((trade // 2, 2) + size)
            got = yield bit, lax.dynamic_index_in_dim(pairs, 1 - self.mine(bit), 1, keepdims=False)
            own = lax.dynamic_index_in_dim(pairs, self.mine(bit), 1, keepdims=False)
            a = jnp.concatenate([self.join(own, got, bit, 0).reshape((trade,) + size), a[trade:]])
        if trade == "patch":
            a = a.reshape((blocks, self.patches) + a.shape[-2:])
            a = yield "patch", a
            a = a.reshape((blocks * self.patches,) + a.shape[-2:])
        have = []
        for bit in self.expand(back):
            got = yield bit, a
            at = 1 + sum(layout.index(other) < layout.index(bit) for other in have)
            have.append(bit)
            a = self.join(a, got, bit, at)
        return a.reshape(a.shape[0], -1, 128)

    def join(self, a, got, bit, at):
        return jnp.where(
            self.mine(bit) == 0, jnp.stack([a, got], axis=at), jnp.stack([got, a], axis=at)
        )

    def chain(self, a, axes, order, back, trade=None, layout="yz", first=None):
        return Chain(self.hops(a, axes, order, back, trade, layout, first))

    def apart(self, a):
        got = {0: a}
        bit = self.patches // 2
        while bit > 1:
            for j in sorted(got):
                got[j | bit] = self.swap_patch(got[j], bit)
            bit //= 2
        return got

    def items(self, a):
        got = self.apart(a)
        for j in sorted(got):
            got[j | 1] = self.swap_patch(got[j], 1)
        return got

    def deal(self, parts):
        return [parts[0]] + [self.swap_patch(parts[j], j) for j in range(1, self.patches)]


def assemble_kernel(count, order, valid, *refs):
    out = refs[count]
    pieces = [refs[n][b][:, :valid].astype(F32) for n, b in order]
    out[...] = jnp.concatenate(pieces, axis=1)


def assemble(parts, order, valid=128):
    rows = parts[0].shape[1]
    step = min(rows, 128)
    return pl.pallas_call(
        functools.partial(assemble_kernel, len(parts), order, valid),
        grid=(rows // step,),
        in_specs=[pl.BlockSpec((a.shape[0], step, 128), lambda i: (0, i, 0)) for a in parts],
        out_specs=pl.BlockSpec((step, len(order) * valid), lambda i: (i, 0)),
        out_shape=jax.ShapeDtypeStruct((rows, len(order) * valid), F32),
        compiler_params=params("arbitrary"),
        cost_estimate=cost(2),
        name="assemble",
    )(*parts)


def pieces_kernel(steps, a_ref, out):
    piece = pl.program_id(0) // steps
    blocks = a_ref.shape[0] // 2

    def put(n):
        for b in range(blocks):
            out[:, b * 128 : (b + 1) * 128] = a_ref[2 * b + n].astype(F32)

    for n in range(2):
        pl.when(piece == n)(functools.partial(put, n))


def pieces_call(a):
    blocks, rows, _ = a.shape
    step = min(rows, 128)
    steps = rows // step
    return pl.pallas_call(
        functools.partial(pieces_kernel, steps),
        grid=(2 * steps,),
        in_specs=[pl.BlockSpec((blocks, step, 128), lambda i: (0, i % steps, 0))],
        out_specs=pl.BlockSpec((step, blocks * 64), lambda i: (i, 0)),
        out_shape=jax.ShapeDtypeStruct((2 * rows, blocks * 64), F32),
        compiler_params=params("arbitrary"),
        cost_estimate=cost(4),
        name="pieces",
    )(a)


def tables(code, times):
    head = 64
    half = head // 6
    band = 2 * half
    dims = jnp.arange(head)
    freq = jnp.power(THETA, -2.0 * (dims % half).astype(F32) / band)
    places = jnp.stack([times, (code // GRID).astype(F32), (code % GRID).astype(F32)], axis=-1)
    which = jnp.minimum(dims // band, 2)
    pick = jnp.where(
        which == 0, places[..., 0:1], jnp.where(which == 1, places[..., 1:2], places[..., 2:3])
    )
    angle = pick * freq
    turned = dims < 3 * band
    cos = jnp.where(turned, jnp.cos(angle), 1.0)
    sin = jnp.where(turned, jnp.sin(angle) * jnp.where(dims % band < half, -1.0, 1.0), 0.0)
    return jnp.concatenate([cos, cos, sin, sin], axis=-1)


def per_device(
    batches, patches, tokens, cotangent, episode_frames, kinds, patch_pos,
    ln1_gain, ln1_shift, w_qkv, w_out, ln2_gain, ln2_shift, w_up, w_down,
):
    tokens = tokens[0]
    frames, width, dim = tokens.shape
    rows = frames * width
    local = dim // patches
    links = Links(batches, patches)
    me = links.patch
    core = me & 1
    gain1, shift1, gain2, shift2 = (
        a.astype(F32).reshape(1, dim) for a in (ln1_gain, ln1_shift, ln2_gain, ln2_shift)
    )
    dy = cotangent.reshape(rows, dim)

    code = jnp.where(kinds[0] == 0, patch_pos[0], 0)
    codes = links.items(code)
    mate = links.swap_patch(tokens, 1)
    dy_mate = links.swap_patch(dy, 1)
    apart = links.apart(tokens)
    ends = jnp.cumsum(episode_frames[0])
    frame_ids = jnp.arange(frames, dtype=jnp.int32)
    starts = jnp.max(
        jnp.where(ends[None, :] <= frame_ids[:, None], ends[None, :], 0), axis=1
    )
    firsts = [links.mine(bits[0])[None] for bits in (links.bits["y"], links.bits["z"])]
    info = jnp.concatenate([me[None], starts, *firsts]).astype(jnp.int32)
    pad = max(128, local)
    pairs = pad // 128
    valid = min(128, local)
    if valid == 128:
        w_local = columns_call(info, w_qkv, pairs)
    else:
        columns = []
        for n in range(3):
            at = n * dim + me * local
            columns.append(lax.dynamic_slice(w_qkv, (jnp.int32(0), at), (dim, valid)))
            columns.append(jnp.zeros((dim, 128 - valid), BF))
        w_local = jnp.concatenate(columns, axis=1)

    members = [[0, 1], list(range(2, patches))]
    css = []
    for group in members:
        place = jnp.concatenate([codes[j] for j in group], axis=1)
        times = jnp.broadcast_to(frame_ids.astype(F32)[:, None], place.shape)
        css.append(tables(place, times))
    near = qkv_call([tokens, mate], css[0], w_local, gain1, shift1)
    dg = pre_call(info, dy, dy_mate, w_down, patches)
    near, dg, apart, css = lax.optimization_barrier((near, dg, apart, css))
    far_items = []
    for j in range(2, patches, 2):
        far_items += [apart[j], links.swap_patch(apart[j], 1)]
    far = qkv_call(far_items, css[1], w_local, gain1, shift1)
    hs, qkvs = [near[0], far[0]], [near[1], far[1]]

    *o_send, o_full, lse = attend_call(info, qkvs, patches)
    o_in = links.deal([a[..., :local] for a in o_send])
    x1, h2, o_own = project_call(info, o_in, tokens, w_out, gain2, shift2)
    h2_mate = links.swap_patch(h2, 1)
    o_mate = links.swap_patch(o_own, 1)
    stage = Stage(links)
    g, du, keep0, send0, keep1, send1, dh_own, dh_mate = ffn_call(
        info, h2, h2_mate, dy, dy_mate, dg, w_up, patches
    )
    inner, outer = links.bits["z"][:1], links.bits["z"][1:]
    ys, xs = links.bits["y"], links.bits["x"]

    def two_pieces(a):
        return a.reshape(a.shape[0] * 2, a.shape[1] // 2, 128)

    def step(held, *chains):
        held = stage.join(held, *chains)
        for chain in chains:
            stage.start(chain)
        return held

    def finish(held, *chains):
        while not all(c.done for c in chains):
            held = step(held, *chains)
        return held

    d1 = links.chain(two_pieces(keep0), xs[::-1] + inner + outer, inner, "", first=(ys[0], two_pieces(send0)))
    d2 = links.chain(two_pieces(keep1), xs[::-1] + ys + outer, ys, "", first=(inner[0], two_pieces(send1)))
    stage.start(d1)
    stage.start(d2)
    dh_recv = links.swap_patch(dh_mate, 1)
    dx1, da, sums2, *d_o = mid_call(
        info, dh_own, dh_recv, x1, dy, w_out, gain2, frames, patches
    )
    da_mate = links.swap_patch(da, 1)
    do_in = links.deal(d_o)
    sides = (o_own, o_mate, da, da_mate)
    dw1 = up_call(info, h2, h2_mate, du, *sides, patches, 0)
    dw2 = up_call(info, h2, h2_mate, du, *sides, patches, 1)
    out_own, out_mate = down_call(info, x1, g, w_down, patches)
    do_in, dw1, dw2, out_own, out_mate = step((do_in, dw1, dw2, out_own, out_mate), d1, d2)
    out_recv = links.swap_patch(out_mate, 1)
    u1 = links.chain(dw1, "Xcyz", xs + inner + ys, "")
    u2 = links.chain(dw2, "Xcyz", ys + xs + inner, "")
    stage.start(u1)
    if pad > local:
        do_in = [jnp.pad(a, ((0, 0), (0, 0), (0, pad - local))) for a in do_in]
    dqkv = attend_back_call(info, qkvs, css, do_in, o_full, lse, patches, 0)
    dwq = [dwq_call(hs, dqkv)]
    dqkv, dwq, do_in = step((dqkv, dwq, do_in), d1, d2)
    dqkv = finish(dqkv, d1, d2)
    dqkvs = [dqkv]
    d = links.chain(
        jnp.concatenate([d1.value, d2.value], axis=0),
        xs[::-1] + outer,
        outer + xs,
        outer[::-1] + inner + ys,
    )
    stage.start(d)
    stage.start(u2)
    for pair in range(1, pairs):
        dqkvs.append(attend_back_call(info, qkvs, css, do_in, o_full, lse, patches, pair))
    for one in dqkvs[1:]:
        dwq.append(dwq_call(hs, one))
    even, odd = dh_call(dqkvs, w_local, patches)
    odd, even, dwq = stage.join((odd, even, dwq), u1, d, u2)
    q = links.chain(jnp.concatenate(dwq, axis=0), "Xcyz", "yz", "zy", "patch")
    for chain in (q, u1, d, u2):
        stage.start(chain)
    odd = links.swap_patch(odd, 1)
    odd, even, sums2 = step((odd, even, sums2), u1)
    slots = (even.astype(F32) + odd.astype(F32)).astype(BF)
    bit = patches // 2
    while bit > 2:
        n = slots.shape[0] // 2
        slots = (slots[:n].astype(F32) + links.swap_patch(slots[n:], bit).astype(F32)).astype(BF)
        bit //= 2
    got = links.swap_patch(slots[1], 2)
    sums2 = step(sums2, q)
    sums2 = step(sums2, u2, d)
    sums2 = step(sums2, u1, u2)
    sums2 = finish(sums2, u1, u2)
    w = jnp.concatenate([u1.value, u2.value], axis=0)
    w = w.reshape(2 * w.shape[0], -1, 128)
    w = links.chain(w, outer, outer, outer[::-1], w.shape[0])
    stage.start(w)
    sums2 = step(sums2, q)
    sums2 = step(sums2, d)
    sums2 = step(sums2, w)
    slots, got, sums2 = step((slots, got, sums2), q)
    sums2 = step(sums2, w)
    sums2 = step(sums2, d)
    grad_tokens, sums1 = last_call(
        slots[0].reshape(rows, dim), got.reshape(rows, dim), tokens.reshape(rows, dim), dx1, gain1
    )
    sums = jnp.concatenate([sums1, sums2], axis=0)
    sums = step(sums, q)
    sums = step(sums, w)
    sums = finish(sums, w)
    half = w.value.shape[0] // 2
    wa = links.chain(w.value[:half], [], [], ys + inner)
    wb = links.chain(w.value[half:], [], [], inner + ys)
    stage.start(wa)
    stage.start(wb)
    sums, out_own, out_recv = step((sums, out_own, out_recv), q)
    out = (out_own + out_recv.astype(F32)).astype(BF)
    sums = sums.reshape(4, patches, local).transpose(1, 0, 2)
    sums = jnp.broadcast_to(sums[None], (batches,) + sums.shape)
    sums = lax.all_to_all(sums.reshape((-1,) + sums.shape[2:]), AXES, 0, 0, tiled=True)
    held = step(grad_tokens, wa, wb)
    held = step(held, q)
    held = step(held, d)
    held, sums = step((held, sums), wa, wb)
    grad_tokens = step(held, q)
    sums = jnp.sum(sums, axis=0)
    grad_tokens = finish(grad_tokens, wa, wb)
    grad_tokens = finish(grad_tokens, q)
    grad_tokens = finish(grad_tokens, d)
    down = pieces_call(d.value)

    nx = patches // 2
    each = dw1.shape[0]
    per = (each - dim // 512) // nx
    ups, wos = [], []
    for owner in range(2):
        for n in range(2):
            wos += [(owner, n * each + nx * per + t) for t in range(dim // 512)]
    for i in range(nx):
        for owner in range(2):
            for n in range(2):
                ups += [(owner, n * each + i * per + t) for t in range(per)]
    up = assemble([wa.value, wb.value], ups)
    grad_wo = assemble([wa.value, wb.value], wos)
    order = []
    for n in range(3):
        for p in range(patches):
            order += [(0, (pair * 3 + n) * patches + p) for pair in range(pairs)]
    qkv = assemble([q.value], order, valid)

    return (
        out.reshape(1, frames, width, dim),
        grad_tokens.reshape(1, frames, width, dim),
        sums[0],
        sums[1],
        qkv,
        grad_wo,
        sums[2],
        sums[3],
        up,
        down,
    )


def solution(mesh):
    placed = (
        P("batch", None, "patch", None),
        P("batch", None, "patch", None),
        P("batch", None),
        P("batch", None, "patch"),
        P("batch", None, "patch"),
    ) + (P(),) * 8
    return jax.shard_map(
        functools.partial(per_device, mesh.shape["batch"], mesh.shape["patch"]),
        mesh=mesh,
        in_specs=placed,
        out_specs=(
            P("batch", None, "patch", None),
            P("batch", None, "patch", None),
            P("patch"),
            P("patch"),
            P("patch", None),
            P("patch", None),
            P("patch"),
            P("patch"),
            P("patch", None),
            P("patch", None),
        ),
        check_vma=False,
    )
```

```python
import functools
import math

import jax
import jax.numpy as jnp
from jax import lax
from jax.experimental import pallas as pl
from jax.experimental.pallas import tpu as pltpu
from jax.sharding import PartitionSpec as P

GRID = 16
EPS = 1e-06
THETA = 10000.0
MASKED = -1e30
LIMIT = 40 * 1024 * 1024
BF = jnp.bfloat16
F32 = jnp.float32
AXES = ("batch", "patch")


def nn(a, b):
    return lax.dot_general(a, b, (((1,), (0,)), ((), ())), preferred_element_type=F32)


def nt(a, b):
    return lax.dot_general(a, b, (((1,), (1,)), ((), ())), preferred_element_type=F32)


def tn(a, b):
    return lax.dot_general(a, b, (((0,), (0,)), ((), ())), preferred_element_type=F32)


def params(*semantics):
    return pltpu.CompilerParams(
        dimension_semantics=semantics, vmem_limit_bytes=LIMIT
    )


def cost(micros):
    return pl.CostEstimate(flops=int(micros * 2.875e+08), bytes_accessed=1, transcendentals=0)


def full(shape, memory=None):
    zeros = (0,) * len(shape)
    return pl.BlockSpec(shape, lambda *_: zeros)


def blocked(ref, value):
    for n in range(ref.shape[0]):
        ref[n] = value[:, n * 128 : (n + 1) * 128].astype(BF)


def hbm(a):
    return pltpu.with_memory_space_constraint(a, pltpu.HBM)


def smem():
    return pl.BlockSpec(memory_space=pltpu.SMEM)


def normalise(x):
    mean = jnp.mean(x, axis=-1, keepdims=True)
    centred = x - mean
    spread = jnp.mean(centred * centred, axis=-1, keepdims=True)
    rstd = lax.rsqrt(spread + EPS)
    return centred * rstd, rstd


def norm_back(d_h, hat, rstd, gain):
    d_hat = d_h * gain
    first = jnp.mean(d_hat, axis=-1, keepdims=True)
    second = jnp.mean(d_hat * hat, axis=-1, keepdims=True)
    return rstd * (d_hat - first - hat * second)


def partner(value):
    head = 64
    half = head // 6
    width = value.shape[1]
    ahead = jnp.concatenate([value[:, half:], value[:, :half]], axis=1)
    behind = jnp.concatenate([value[:, width - half :], value[:, : width - half]], axis=1)
    lane = lax.broadcasted_iota(jnp.int32, value.shape, 1) % head
    return jnp.where(lane % (2 * half) < half, ahead, behind)


def columns_kernel(info_ref, w_ref, out_ref):
    out_ref[...] = w_ref[...]


def columns_call(info, w_qkv, pairs):
    dim = w_qkv.shape[0]
    blocks = dim // 128

    def at(i, info):
        return (0, (i % 3) * blocks + info[0] * pairs + i // 3)

    return pl.pallas_call(
        columns_kernel,
        grid_spec=pltpu.PrefetchScalarGridSpec(
            num_scalar_prefetch=1,
            grid=(3 * pairs,),
            in_specs=[pl.BlockSpec((dim, 128), at)],
            out_specs=pl.BlockSpec((dim, 128), lambda i, info: (0, i)),
        ),
        out_shape=jax.ShapeDtypeStruct((dim, 384 * pairs), BF),
        compiler_params=params("arbitrary"),
        cost_estimate=cost(2),
        name="columns",
    )(info, hbm(w_qkv))


def qkv_kernel(count, local, *refs):
    tok = refs[:count]
    cs_ref, w_ref, gain_ref, shift_ref = refs[count : count + 4]
    h_ref, qkv_ref = refs[count + 4 :]
    x = jnp.concatenate([t[...] for t in tok], axis=1)
    fb, rows, dim = x.shape
    x = x.reshape(fb * rows, dim).astype(F32)
    hat, _ = normalise(x)
    h = (hat * gain_ref[...] + shift_ref[...]).astype(BF)
    h_ref[...] = h.reshape(fb, rows, dim)
    y = nn(h, w_ref[...])
    cs = cs_ref[...].reshape(fb * rows, 256)
    cos = cs[:, :128]
    sin = cs[:, 128:]
    for at in range(0, 3 * local, 384):
        q = y[:, at : at + 128]
        k = y[:, at + 128 : at + 256]
        q = (q * cos + partner(q) * sin).astype(BF) * BF(0.125)
        k = (k * cos + partner(k) * sin).astype(BF)
        v = y[:, at + 256 : at + 384].astype(BF)
        qkv_ref[:, :, at : at + 128] = q.reshape(fb, rows, 128)
        qkv_ref[:, :, at + 128 : at + 256] = k.reshape(fb, rows, 128)
        qkv_ref[:, :, at + 256 : at + 384] = v.reshape(fb, rows, 128)


def qkv_call(items, cs, w_local, gain, shift):
    count = len(items)
    frames, width, dim = items[0].shape
    local = w_local.shape[1] // 3
    rows = count * width
    fb = max(1, min(frames, 512 // rows))
    while frames % fb:
        fb -= 1
    shapes = [
        pltpu.HBM((frames, rows, dim), BF),
        pltpu.HBM((frames, rows, 3 * local), BF),
    ]
    return pl.pallas_call(
        functools.partial(qkv_kernel, count, local),
        grid=(frames // fb,),
        in_specs=[pl.BlockSpec((fb, width, dim), lambda i: (i, 0, 0))] * count
        + [
            pl.BlockSpec((fb, rows, 256), lambda i: (i, 0, 0)),
            full(w_local.shape),
            full(gain.shape),
            full(shift.shape),
        ],
        out_specs=[
            pl.BlockSpec((fb, rows, dim), lambda i: (i, 0, 0)),
            pl.BlockSpec((fb, rows, 3 * local), lambda i: (i, 0, 0)),
        ],
        out_shape=shapes,
        compiler_params=params("arbitrary"),
        cost_estimate=cost(5.5),
        name="qkv",
    )(*items, cs, w_local, gain, shift)


def lane_halves(shape):
    lane = lax.broadcasted_iota(jnp.int32, shape, 1)
    return lane < 64


def attend_kernel(groups, local, patches, most, info_ref, *refs):
    ins = refs[:groups]
    o_refs = refs[groups : groups + patches]
    of_ref, lse_ref = refs[groups + patches :]
    f = pl.program_id(0)
    begin = info_ref[1 + f]
    rows = sum(r.shape[1] for r in ins)
    low = lane_halves((rows, 128))
    one = jnp.ones((rows, 128), BF)
    zero = jnp.zeros((rows, 128), BF)
    lane = lax.broadcasted_iota(jnp.int32, (rows, 128), 1)

    def part_of(g, pair, n):
        at = pair * 384 + n * 128
        return jnp.concatenate([r[g, :, at : at + 128] for r in ins], axis=0)

    def finish(pair, tops, accs, lses):
        num = jnp.where(low, accs[0], accs[1])
        den = pltpu.roll(jnp.where(low, accs[1], accs[0]), 64, 1)
        of_ref[0, :, pair * 128 : (pair + 1) * 128] = num / den
        logs = jnp.log(jnp.where(low, accs[1], accs[0]))
        lses = jnp.where(lane == 2 * pair + 64, tops[0] + logs, lses)
        return jnp.where(lane == 2 * pair + 1, tops[1] + logs, lses)

    def store(lses):
        even = lane % 2 == 0
        lses = jnp.where(even, pltpu.roll(lses, 64, 1), lses)
        lse_ref[0] = lses.T[:8]

    def whole(count):
        lses = jnp.zeros((rows, 128), F32)
        for pair in range(local // 128):
            q = part_of(f, pair, 0)
            tops, accs = [], []
            for h in range(2):
                qm = jnp.where(low == (h == 0), q, zero)
                scores = [nt(qm, part_of(begin + n, pair, 1)) for n in range(count)]
                top = scores[0]
                for s in scores[1:]:
                    top = jnp.maximum(top, s)
                top = jnp.max(top, axis=1, keepdims=True)
                acc = None
                for n, s in enumerate(scores):
                    v = jnp.where(low == (h == 0), part_of(begin + n, pair, 2), one)
                    part = nn(jnp.exp(s - top).astype(BF), v)
                    acc = part if acc is None else acc + part
                tops.append(top)
                accs.append(acc)
            lses = finish(pair, tops, accs, lses)
        store(lses)

    if most <= 4:
        for count in range(1, most + 1):
            pl.when(f + 1 - begin == count)(functools.partial(whole, count))
    else:
        lses = jnp.zeros((rows, 128), F32)
        for pair in range(local // 128):
            q = part_of(f, pair, 0)

            def body(g, state, pair=pair, q=q):
                new = []
                for h in range(2):
                    top, acc = state[2 * h : 2 * h + 2]
                    qm = jnp.where(low == (h == 0), q, zero)
                    s = nt(qm, part_of(g, pair, 1))
                    new_top = jnp.maximum(top, jnp.max(s, axis=1, keepdims=True))
                    v = jnp.where(low == (h == 0), part_of(g, pair, 2), one)
                    p = jnp.exp(s - new_top).astype(BF)
                    new += [new_top, acc * jnp.exp(top - new_top) + nn(p, v)]
                return tuple(new)

            blank = (jnp.full((rows, 1), MASKED, F32), jnp.zeros((rows, 128), F32))
            state = lax.fori_loop(begin, f + 1, body, blank + blank)
            lses = finish(pair, state[0::2], state[1::2], lses)
        store(lses)

    o = of_ref[0].astype(BF)
    width = rows // patches
    for j in range(patches):
        o_refs[j][0] = o[j * width : (j + 1) * width]


def attend_call(info, qkv, patches):
    groups = len(qkv)
    frames = qkv[0].shape[0]
    local = qkv[0].shape[2] // 3
    rows = sum(a.shape[1] for a in qkv)
    width = rows // patches
    shapes = [jax.ShapeDtypeStruct((frames, width, local), BF)] * patches
    sizes = [(frames, width, local)] * patches + [(frames, rows, local), (frames, 8, rows)]
    shapes += [pltpu.HBM((frames, rows, local), F32), pltpu.HBM((frames, 8, rows), F32)]
    return pl.pallas_call(
        functools.partial(attend_kernel, groups, local, patches, frames // 2),
        grid=(frames,),
        in_specs=[smem()] + [full(a.shape) for a in qkv],
        out_specs=[pl.BlockSpec((1,) + s[1:], lambda i: (i, 0, 0)) for s in sizes],
        out_shape=shapes,
        compiler_params=params("arbitrary"),
        cost_estimate=cost(12.5),
        name="attend",
    )(info, *[hbm(a) for a in qkv])


def attend_back_kernel(groups, pair, patches, info_ref, *refs):
    ins = refs[:groups]
    css = refs[groups : 2 * groups]
    do_refs = refs[2 * groups : 2 * groups + patches]
    refs = refs[2 * groups + patches :]
    of_ref, lse_ref = refs[:2]
    outs = refs[2 : groups + 2]
    dk_ref, dv_ref, dq_ref, kt_ref = refs[groups + 2 :]
    f = pl.program_id(0)
    frames = pl.num_programs(0)
    begin = info_ref[1 + f]

    def part_of(g, n):
        return jnp.concatenate([r[g, :, n * 128 : (n + 1) * 128] for r in ins], axis=0)

    q = part_of(f, 0)
    d_o = jnp.concatenate([r[0] for r in do_refs], axis=0)
    rows = q.shape[0]
    low = lane_halves((rows, 128))
    zero = jnp.zeros((rows, 128), BF)
    turned = (d_o.astype(F32) * of_ref[0]).T
    delta = [jnp.sum(turned[h * 64 : (h + 1) * 64], axis=0, keepdims=True) for h in range(2)]
    lse = lse_ref[0, 2 * pair : 2 * pair + 2]
    dk_ref[f] = jnp.zeros((rows, 128), F32)
    dv_ref[f] = jnp.zeros((rows, 128), F32)
    dq_ref[...] = jnp.zeros((128, rows), F32)
    kt_ref[f] = part_of(f, 1).T
    qm = [jnp.where(low == (h == 0), q, zero) for h in range(2)]
    dom = [jnp.where(low == (h == 0), d_o, zero) for h in range(2)]

    @pl.loop(begin, f + 1)
    def _(g):
        k = part_of(g, 1)
        v = part_of(g, 2)
        scores = [nt(k, qm[h]) for h in range(2)]
        dps = [nt(v, dom[h]) for h in range(2)]
        dk = dv = None
        for h in range(2):
            p = jnp.exp(scores[h] - lse[h : h + 1])
            ds = (p * (dps[h] - delta[h])).astype(BF)
            dq_ref[h * 64 : (h + 1) * 64] += nn(kt_ref[g, h * 64 : (h + 1) * 64], ds)
            part_k = nn(ds, qm[h])
            part_v = nn(p.astype(BF), dom[h])
            dk = part_k if dk is None else dk + part_k
            dv = part_v if dv is None else dv + part_v
        dk_ref[g] += dk
        dv_ref[g] += dv

    def turn_back(t, value):
        cs = jnp.concatenate([r[t] for r in css], axis=0)
        return (value * cs[:, :128] - partner(value) * cs[:, 128:]).astype(BF)

    def put(t, n, value):
        start = 0
        for out in outs:
            count = out.shape[1]
            out[t, :, n * 128 : (n + 1) * 128] = value[start : start + count]
            start += count

    put(f, 0, turn_back(f, dq_ref[...].T * 0.125))

    @pl.when(f == frames - 1)
    def _():
        @pl.loop(0, frames)
        def _(t):
            put(t, 1, turn_back(t, dk_ref[t]))
            put(t, 2, dv_ref[t].astype(BF))


def attend_back_call(info, qkv, cs, d_o, o_full, lse, patches, pair):
    groups = len(qkv)
    frames = qkv[0].shape[0]
    rows = sum(a.shape[1] for a in qkv)
    width = rows // patches
    shapes = [jax.ShapeDtypeStruct((frames, a.shape[1], 384), BF) for a in qkv]
    return pl.pallas_call(
        functools.partial(attend_back_kernel, groups, pair, patches),
        grid=(frames,),
        in_specs=[smem()]
        + [pl.BlockSpec(a.shape[:2] + (384,), lambda i: (0, 0, pair)) for a in qkv]
        + [full(a.shape) for a in cs]
        + [pl.BlockSpec((1, width, 128), lambda i: (i, 0, pair))] * patches
        + [
            pl.BlockSpec((1, rows, 128), lambda i: (i, 0, pair)),
            pl.BlockSpec((1, 8, rows), lambda i: (i, 0, 0)),
        ],
        out_specs=[full(s.shape) for s in shapes],
        out_shape=shapes,
        scratch_shapes=[
            pltpu.VMEM((frames, rows, 128), F32),
            pltpu.VMEM((frames, rows, 128), F32),
            pltpu.VMEM((128, rows), F32),
            pltpu.VMEM((frames, 128, rows), BF),
        ],
        compiler_params=params("arbitrary"),
        cost_estimate=cost(15),
        name="attend_back",
    )(info, *[hbm(a) for a in (*qkv, *cs)], *d_o, hbm(o_full), hbm(lse))


def heads_rows(info_ref, j, local):
    return pl.ds(pl.multiple_of((info_ref[0] ^ j) * local, local), local)


def project_kernel(patches, info_ref, *refs):
    o_refs = refs[:patches]
    x_ref, w_ref, gain_ref, shift_ref, x1_ref, h_ref, o_ref, kept_ref = refs[patches:]
    fb, width, local = o_refs[0].shape
    rows = fb * width
    for j, ref in enumerate(o_refs):
        kept_ref[j] = ref[...].reshape(rows, local)
    o = jnp.concatenate([kept_ref[info_ref[0] ^ p] for p in range(patches)], axis=1)
    o_ref[...] = o
    acc = x_ref[...].astype(F32).reshape(rows, -1) + nn(o, w_ref[...])
    x1_ref[...] = acc
    hat, _ = normalise(acc)
    h_ref[...] = (hat * gain_ref[...] + shift_ref[...]).astype(BF)


def project_call(info, o_in, tokens, w_out, gain, shift):
    patches = len(o_in)
    frames, width, local = o_in[0].shape
    dim = w_out.shape[0]
    fb = frames
    rows = frames * width
    return pl.pallas_call(
        functools.partial(project_kernel, patches),
        grid=(1,),
        in_specs=[smem()]
        + [pl.BlockSpec((fb, width, local), lambda i: (i, 0, 0))] * patches
        + [
            pl.BlockSpec((fb, width, dim), lambda i: (i, 0, 0)),
            full(w_out.shape),
            full(gain.shape),
            full(shift.shape),
        ],
        out_specs=[
            pl.BlockSpec((rows, dim), lambda i: (i, 0)),
            pl.BlockSpec((rows, dim), lambda i: (i, 0)),
            pl.BlockSpec((rows, dim), lambda i: (i, 0)),
        ],
        out_shape=[
            pltpu.HBM((rows, dim), F32),
            jax.ShapeDtypeStruct((rows, dim), BF),
            jax.ShapeDtypeStruct((rows, dim), BF),
        ],
        scratch_shapes=[pltpu.VMEM((patches, rows, local), BF)],
        compiler_params=params("arbitrary"),
        cost_estimate=cost(3.7),
        name="project",
    )(info, *o_in, tokens, w_out, gain, shift)


def tile_at(piece, steps):
    return lambda i, info: ((i % steps) * 2 + (info[0] & 1)) * 2 + (
        i // steps if piece is None else piece
    )


def pre_kernel(info_ref, dy_own, dy_mate, down_ref, dg_ref):
    half = dy_own.shape[0]
    dg_ref[:half] = nt(dy_own[...], down_ref[...]).astype(BF)
    dg_ref[half:] = nt(dy_mate[...], down_ref[...]).astype(BF)


def pre_call(info, dy_own, dy_mate, w_down, patches):
    half, dim = dy_own.shape
    hidden = w_down.shape[0]
    tile, steps = hidden // patches // 2, patches // 2
    at = tile_at(None, steps)
    return pl.pallas_call(
        pre_kernel,
        grid_spec=pltpu.PrefetchScalarGridSpec(
            num_scalar_prefetch=1,
            grid=(2 * steps,),
            in_specs=[full((half, dim))] * 2
            + [pl.BlockSpec((tile, dim), lambda i, info: (at(i, info), 0))],
            out_specs=pl.BlockSpec((2 * half, tile), lambda i, info: (0, i)),
        ),
        out_shape=pltpu.HBM((2 * half, hidden // 2), BF),
        compiler_params=params("arbitrary"),
        cost_estimate=cost(8.5),
        name="pre",
    )(info, dy_own, dy_mate, w_down)


def ffn_kernel(
    info_ref, h_own, h_mate, dy_own, dy_mate, dg_ref, up_ref,
    g_ref, du_ref, keep0, send0, keep1, send1, dh_own, dh_mate, acc_ref,
):
    step = pl.program_id(0)
    half = h_own.shape[0]

    @pl.when(step == 0)
    def _():
        acc_ref[...] = jnp.zeros(acc_ref.shape, F32)

    w_up = up_ref[...]
    chunk = half // 2
    for n in range(4):
        h_ref = (h_own, h_mate)[n // 2]
        here = slice((n % 2) * chunk, (n % 2 + 1) * chunk)
        rows = slice(n * chunk, (n + 1) * chunk)
        u = nn(h_ref[here], w_up)
        cdf = 0.5 + 0.5 * lax.erf(u * math.sqrt(0.5))
        pdf = jnp.exp(u * u * -0.5) * (1.0 / math.sqrt(2.0 * math.pi))
        g = (u * cdf).astype(BF)
        du = (dg_ref[rows].astype(F32) * (cdf + u * pdf)).astype(BF)
        g_ref[rows] = g
        du_ref[rows] = du
        acc_ref[rows] += nt(du, w_up)
    total = tn(g_ref[:half], dy_own[...]) + tn(g_ref[half:], dy_mate[...])
    middle = total.shape[1] // 2
    part = total.shape[0] // 2
    for n, (keep_ref, send_ref) in enumerate(((keep0, send0), (keep1, send1))):
        value = total[:, n * middle : (n + 1) * middle]
        if n == 0:
            low, high = value[:part], value[part:]
        else:
            some = part // 2
            low = jnp.concatenate([value[:some], value[part : part + some]], axis=0)
            high = jnp.concatenate([value[some:part], value[part + some :]], axis=0)
        first = info_ref[info_ref.shape[0] - 2 + n] == 0
        blocked(keep_ref, jnp.where(first, low, high))
        blocked(send_ref, jnp.where(first, high, low))

    @pl.when(step == pl.num_programs(0) - 1)
    def _():
        dh_own[...] = acc_ref[:half]
        dh_mate[...] = acc_ref[half:].astype(BF)


def ffn_call(info, h_own, h_mate, dy_own, dy_mate, dg, w_up, patches):
    half, dim = h_own.shape
    hidden = w_up.shape[1]
    tile, steps = hidden // patches // 2, patches // 2
    at = tile_at(None, steps)
    column = pl.BlockSpec((2 * half, tile), lambda i, info: (0, i))
    return pl.pallas_call(
        ffn_kernel,
        grid_spec=pltpu.PrefetchScalarGridSpec(
            num_scalar_prefetch=1,
            grid=(2 * steps,),
            in_specs=[full((half, dim))] * 4
            + [column, pl.BlockSpec((dim, tile), lambda i, info: (0, at(i, info)))],
            out_specs=[
                column,
                column,
            ]
            + [pl.BlockSpec((dim // 256, tile // 2, 128), lambda i, info: (0, i, 0))] * 4
            + [
                full((half, dim)),
                full((half, dim)),
            ],
            scratch_shapes=[pltpu.VMEM((2 * half, dim), F32)],
        ),
        out_shape=[
            pltpu.HBM((2 * half, hidden // 2), BF),
            pltpu.HBM((2 * half, hidden // 2), BF),
        ]
        + [pltpu.HBM((dim // 256, hidden // 4, 128), BF)] * 4
        + [
            pltpu.HBM((half, dim), F32),
            jax.ShapeDtypeStruct((half, dim), BF),
        ],
        compiler_params=params("arbitrary"),
        cost_estimate=cost(25),
        name="ffn",
    )(info, h_own, h_mate, hbm(dy_own), hbm(dy_mate), hbm(dg), hbm(w_up))


def up_kernel(steps, tile, h_own, h_mate, du_ref, o_own, o_mate, da_own, da_mate, dw_ref):
    half = h_own.shape[0]
    step = pl.program_id(0)
    count = tile // 128

    def put(at, value):
        for n in range(value.shape[1] // 128):
            dw_ref[at + n] = value[:, n * 128 : (n + 1) * 128].astype(BF)

    @pl.when(step < steps)
    def _():
        value = tn(h_own[...], du_ref[:half]) + tn(h_mate[...], du_ref[half:])
        put(step * count, value)

    @pl.when(step == steps)
    def _():
        put(steps * count, tn(o_own[...], da_own[...]) + tn(o_mate[...], da_mate[...]))


def up_call(info, h_own, h_mate, du, o_own, o_mate, da_own, da_mate, patches, piece):
    half, dim = h_own.shape
    columns = du.shape[1] // 2
    steps = patches // 2
    tile = columns // steps
    shape = (columns // 128 + dim // 512, dim, 128)
    quarter = pl.BlockSpec((half, dim // 4), lambda i, info: (0, (info[0] & 1) * 2 + piece))

    def kernel(info_ref, *refs):
        up_kernel(steps, tile, *refs)

    return pl.pallas_call(
        kernel,
        grid_spec=pltpu.PrefetchScalarGridSpec(
            num_scalar_prefetch=1,
            grid=(steps + 1,),
            in_specs=[full((half, dim))] * 2
            + [
                pl.BlockSpec(
                    (2 * half, tile),
                    lambda i, info: (0, piece * steps + jnp.minimum(i, steps - 1)),
                )
            ]
            + [full((half, dim))] * 2
            + [quarter] * 2,
            out_specs=full(shape),
        ),
        out_shape=jax.ShapeDtypeStruct(shape, BF),
        compiler_params=params("arbitrary"),
        cost_estimate=cost(6),
        name="up",
    )(info, hbm(h_own), hbm(h_mate), hbm(du), hbm(o_own), hbm(o_mate), hbm(da_own), hbm(da_mate))


def down_kernel(info_ref, x1_ref, g0_ref, g1_ref, down0_ref, down1_ref, own_ref, mate_ref, acc_ref):
    step = pl.program_id(0)
    half = x1_ref.shape[0]

    @pl.when(step == 0)
    def _():
        acc_ref[:half] = x1_ref[...]
        acc_ref[half:] = jnp.zeros_like(x1_ref)

    for n in range(2):
        rows = slice(n * half, (n + 1) * half)
        acc_ref[rows] += nn(g0_ref[rows], down0_ref[...]) + nn(g1_ref[rows], down1_ref[...])

    @pl.when(step == pl.num_programs(0) - 1)
    def _():
        own_ref[...] = acc_ref[:half]
        mate_ref[...] = acc_ref[half:].astype(BF)


def down_call(info, x1, g, w_down, patches):
    half, dim = x1.shape
    hidden = w_down.shape[0]
    tile, steps = hidden // patches // 2, patches // 2
    first, second = tile_at(0, steps), tile_at(1, steps)
    return pl.pallas_call(
        down_kernel,
        grid_spec=pltpu.PrefetchScalarGridSpec(
            num_scalar_prefetch=1,
            grid=(steps,),
            in_specs=[
                full((half, dim)),
                pl.BlockSpec((2 * half, tile), lambda i, info: (0, i)),
                pl.BlockSpec((2 * half, tile), lambda i, info: (0, steps + i)),
                pl.BlockSpec((tile, dim), lambda i, info: (first(i, info), 0)),
                pl.BlockSpec((tile, dim), lambda i, info: (second(i, info), 0)),
            ],
            out_specs=[full((half, dim)), full((half, dim))],
            scratch_shapes=[pltpu.VMEM((2 * half, dim), F32)],
        ),
        out_shape=[
            pltpu.HBM((half, dim), F32),
            pltpu.HBM((half, dim), BF),
        ],
        compiler_params=params("arbitrary"),
        cost_estimate=cost(8.5),
        name="down",
    )(info, hbm(x1), hbm(g), hbm(g), hbm(w_down), hbm(w_down))


def mid_kernel(
    patches, info_ref, dh_ref, recv_ref, x1_ref, dy_ref, w_ref, gain_ref, dx_ref, da_ref, gs_ref,
    *do_refs,
):
    step = pl.program_id(0)
    fb, width, local = do_refs[0].shape
    hat, rstd = normalise(x1_ref[...])
    dh = dh_ref[...] + recv_ref[...].astype(F32)
    dx = dy_ref[...].astype(F32) + norm_back(dh, hat, rstd, gain_ref[...])
    dx_ref[...] = dx
    da = dx.astype(BF)
    da_ref[...] = da
    sums = jnp.concatenate(
        [jnp.sum(dh * hat, axis=0, keepdims=True), jnp.sum(dh, axis=0, keepdims=True)], axis=0
    )

    @pl.when(step == 0)
    def _():
        gs_ref[...] = sums

    @pl.when(step > 0)
    def _():
        gs_ref[...] += sums

    for j, do_ref in enumerate(do_refs):
        part = nt(da, w_ref[heads_rows(info_ref, j, local), :])
        do_ref[...] = part.astype(BF).reshape(fb, width, local)


def mid_call(info, dh, recv, x1, dy, w_out, gain, frames, patches):
    rows, dim = x1.shape
    width = rows // frames
    local = dim // patches
    fb = frames
    row = pl.BlockSpec((rows, dim), lambda i: (i, 0))
    return pl.pallas_call(
        functools.partial(mid_kernel, patches),
        grid=(1,),
        in_specs=[smem(), row, row, row, row, full(w_out.shape), full(gain.shape)],
        out_specs=[row, row, full((2, dim))]
        + [pl.BlockSpec((fb, width, local), lambda i: (i, 0, 0))] * patches,
        out_shape=[
            pltpu.HBM((rows, dim), F32),
            pltpu.HBM((rows, dim), BF),
            jax.ShapeDtypeStruct((2, dim), F32),
        ]
        + [pltpu.HBM((frames, width, local), BF)] * patches,
        compiler_params=params("arbitrary"),
        cost_estimate=cost(6),
        name="mid",
    )(info, hbm(dh), recv, hbm(x1), hbm(dy), hbm(w_out), gain)


def dwq_kernel(groups, pairs, *refs):
    hs = refs[:groups]
    ds = [refs[groups * (1 + p) : groups * (2 + p)] for p in range(pairs)]
    dw_ref, acc_ref = refs[groups * (1 + pairs) :]
    step = pl.program_id(0)

    @pl.when(step == 0)
    def _():
        acc_ref[...] = jnp.zeros(acc_ref.shape, F32)

    total = None
    for n, h_ref in enumerate(hs):
        fb, rows, dim = h_ref.shape
        d = jnp.concatenate([pair[n][...] for pair in ds], axis=2)
        part = tn(h_ref[...].reshape(fb * rows, dim), d.reshape(fb * rows, -1))
        total = part if total is None else total + part
    acc_ref[...] += total

    @pl.when(step == pl.num_programs(0) - 1)
    def _():
        blocked(dw_ref, acc_ref)


def frame_blocks(a, fb):
    return pl.BlockSpec((fb,) + a.shape[1:], lambda i: (i, 0, 0))


def dwq_call(hs, ds):
    groups, pairs = len(hs), len(ds)
    frames, _, dim = hs[0].shape
    fb = max(1, frames // 2 if frames <= 8 else frames // 8)
    flat = [a for d in ds for a in d]
    return pl.pallas_call(
        functools.partial(dwq_kernel, groups, pairs),
        grid=(frames // fb,),
        in_specs=[frame_blocks(a, fb) for a in (*hs, *flat)],
        out_specs=full((3 * pairs, dim, 128)),
        out_shape=pltpu.HBM((3 * pairs, dim, 128), BF),
        scratch_shapes=[pltpu.VMEM((dim, 384 * pairs), F32)],
        compiler_params=params("arbitrary"),
        cost_estimate=cost(7),
        name="dwq",
    )(*[hbm(a) for a in hs], *flat)


def dh_kernel(groups, pairs, width, *refs):
    ds = [refs[n * groups : (n + 1) * groups] for n in range(pairs)]
    w_ref, even_ref, odd_ref = refs[pairs * groups :]
    j = 0
    for n in range(groups):
        fb, rows, _ = ds[0][n].shape
        d = jnp.concatenate([ds[p][n][...] for p in range(pairs)], axis=2)
        dh = nt(d.reshape(fb * rows, -1), w_ref[...]).astype(BF).reshape(fb, rows, -1)
        for at in range(0, rows, width):
            out = odd_ref if j % 2 else even_ref
            out[j // 2] = dh[:, at : at + width]
            j += 1


def dh_call(ds, w_local, patches):
    pairs, groups = len(ds), len(ds[0])
    frames = ds[0][0].shape[0]
    rows = sum(a.shape[1] for a in ds[0])
    width = rows // patches
    dim = w_local.shape[0]
    fb = max(1, frames // 4 if frames <= 8 else frames // 16)
    shape = (patches // 2, frames, width, dim)
    block = pl.BlockSpec((patches // 2, fb, width, dim), lambda i: (0, i, 0, 0))
    return pl.pallas_call(
        functools.partial(dh_kernel, groups, pairs, width),
        grid=(frames // fb,),
        in_specs=[frame_blocks(a, fb) for d in ds for a in d] + [full(w_local.shape)],
        out_specs=[block, block],
        out_shape=[pltpu.HBM(shape, BF)] * 2,
        compiler_params=params("arbitrary"),
        cost_estimate=cost(5),
        name="dh",
    )(*[a for d in ds for a in d], w_local)


def last_kernel(a_ref, b_ref, x_ref, dx_ref, gain_ref, gt_ref, gs_ref):
    step = pl.program_id(0)
    hat, rstd = normalise(x_ref[...].astype(F32))
    dh = a_ref[...].astype(F32) + b_ref[...].astype(F32)
    gt_ref[...] = (dx_ref[...] + norm_back(dh, hat, rstd, gain_ref[...])).astype(BF)
    sums = jnp.concatenate(
        [jnp.sum(dh * hat, axis=0, keepdims=True), jnp.sum(dh, axis=0, keepdims=True)], axis=0
    )

    @pl.when(step == 0)
    def _():
        gs_ref[...] = sums

    @pl.when(step > 0)
    def _():
        gs_ref[...] += sums


def last_call(a, b, x, dx, gain):
    rows, dim = x.shape
    row = pl.BlockSpec((rows // 2, dim), lambda i: (i, 0))
    return pl.pallas_call(
        last_kernel,
        grid=(2,),
        in_specs=[row, row, row, row, full(gain.shape)],
        out_specs=[row, full((2, dim))],
        out_shape=[
            jax.ShapeDtypeStruct((rows, dim), BF),
            jax.ShapeDtypeStruct((2, dim), F32),
        ],
        compiler_params=params("arbitrary"),
        cost_estimate=cost(3),
        name="last",
    )(a, b, hbm(x), hbm(dx), gain)


class Chain:
    def __init__(self, hops):
        self.hops, self.value, self.got, self.begun, self.done = hops, None, None, False, False
        self.move = None

    def request(self):
        try:
            return self.hops.send(self.got) if self.begun else next(self.hops)
        except StopIteration as stop:
            self.value, self.done = stop.value, True
            return None
        finally:
            self.begun = True


class Move:
    def __init__(self, bit, members, got):
        self.bit, self.members, self.got = bit, members, got

    def settle(self, got):
        start = 0
        for chain, a in self.members:
            chain.move = None
            if len(self.members) == 1:
                chain.got = got
            elif self.bit == "patch":
                chain.got = got[start : start + a.shape[0]]
                start += a.shape[0]
            else:
                n = a.size // 128
                chain.got = got[start : start + n].reshape(a.shape)
                start += n


class Stage:
    def __init__(self, links):
        self.links = links

    def start(self, *chains):
        wanted = {}
        for chain in chains:
            if chain.done or chain.move is not None:
                continue
            request = chain.request()
            if request is not None:
                wanted.setdefault(request[0], []).append((chain, request[1]))
        for bit, members in wanted.items():
            arrays = [a for _, a in members]
            if bit == "patch":
                sent = arrays[0] if len(arrays) == 1 else jnp.concatenate(arrays, axis=0)
                got = lax.all_to_all(sent, "patch", 1, 1, tiled=True)
            elif len(arrays) == 1:
                got = self.links.swap(arrays[0], bit)
            else:
                sent = jnp.concatenate([a.reshape(-1, 128) for a in arrays], axis=0)
                got = self.links.swap(sent, bit)
            move = Move(bit, members, got)
            for chain, _ in members:
                chain.move = move

    def join(self, values, *chains):
        moves = []
        for chain in chains:
            if chain.move is not None and chain.move not in moves:
                moves.append(chain.move)
        held, values = lax.optimization_barrier(([m.got for m in moves], values))
        for move, got in zip(moves, held):
            move.settle(got)
        return values


class Links:
    def __init__(self, batches, patches):
        self.batches, self.patches = batches, patches
        self.patch = lax.axis_index("patch")
        self.batch = lax.axis_index("batch")
        self.bits = {"c": [("p", 1)], "y": [("b", 1)], "x": [], "z": []}
        bit = 2
        while bit < patches:
            self.bits["x"].append(("p", bit))
            bit *= 2
        bit = 2
        while bit < batches:
            self.bits["z"].append(("b", bit))
            bit *= 2

    def swap(self, a, bit):
        axis, step = bit
        step = step if axis == "p" else step * self.patches
        n = self.batches * self.patches
        return lax.ppermute(a, AXES, [(i, i ^ step) for i in range(n)])

    def swap_patch(self, a, bit):
        return self.swap(a, ("p", bit))

    def mine(self, bit):
        axis, step = bit
        return ((self.patch if axis == "p" else self.batch) // step) & 1

    def expand(self, order):
        if not isinstance(order, str):
            return order
        bits = []
        for axis in order:
            one = self.bits[axis.lower()]
            bits += one if axis.islower() else one[::-1]
        return bits

    def hops(self, a, axes, order, back, trade, layout, first, raw):
        if first is not None:
            got = yield first
            a = (a.astype(F32) + got.astype(F32)).astype(BF)
        names = list(self.expand(axes))
        blocks, rows, _ = a.shape
        a = a.reshape((blocks,) + (2,) * len(names) + (rows // 2 ** len(names), 128))
        layout = self.expand(layout)
        for bit in self.expand(order):
            at = names.index(bit) + 1
            names.pop(at - 1)
            got = yield bit, lax.dynamic_index_in_dim(a, 1 - self.mine(bit), at, keepdims=False)
            keep = lax.dynamic_index_in_dim(a, self.mine(bit), at, keepdims=False)
            a = (keep.astype(F32) + got.astype(F32)).astype(BF)
        if trade is not None and trade != "patch":
            bit = ("p", 1)
            size = a.shape[1:]
            pairs = a[:trade].reshape((trade // 2, 2) + size)
            got = yield bit, lax.dynamic_index_in_dim(pairs, 1 - self.mine(bit), 1, keepdims=False)
            own = lax.dynamic_index_in_dim(pairs, self.mine(bit), 1, keepdims=False)
            a = jnp.concatenate([self.join(own, got, bit, 0).reshape((trade,) + size), a[trade:]])
        if trade == "patch":
            a = a.reshape((blocks, self.patches) + a.shape[-2:])
            a = yield "patch", a
            a = a.reshape((blocks * self.patches,) + a.shape[-2:])
        have = []
        for bit in self.expand(back):
            got = yield bit, a
            at = 1 + sum(layout.index(other) < layout.index(bit) for other in have)
            have.append(bit)
            if raw and len(have) == len(self.expand(back)):
                return a, got
            a = self.join(a, got, bit, at)
        return a.reshape(a.shape[0], -1, 128)

    def join(self, a, got, bit, at):
        return jnp.where(
            self.mine(bit) == 0, jnp.stack([a, got], axis=at), jnp.stack([got, a], axis=at)
        )

    def chain(self, a, axes, order, back, trade=None, layout="yz", first=None, raw=False):
        return Chain(self.hops(a, axes, order, back, trade, layout, first, raw))

    def apart(self, a):
        got = {0: a}
        bit = self.patches // 2
        while bit > 1:
            for j in sorted(got):
                got[j | bit] = self.swap_patch(got[j], bit)
            bit //= 2
        return got

    def items(self, a):
        got = self.apart(a)
        for j in sorted(got):
            got[j | 1] = self.swap_patch(got[j], 1)
        return got

    def deal(self, parts):
        return [parts[0]] + [self.swap_patch(parts[j], j) for j in range(1, self.patches)]


def assemble_q_kernel(order, valid, info_ref, mine_ref, got_ref, out):
    own = info_ref[info_ref.shape[0] - 2] == pl.program_id(0)
    pieces = [jnp.where(own, mine_ref[b], got_ref[b])[:, :valid].astype(F32) for b in order]
    out[...] = jnp.concatenate(pieces, axis=1)


def assemble_q(info, pair, order, valid):
    mine, got = (a.reshape(a.shape[0], -1, 128) for a in pair)
    blocks, rows, _ = mine.shape
    return pl.pallas_call(
        functools.partial(assemble_q_kernel, order, valid),
        grid=(2,),
        in_specs=[smem()] + [full(mine.shape)] * 2,
        out_specs=pl.BlockSpec((rows, len(order) * valid), lambda i: (i, 0)),
        out_shape=jax.ShapeDtypeStruct((2 * rows, len(order) * valid), F32),
        compiler_params=params("arbitrary"),
        cost_estimate=cost(2),
        name="assemble_q",
    )(info, mine, got)


def assemble_w_kernel(ups, wos, info_ref, *refs):
    up_ref, wo_ref = refs[4:]
    count = info_ref.shape[0]
    y, z = pl.program_id(0) // 2, pl.program_id(0) % 2
    own_y = info_ref[count - 2] == y
    own_z = info_ref[count - 1] == z

    def block(n, b):
        if n == 0:
            return jnp.where(own_z, refs[0][b, y], refs[1][b, y]).astype(F32)
        return jnp.where(own_y, refs[2][b, z], refs[3][b, z]).astype(F32)

    for ref, order in ((up_ref, ups), (wo_ref, wos)):
        for at, (n, b) in enumerate(order):
            ref[:, at * 128 : (at + 1) * 128] = block(n, b)


def assemble_w(info, first, second, ups, wos):
    arrays = [a.reshape(a.shape[0], 2, -1, 128) for a in (*first, *second)]
    rows = arrays[0].shape[2]
    return pl.pallas_call(
        functools.partial(assemble_w_kernel, ups, wos),
        grid=(4,),
        in_specs=[smem()] + [full(a.shape) for a in arrays],
        out_specs=[
            pl.BlockSpec((rows, len(order) * 128), lambda i: (i, 0)) for order in (ups, wos)
        ],
        out_shape=[
            jax.ShapeDtypeStruct((4 * rows, len(order) * 128), F32) for order in (ups, wos)
        ],
        compiler_params=params("arbitrary"),
        cost_estimate=cost(3),
        name="assemble_w",
    )(info, *arrays)


def pieces_kernel(steps, a_ref, out):
    piece = pl.program_id(0) // steps
    blocks = a_ref.shape[0] // 2

    def put(n):
        for b in range(blocks):
            out[:, b * 128 : (b + 1) * 128] = a_ref[2 * b + n].astype(F32)

    for n in range(2):
        pl.when(piece == n)(functools.partial(put, n))


def pieces_call(a):
    blocks, rows, _ = a.shape
    step = min(rows, 128)
    steps = rows // step
    return pl.pallas_call(
        functools.partial(pieces_kernel, steps),
        grid=(2 * steps,),
        in_specs=[pl.BlockSpec((blocks, step, 128), lambda i: (0, i % steps, 0))],
        out_specs=pl.BlockSpec((step, blocks * 64), lambda i: (i, 0)),
        out_shape=jax.ShapeDtypeStruct((2 * rows, blocks * 64), F32),
        compiler_params=params("arbitrary"),
        cost_estimate=cost(4),
        name="pieces",
    )(a)


def tables(code, times):
    head = 64
    half = head // 6
    band = 2 * half
    dims = jnp.arange(head)
    freq = jnp.power(THETA, -2.0 * (dims % half).astype(F32) / band)
    places = jnp.stack([times, (code // GRID).astype(F32), (code % GRID).astype(F32)], axis=-1)
    which = jnp.minimum(dims // band, 2)
    pick = jnp.where(
        which == 0, places[..., 0:1], jnp.where(which == 1, places[..., 1:2], places[..., 2:3])
    )
    angle = pick * freq
    turned = dims < 3 * band
    cos = jnp.where(turned, jnp.cos(angle), 1.0)
    sin = jnp.where(turned, jnp.sin(angle) * jnp.where(dims % band < half, -1.0, 1.0), 0.0)
    return jnp.concatenate([cos, cos, sin, sin], axis=-1)


def per_device(
    batches, patches, tokens, cotangent, episode_frames, kinds, patch_pos,
    ln1_gain, ln1_shift, w_qkv, w_out, ln2_gain, ln2_shift, w_up, w_down,
):
    tokens = tokens[0]
    frames, width, dim = tokens.shape
    rows = frames * width
    local = dim // patches
    links = Links(batches, patches)
    me = links.patch
    core = me & 1
    gain1, shift1, gain2, shift2 = (
        a.astype(F32).reshape(1, dim) for a in (ln1_gain, ln1_shift, ln2_gain, ln2_shift)
    )
    dy = cotangent.reshape(rows, dim)

    code = jnp.where(kinds[0] == 0, patch_pos[0], 0)
    codes = links.items(code)
    mate = links.swap_patch(tokens, 1)
    dy_mate = links.swap_patch(dy, 1)
    apart = links.apart(tokens)
    ends = jnp.cumsum(episode_frames[0])
    frame_ids = jnp.arange(frames, dtype=jnp.int32)
    starts = jnp.max(
        jnp.where(ends[None, :] <= frame_ids[:, None], ends[None, :], 0), axis=1
    )
    firsts = [links.mine(bits[0])[None] for bits in (links.bits["y"], links.bits["z"])]
    info = jnp.concatenate([me[None], starts, *firsts]).astype(jnp.int32)
    pad = max(128, local)
    pairs = pad // 128
    valid = min(128, local)
    if valid == 128:
        w_local = columns_call(info, w_qkv, pairs)
    else:
        columns = []
        for n in range(3):
            at = n * dim + me * local
            columns.append(lax.dynamic_slice(w_qkv, (jnp.int32(0), at), (dim, valid)))
            columns.append(jnp.zeros((dim, 128 - valid), BF))
        w_local = jnp.concatenate(columns, axis=1)

    members = [[0, 1], list(range(2, patches))]
    css = []
    for group in members:
        place = jnp.concatenate([codes[j] for j in group], axis=1)
        times = jnp.broadcast_to(frame_ids.astype(F32)[:, None], place.shape)
        css.append(tables(place, times))
    near = qkv_call([tokens, mate], css[0], w_local, gain1, shift1)
    dg = pre_call(info, dy, dy_mate, w_down, patches)
    near, dg, apart, css = lax.optimization_barrier((near, dg, apart, css))
    far_items = []
    for j in range(2, patches, 2):
        far_items += [apart[j], links.swap_patch(apart[j], 1)]
    far = qkv_call(far_items, css[1], w_local, gain1, shift1)
    hs, qkvs = [near[0], far[0]], [near[1], far[1]]

    *o_send, o_full, lse = attend_call(info, qkvs, patches)
    o_in = links.deal([a[..., :local] for a in o_send])
    x1, h2, o_own = project_call(info, o_in, tokens, w_out, gain2, shift2)
    h2_mate = links.swap_patch(h2, 1)
    o_mate = links.swap_patch(o_own, 1)
    stage = Stage(links)
    g, du, keep0, send0, keep1, send1, dh_own, dh_mate = ffn_call(
        info, h2, h2_mate, dy, dy_mate, dg, w_up, patches
    )
    inner, outer = links.bits["z"][:1], links.bits["z"][1:]
    ys, xs = links.bits["y"], links.bits["x"]

    def two_pieces(a):
        return a.reshape(a.shape[0] * 2, a.shape[1] // 2, 128)

    def step(held, *chains):
        held = stage.join(held, *chains)
        for chain in chains:
            stage.start(chain)
        return held

    def finish(held, *chains):
        while not all(c.done for c in chains):
            held = step(held, *chains)
        return held

    d1 = links.chain(two_pieces(keep0), xs[::-1] + inner + outer, inner, "", first=(ys[0], two_pieces(send0)))
    d2 = links.chain(two_pieces(keep1), xs[::-1] + ys + outer, ys, "", first=(inner[0], two_pieces(send1)))
    stage.start(d1)
    stage.start(d2)
    dh_recv = links.swap_patch(dh_mate, 1)
    dx1, da, sums2, *d_o = mid_call(
        info, dh_own, dh_recv, x1, dy, w_out, gain2, frames, patches
    )
    da_mate = links.swap_patch(da, 1)
    do_in = links.deal(d_o)
    sides = (o_own, o_mate, da, da_mate)
    dw1 = up_call(info, h2, h2_mate, du, *sides, patches, 0)
    dw2 = up_call(info, h2, h2_mate, du, *sides, patches, 1)
    out_own, out_mate = down_call(info, x1, g, w_down, patches)
    do_in, dw1, dw2, out_own, out_mate = step((do_in, dw1, dw2, out_own, out_mate), d1, d2)
    out_recv = links.swap_patch(out_mate, 1)
    u1 = links.chain(dw1, "Xcyz", xs + inner + ys, "")
    u2 = links.chain(dw2, "Xcyz", ys + xs + inner, "")
    stage.start(u1)
    if pad > local:
        do_in = [jnp.pad(a, ((0, 0), (0, 0), (0, pad - local))) for a in do_in]
    dqkv = attend_back_call(info, qkvs, css, do_in, o_full, lse, patches, 0)
    dqkv, do_in = step((dqkv, do_in), d1, d2)
    dqkv = finish(dqkv, d1, d2)
    dqkvs = [dqkv]
    d = links.chain(
        jnp.concatenate([d1.value, d2.value], axis=0),
        xs[::-1] + outer,
        outer + xs,
        outer[::-1] + inner + ys,
    )
    stage.start(d)
    stage.start(u2)
    for pair in range(1, pairs):
        dqkvs.append(attend_back_call(info, qkvs, css, do_in, o_full, lse, patches, pair))
    dwq = dwq_call(hs, dqkvs)
    even, odd = dh_call(dqkvs, w_local, patches)
    odd, even, dwq = stage.join((odd, even, dwq), u1, d, u2)
    q = links.chain(dwq, "Xcyz", "yz", "zy", "patch", raw=True)
    for chain in (q, u1, d, u2):
        stage.start(chain)
    odd = links.swap_patch(odd, 1)
    odd, even, sums2 = step((odd, even, sums2), u1)
    slots = (even.astype(F32) + odd.astype(F32)).astype(BF)
    bit = patches // 2
    while bit > 2:
        n = slots.shape[0] // 2
        slots = (slots[:n].astype(F32) + links.swap_patch(slots[n:], bit).astype(F32)).astype(BF)
        bit //= 2
    got = links.swap_patch(slots[1], 2)
    sums2 = step(sums2, q)
    sums2 = step(sums2, u2, d)
    sums2 = step(sums2, u1, u2)
    sums2 = finish(sums2, u1, u2)
    w = jnp.concatenate([u1.value, u2.value], axis=0)
    w = w.reshape(2 * w.shape[0], -1, 128)
    w = links.chain(w, outer, outer, outer[::-1], w.shape[0])
    stage.start(w)
    sums2 = step(sums2, q)
    sums2 = step(sums2, d)
    sums2 = step(sums2, w)
    slots, got, sums2 = step((slots, got, sums2), q)
    sums2 = step(sums2, w)
    sums2 = step(sums2, d)
    grad_tokens, sums1 = last_call(
        slots[0].reshape(rows, dim), got.reshape(rows, dim), tokens.reshape(rows, dim), dx1, gain1
    )
    sums = jnp.concatenate([sums1, sums2], axis=0)
    sums = step(sums, q)
    sums = step(sums, w)
    sums = finish(sums, w)
    half = w.value.shape[0] // 2
    wa = links.chain(w.value[:half], [], [], ys + inner, raw=True)
    wb = links.chain(w.value[half:], [], [], inner + ys, raw=True)
    stage.start(wa)
    stage.start(wb)
    sums, out_own, out_recv = step((sums, out_own, out_recv), q)
    out = (out_own + out_recv.astype(F32)).astype(BF)
    sums = sums.reshape(4, patches, local).transpose(1, 0, 2)
    sums = jnp.broadcast_to(sums[None], (batches,) + sums.shape)
    sums = lax.all_to_all(sums.reshape((-1,) + sums.shape[2:]), AXES, 0, 0, tiled=True)
    held = step(grad_tokens, wa, wb)
    held = step(held, q)
    held = step(held, d)
    held, sums = step((held, sums), wa, wb)
    grad_tokens = step(held, q)
    sums = jnp.sum(sums, axis=0)
    grad_tokens = finish(grad_tokens, wa, wb)
    grad_tokens = finish(grad_tokens, q)
    grad_tokens = finish(grad_tokens, d)
    down = pieces_call(d.value)

    nx = patches // 2
    each = dw1.shape[0]
    per = (each - dim // 512) // nx
    ups, wos = [], []
    for owner in range(2):
        for n in range(2):
            wos += [(owner, n * each + nx * per + t) for t in range(dim // 512)]
    for i in range(nx):
        for owner in range(2):
            for n in range(2):
                ups += [(owner, n * each + i * per + t) for t in range(per)]
    up, grad_wo = assemble_w(info, wa.value, wb.value, ups, wos)
    order = []
    for n in range(3):
        for p in range(patches):
            order += [(pair * 3 + n) * patches + p for pair in range(pairs)]
    qkv = assemble_q(info, q.value, order, valid)

    return (
        out.reshape(1, frames, width, dim),
        grad_tokens.reshape(1, frames, width, dim),
        sums[0],
        sums[1],
        qkv,
        grad_wo,
        sums[2],
        sums[3],
        up,
        down,
    )


def solution(mesh):
    placed = (
        P("batch", None, "patch", None),
        P("batch", None, "patch", None),
        P("batch", None),
        P("batch", None, "patch"),
        P("batch", None, "patch"),
    ) + (P(),) * 8
    return jax.shard_map(
        functools.partial(per_device, mesh.shape["batch"], mesh.shape["patch"]),
        mesh=mesh,
        in_specs=placed,
        out_specs=(
            P("batch", None, "patch", None),
            P("batch", None, "patch", None),
            P("patch"),
            P("patch"),
            P("patch", None),
            P("patch", None),
            P("patch"),
            P("patch"),
            P("patch", None),
            P("patch", None),
        ),
        check_vma=False,
    )
```

```python
import functools
import math

import jax
import jax.numpy as jnp
from jax import lax
from jax.experimental import pallas as pl
from jax.experimental.pallas import tpu as pltpu
from jax.sharding import PartitionSpec as P

GRID = 16
EPS = 1e-06
THETA = 10000.0
MASKED = -1e30
LIMIT = 40 * 1024 * 1024
BF = jnp.bfloat16
F32 = jnp.float32
AXES = ("batch", "patch")


def nn(a, b):
    return lax.dot_general(a, b, (((1,), (0,)), ((), ())), preferred_element_type=F32)


def nt(a, b):
    return lax.dot_general(a, b, (((1,), (1,)), ((), ())), preferred_element_type=F32)


def tn(a, b):
    return lax.dot_general(a, b, (((0,), (0,)), ((), ())), preferred_element_type=F32)


def params(*semantics):
    return pltpu.CompilerParams(
        dimension_semantics=semantics, vmem_limit_bytes=LIMIT
    )


def cost(micros):
    return pl.CostEstimate(flops=int(micros * 5e+08), bytes_accessed=1, transcendentals=0)


def full(shape, memory=None):
    zeros = (0,) * len(shape)
    return pl.BlockSpec(shape, lambda *_: zeros)


def blocked(ref, value):
    for n in range(ref.shape[0]):
        ref[n] = value[:, n * 128 : (n + 1) * 128].astype(BF)


def hbm(a):
    return pltpu.with_memory_space_constraint(a, pltpu.HBM)


def smem():
    return pl.BlockSpec(memory_space=pltpu.SMEM)


def normalise(x):
    mean = jnp.mean(x, axis=-1, keepdims=True)
    centred = x - mean
    spread = jnp.mean(centred * centred, axis=-1, keepdims=True)
    rstd = lax.rsqrt(spread + EPS)
    return centred * rstd, rstd


def norm_back(d_h, hat, rstd, gain):
    d_hat = d_h * gain
    first = jnp.mean(d_hat, axis=-1, keepdims=True)
    second = jnp.mean(d_hat * hat, axis=-1, keepdims=True)
    return rstd * (d_hat - first - hat * second)


def partner(value):
    head = 64
    half = head // 6
    width = value.shape[1]
    ahead = jnp.concatenate([value[:, half:], value[:, :half]], axis=1)
    behind = jnp.concatenate([value[:, width - half :], value[:, : width - half]], axis=1)
    lane = lax.broadcasted_iota(jnp.int32, value.shape, 1) % head
    return jnp.where(lane % (2 * half) < half, ahead, behind)


def columns_kernel(info_ref, w_ref, out_ref):
    out_ref[...] = w_ref[...]


def columns_call(info, w_qkv, pairs):
    dim = w_qkv.shape[0]
    blocks = dim // 128

    def at(i, info):
        return (0, (i % 3) * blocks + info[0] * pairs + i // 3)

    return pl.pallas_call(
        columns_kernel,
        grid_spec=pltpu.PrefetchScalarGridSpec(
            num_scalar_prefetch=1,
            grid=(3 * pairs,),
            in_specs=[pl.BlockSpec((dim, 128), at)],
            out_specs=pl.BlockSpec((dim, 128), lambda i, info: (0, i)),
        ),
        out_shape=jax.ShapeDtypeStruct((dim, 384 * pairs), BF),
        compiler_params=params("arbitrary"),
        cost_estimate=cost(2),
        name="columns",
    )(info, hbm(w_qkv))


def qkv_kernel(count, local, *refs):
    tok = refs[:count]
    cs_ref, w_ref, gain_ref, shift_ref = refs[count : count + 4]
    h_ref, qkv_ref = refs[count + 4 :]
    x = jnp.concatenate([t[...] for t in tok], axis=1)
    fb, rows, dim = x.shape
    x = x.reshape(fb * rows, dim).astype(F32)
    hat, _ = normalise(x)
    h = (hat * gain_ref[...] + shift_ref[...]).astype(BF)
    h_ref[...] = h.reshape(fb, rows, dim)
    y = nn(h, w_ref[...])
    cs = cs_ref[...].reshape(fb * rows, 256)
    cos = cs[:, :128]
    sin = cs[:, 128:]
    for at in range(0, 3 * local, 384):
        q = y[:, at : at + 128]
        k = y[:, at + 128 : at + 256]
        q = (q * cos + partner(q) * sin).astype(BF) * BF(0.125)
        k = (k * cos + partner(k) * sin).astype(BF)
        v = y[:, at + 256 : at + 384].astype(BF)
        qkv_ref[:, :, at : at + 128] = q.reshape(fb, rows, 128)
        qkv_ref[:, :, at + 128 : at + 256] = k.reshape(fb, rows, 128)
        qkv_ref[:, :, at + 256 : at + 384] = v.reshape(fb, rows, 128)


def qkv_call(items, cs, w_local, gain, shift):
    count = len(items)
    frames, width, dim = items[0].shape
    local = w_local.shape[1] // 3
    rows = count * width
    fb = max(1, min(frames, 512 // rows))
    while frames % fb:
        fb -= 1
    shapes = [
        pltpu.HBM((frames, rows, dim), BF),
        pltpu.HBM((frames, rows, 3 * local), BF),
    ]
    return pl.pallas_call(
        functools.partial(qkv_kernel, count, local),
        grid=(frames // fb,),
        in_specs=[pl.BlockSpec((fb, width, dim), lambda i: (i, 0, 0))] * count
        + [
            pl.BlockSpec((fb, rows, 256), lambda i: (i, 0, 0)),
            full(w_local.shape),
            full(gain.shape),
            full(shift.shape),
        ],
        out_specs=[
            pl.BlockSpec((fb, rows, dim), lambda i: (i, 0, 0)),
            pl.BlockSpec((fb, rows, 3 * local), lambda i: (i, 0, 0)),
        ],
        out_shape=shapes,
        compiler_params=params("arbitrary"),
        cost_estimate=cost(5.5),
        name="qkv",
    )(*items, cs, w_local, gain, shift)


def lane_halves(shape):
    lane = lax.broadcasted_iota(jnp.int32, shape, 1)
    return lane < 64


def attend_kernel(groups, local, patches, most, info_ref, *refs):
    ins = refs[:groups]
    o_refs = refs[groups : groups + patches]
    of_ref, lse_ref = refs[groups + patches :]
    f = pl.program_id(0)
    begin = info_ref[1 + f]
    rows = sum(r.shape[1] for r in ins)
    low = lane_halves((rows, 128))
    one = jnp.ones((rows, 128), BF)
    zero = jnp.zeros((rows, 128), BF)
    lane = lax.broadcasted_iota(jnp.int32, (rows, 128), 1)

    def part_of(g, pair, n):
        at = pair * 384 + n * 128
        return jnp.concatenate([r[g, :, at : at + 128] for r in ins], axis=0)

    def finish(pair, tops, accs, lses):
        num = jnp.where(low, accs[0], accs[1])
        den = pltpu.roll(jnp.where(low, accs[1], accs[0]), 64, 1)
        of_ref[0, :, pair * 128 : (pair + 1) * 128] = num / den
        logs = jnp.log(jnp.where(low, accs[1], accs[0]))
        lses = jnp.where(lane == 2 * pair + 64, tops[0] + logs, lses)
        return jnp.where(lane == 2 * pair + 1, tops[1] + logs, lses)

    def store(lses):
        even = lane % 2 == 0
        lses = jnp.where(even, pltpu.roll(lses, 64, 1), lses)
        lse_ref[0] = lses.T[:8]

    def whole(count):
        lses = jnp.zeros((rows, 128), F32)
        for pair in range(local // 128):
            q = part_of(f, pair, 0)
            tops, accs = [], []
            for h in range(2):
                qm = jnp.where(low == (h == 0), q, zero)
                scores = [nt(qm, part_of(begin + n, pair, 1)) for n in range(count)]
                top = scores[0]
                for s in scores[1:]:
                    top = jnp.maximum(top, s)
                top = jnp.max(top, axis=1, keepdims=True)
                acc = None
                for n, s in enumerate(scores):
                    v = jnp.where(low == (h == 0), part_of(begin + n, pair, 2), one)
                    part = nn(jnp.exp(s - top).astype(BF), v)
                    acc = part if acc is None else acc + part
                tops.append(top)
                accs.append(acc)
            lses = finish(pair, tops, accs, lses)
        store(lses)

    if most <= 4:
        for count in range(1, most + 1):
            pl.when(f + 1 - begin == count)(functools.partial(whole, count))
    else:
        lses = jnp.zeros((rows, 128), F32)
        for pair in range(local // 128):
            q = part_of(f, pair, 0)

            def body(g, state, pair=pair, q=q):
                new = []
                for h in range(2):
                    top, acc = state[2 * h : 2 * h + 2]
                    qm = jnp.where(low == (h == 0), q, zero)
                    s = nt(qm, part_of(g, pair, 1))
                    new_top = jnp.maximum(top, jnp.max(s, axis=1, keepdims=True))
                    v = jnp.where(low == (h == 0), part_of(g, pair, 2), one)
                    p = jnp.exp(s - new_top).astype(BF)
                    new += [new_top, acc * jnp.exp(top - new_top) + nn(p, v)]
                return tuple(new)

            blank = (jnp.full((rows, 1), MASKED, F32), jnp.zeros((rows, 128), F32))
            state = lax.fori_loop(begin, f + 1, body, blank + blank)
            lses = finish(pair, state[0::2], state[1::2], lses)
        store(lses)

    o = of_ref[0].astype(BF)
    width = rows // patches
    for j in range(patches):
        o_refs[j][0] = o[j * width : (j + 1) * width]


def attend_call(info, qkv, patches):
    groups = len(qkv)
    frames = qkv[0].shape[0]
    local = qkv[0].shape[2] // 3
    rows = sum(a.shape[1] for a in qkv)
    width = rows // patches
    shapes = [jax.ShapeDtypeStruct((frames, width, local), BF)] * patches
    sizes = [(frames, width, local)] * patches + [(frames, rows, local), (frames, 8, rows)]
    shapes += [pltpu.HBM((frames, rows, local), F32), pltpu.HBM((frames, 8, rows), F32)]
    return pl.pallas_call(
        functools.partial(attend_kernel, groups, local, patches, frames // 2),
        grid=(frames,),
        in_specs=[smem()] + [full(a.shape) for a in qkv],
        out_specs=[pl.BlockSpec((1,) + s[1:], lambda i: (i, 0, 0)) for s in sizes],
        out_shape=shapes,
        compiler_params=params("arbitrary"),
        cost_estimate=cost(12.5),
        name="attend",
    )(info, *[hbm(a) for a in qkv])


def attend_back_kernel(groups, pair, patches, info_ref, *refs):
    ins = refs[:groups]
    css = refs[groups : 2 * groups]
    do_refs = refs[2 * groups : 2 * groups + patches]
    refs = refs[2 * groups + patches :]
    of_ref, lse_ref = refs[:2]
    outs = refs[2 : groups + 2]
    dk_ref, dv_ref, dq_ref, kt_ref = refs[groups + 2 :]
    f = pl.program_id(0)
    frames = pl.num_programs(0)
    begin = info_ref[1 + f]

    def part_of(g, n):
        return jnp.concatenate([r[g, :, n * 128 : (n + 1) * 128] for r in ins], axis=0)

    q = part_of(f, 0)
    d_o = jnp.concatenate([r[0] for r in do_refs], axis=0)
    rows = q.shape[0]
    low = lane_halves((rows, 128))
    zero = jnp.zeros((rows, 128), BF)
    turned = (d_o.astype(F32) * of_ref[0]).T
    delta = [jnp.sum(turned[h * 64 : (h + 1) * 64], axis=0, keepdims=True) for h in range(2)]
    lse = lse_ref[0, 2 * pair : 2 * pair + 2]
    dk_ref[f] = jnp.zeros((rows, 128), F32)
    dv_ref[f] = jnp.zeros((rows, 128), F32)
    dq_ref[...] = jnp.zeros((128, rows), F32)
    kt_ref[f] = part_of(f, 1).T
    qm = [jnp.where(low == (h == 0), q, zero) for h in range(2)]
    dom = [jnp.where(low == (h == 0), d_o, zero) for h in range(2)]

    @pl.loop(begin, f + 1)
    def _(g):
        k = part_of(g, 1)
        v = part_of(g, 2)
        scores = [nt(k, qm[h]) for h in range(2)]
        dps = [nt(v, dom[h]) for h in range(2)]
        dk = dv = None
        for h in range(2):
            p = jnp.exp(scores[h] - lse[h : h + 1])
            ds = (p * (dps[h] - delta[h])).astype(BF)
            dq_ref[h * 64 : (h + 1) * 64] += nn(kt_ref[g, h * 64 : (h + 1) * 64], ds)
            part_k = nn(ds, qm[h])
            part_v = nn(p.astype(BF), dom[h])
            dk = part_k if dk is None else dk + part_k
            dv = part_v if dv is None else dv + part_v
        dk_ref[g] += dk
        dv_ref[g] += dv

    def turn_back(t, value):
        cs = jnp.concatenate([r[t] for r in css], axis=0)
        return (value * cs[:, :128] - partner(value) * cs[:, 128:]).astype(BF)

    def put(t, n, value):
        start = 0
        for out in outs:
            count = out.shape[1]
            out[t, :, n * 128 : (n + 1) * 128] = value[start : start + count]
            start += count

    put(f, 0, turn_back(f, dq_ref[...].T * 0.125))

    @pl.when(f == frames - 1)
    def _():
        @pl.loop(0, frames)
        def _(t):
            put(t, 1, turn_back(t, dk_ref[t]))
            put(t, 2, dv_ref[t].astype(BF))


def attend_back_call(info, qkv, cs, d_o, o_full, lse, patches, pair):
    groups = len(qkv)
    frames = qkv[0].shape[0]
    rows = sum(a.shape[1] for a in qkv)
    width = rows // patches
    shapes = [jax.ShapeDtypeStruct((frames, a.shape[1], 384), BF) for a in qkv]
    return pl.pallas_call(
        functools.partial(attend_back_kernel, groups, pair, patches),
        grid=(frames,),
        in_specs=[smem()]
        + [pl.BlockSpec(a.shape[:2] + (384,), lambda i: (0, 0, pair)) for a in qkv]
        + [full(a.shape) for a in cs]
        + [pl.BlockSpec((1, width, 128), lambda i: (i, 0, pair))] * patches
        + [
            pl.BlockSpec((1, rows, 128), lambda i: (i, 0, pair)),
            pl.BlockSpec((1, 8, rows), lambda i: (i, 0, 0)),
        ],
        out_specs=[full(s.shape) for s in shapes],
        out_shape=shapes,
        scratch_shapes=[
            pltpu.VMEM((frames, rows, 128), F32),
            pltpu.VMEM((frames, rows, 128), F32),
            pltpu.VMEM((128, rows), F32),
            pltpu.VMEM((frames, 128, rows), BF),
        ],
        compiler_params=params("arbitrary"),
        cost_estimate=cost(15),
        name="attend_back",
    )(info, *[hbm(a) for a in (*qkv, *cs)], *d_o, hbm(o_full), hbm(lse))


def heads_rows(info_ref, j, local):
    return pl.ds(pl.multiple_of((info_ref[0] ^ j) * local, local), local)


def project_kernel(patches, info_ref, *refs):
    o_refs = refs[:patches]
    x_ref, w_ref, gain_ref, shift_ref, x1_ref, h_ref, o_ref, kept_ref = refs[patches:]
    fb, width, local = o_refs[0].shape
    rows = fb * width
    for j, ref in enumerate(o_refs):
        kept_ref[j] = ref[...].reshape(rows, local)
    o = jnp.concatenate([kept_ref[info_ref[0] ^ p] for p in range(patches)], axis=1)
    o_ref[...] = o
    acc = x_ref[...].astype(F32).reshape(rows, -1) + nn(o, w_ref[...])
    x1_ref[...] = acc
    hat, _ = normalise(acc)
    h_ref[...] = (hat * gain_ref[...] + shift_ref[...]).astype(BF)


def project_call(info, o_in, tokens, w_out, gain, shift):
    patches = len(o_in)
    frames, width, local = o_in[0].shape
    dim = w_out.shape[0]
    fb = frames
    rows = frames * width
    return pl.pallas_call(
        functools.partial(project_kernel, patches),
        grid=(1,),
        in_specs=[smem()]
        + [pl.BlockSpec((fb, width, local), lambda i: (i, 0, 0))] * patches
        + [
            pl.BlockSpec((fb, width, dim), lambda i: (i, 0, 0)),
            full(w_out.shape),
            full(gain.shape),
            full(shift.shape),
        ],
        out_specs=[
            pl.BlockSpec((rows, dim), lambda i: (i, 0)),
            pl.BlockSpec((rows, dim), lambda i: (i, 0)),
            pl.BlockSpec((rows, dim), lambda i: (i, 0)),
        ],
        out_shape=[
            pltpu.HBM((rows, dim), F32),
            jax.ShapeDtypeStruct((rows, dim), BF),
            jax.ShapeDtypeStruct((rows, dim), BF),
        ],
        scratch_shapes=[pltpu.VMEM((patches, rows, local), BF)],
        compiler_params=params("arbitrary"),
        cost_estimate=cost(3.7),
        name="project",
    )(info, *o_in, tokens, w_out, gain, shift)


def tile_at(piece, steps):
    return lambda i, info: ((i % steps) * 2 + (info[0] & 1)) * 2 + (
        i // steps if piece is None else piece
    )


def pre_kernel(info_ref, dy_own, dy_mate, down_ref, dg_ref):
    half = dy_own.shape[0]
    dg_ref[:half] = nt(dy_own[...], down_ref[...]).astype(BF)
    dg_ref[half:] = nt(dy_mate[...], down_ref[...]).astype(BF)


def pre_call(info, dy_own, dy_mate, w_down, patches):
    half, dim = dy_own.shape
    hidden = w_down.shape[0]
    tile, steps = hidden // patches // 2, patches // 2
    at = tile_at(None, steps)
    return pl.pallas_call(
        pre_kernel,
        grid_spec=pltpu.PrefetchScalarGridSpec(
            num_scalar_prefetch=1,
            grid=(2 * steps,),
            in_specs=[full((half, dim))] * 2
            + [pl.BlockSpec((tile, dim), lambda i, info: (at(i, info), 0))],
            out_specs=pl.BlockSpec((2 * half, tile), lambda i, info: (0, i)),
        ),
        out_shape=pltpu.HBM((2 * half, hidden // 2), BF),
        compiler_params=params("arbitrary"),
        cost_estimate=cost(8.5),
        name="pre",
    )(info, dy_own, dy_mate, w_down)


def ffn_kernel(
    info_ref, h_own, h_mate, dy_own, dy_mate, dg_ref, up_ref,
    g_ref, du_ref, keep0, send0, keep1, send1, dh_own, dh_mate, acc_ref,
):
    step = pl.program_id(0)
    half = h_own.shape[0]

    @pl.when(step == 0)
    def _():
        acc_ref[...] = jnp.zeros(acc_ref.shape, F32)

    w_up = up_ref[...]
    chunk = half // 2
    for n in range(4):
        h_ref = (h_own, h_mate)[n // 2]
        here = slice((n % 2) * chunk, (n % 2 + 1) * chunk)
        rows = slice(n * chunk, (n + 1) * chunk)
        u = nn(h_ref[here], w_up)
        cdf = 0.5 + 0.5 * lax.erf(u * math.sqrt(0.5))
        pdf = jnp.exp(u * u * -0.5) * (1.0 / math.sqrt(2.0 * math.pi))
        g = (u * cdf).astype(BF)
        du = (dg_ref[rows].astype(F32) * (cdf + u * pdf)).astype(BF)
        g_ref[rows] = g
        du_ref[rows] = du
        acc_ref[rows] += nt(du, w_up)
    total = tn(g_ref[:half], dy_own[...]) + tn(g_ref[half:], dy_mate[...])
    middle = total.shape[1] // 2
    part = total.shape[0] // 2
    for n, (keep_ref, send_ref) in enumerate(((keep0, send0), (keep1, send1))):
        value = total[:, n * middle : (n + 1) * middle]
        if n == 0:
            low, high = value[:part], value[part:]
        else:
            some = part // 2
            low = jnp.concatenate([value[:some], value[part : part + some]], axis=0)
            high = jnp.concatenate([value[some:part], value[part + some :]], axis=0)
        first = info_ref[info_ref.shape[0] - 2 + n] == 0
        blocked(keep_ref, jnp.where(first, low, high))
        blocked(send_ref, jnp.where(first, high, low))

    @pl.when(step == pl.num_programs(0) - 1)
    def _():
        dh_own[...] = acc_ref[:half]
        dh_mate[...] = acc_ref[half:].astype(BF)


def ffn_call(info, h_own, h_mate, dy_own, dy_mate, dg, w_up, patches):
    half, dim = h_own.shape
    hidden = w_up.shape[1]
    tile, steps = hidden // patches // 2, patches // 2
    at = tile_at(None, steps)
    column = pl.BlockSpec((2 * half, tile), lambda i, info: (0, i))
    return pl.pallas_call(
        ffn_kernel,
        grid_spec=pltpu.PrefetchScalarGridSpec(
            num_scalar_prefetch=1,
            grid=(2 * steps,),
            in_specs=[full((half, dim))] * 4
            + [column, pl.BlockSpec((dim, tile), lambda i, info: (0, at(i, info)))],
            out_specs=[
                column,
                column,
            ]
            + [pl.BlockSpec((dim // 256, tile // 2, 128), lambda i, info: (0, i, 0))] * 4
            + [
                full((half, dim)),
                full((half, dim)),
            ],
            scratch_shapes=[pltpu.VMEM((2 * half, dim), F32)],
        ),
        out_shape=[
            pltpu.HBM((2 * half, hidden // 2), BF),
            pltpu.HBM((2 * half, hidden // 2), BF),
        ]
        + [pltpu.HBM((dim // 256, hidden // 4, 128), BF)] * 4
        + [
            pltpu.HBM((half, dim), F32),
            jax.ShapeDtypeStruct((half, dim), BF),
        ],
        compiler_params=params("arbitrary"),
        cost_estimate=cost(25),
        name="ffn",
    )(info, h_own, h_mate, hbm(dy_own), hbm(dy_mate), hbm(dg), hbm(w_up))


def up_kernel(steps, tile, h_own, h_mate, du_ref, o_own, o_mate, da_own, da_mate, dw_ref):
    half = h_own.shape[0]
    step = pl.program_id(0)
    count = tile // 128

    def put(at, value):
        for n in range(value.shape[1] // 128):
            dw_ref[at + n] = value[:, n * 128 : (n + 1) * 128].astype(BF)

    @pl.when(step < steps)
    def _():
        value = tn(h_own[...], du_ref[:half]) + tn(h_mate[...], du_ref[half:])
        put(step * count, value)

    @pl.when(step == steps)
    def _():
        put(steps * count, tn(o_own[...], da_own[...]) + tn(o_mate[...], da_mate[...]))


def up_call(info, h_own, h_mate, du, o_own, o_mate, da_own, da_mate, patches, piece):
    half, dim = h_own.shape
    columns = du.shape[1] // 2
    steps = patches // 2
    tile = columns // steps
    shape = (columns // 128 + dim // 512, dim, 128)
    quarter = pl.BlockSpec((half, dim // 4), lambda i, info: (0, (info[0] & 1) * 2 + piece))

    def kernel(info_ref, *refs):
        up_kernel(steps, tile, *refs)

    return pl.pallas_call(
        kernel,
        grid_spec=pltpu.PrefetchScalarGridSpec(
            num_scalar_prefetch=1,
            grid=(steps + 1,),
            in_specs=[full((half, dim))] * 2
            + [
                pl.BlockSpec(
                    (2 * half, tile),
                    lambda i, info: (0, piece * steps + jnp.minimum(i, steps - 1)),
                )
            ]
            + [full((half, dim))] * 2
            + [quarter] * 2,
            out_specs=full(shape),
        ),
        out_shape=jax.ShapeDtypeStruct(shape, BF),
        compiler_params=params("arbitrary"),
        cost_estimate=cost(6),
        name="up",
    )(info, hbm(h_own), hbm(h_mate), hbm(du), hbm(o_own), hbm(o_mate), hbm(da_own), hbm(da_mate))


def down_kernel(info_ref, x1_ref, g0_ref, g1_ref, down0_ref, down1_ref, own_ref, mate_ref, acc_ref):
    step = pl.program_id(0)
    half = x1_ref.shape[0]

    @pl.when(step == 0)
    def _():
        acc_ref[:half] = x1_ref[...]
        acc_ref[half:] = jnp.zeros_like(x1_ref)

    for n in range(2):
        rows = slice(n * half, (n + 1) * half)
        acc_ref[rows] += nn(g0_ref[rows], down0_ref[...]) + nn(g1_ref[rows], down1_ref[...])

    @pl.when(step == pl.num_programs(0) - 1)
    def _():
        own_ref[...] = acc_ref[:half]
        mate_ref[...] = acc_ref[half:].astype(BF)


def down_call(info, x1, g, w_down, patches):
    half, dim = x1.shape
    hidden = w_down.shape[0]
    tile, steps = hidden // patches // 2, patches // 2
    first, second = tile_at(0, steps), tile_at(1, steps)
    return pl.pallas_call(
        down_kernel,
        grid_spec=pltpu.PrefetchScalarGridSpec(
            num_scalar_prefetch=1,
            grid=(steps,),
            in_specs=[
                full((half, dim)),
                pl.BlockSpec((2 * half, tile), lambda i, info: (0, i)),
                pl.BlockSpec((2 * half, tile), lambda i, info: (0, steps + i)),
                pl.BlockSpec((tile, dim), lambda i, info: (first(i, info), 0)),
                pl.BlockSpec((tile, dim), lambda i, info: (second(i, info), 0)),
            ],
            out_specs=[full((half, dim)), full((half, dim))],
            scratch_shapes=[pltpu.VMEM((2 * half, dim), F32)],
        ),
        out_shape=[
            pltpu.HBM((half, dim), F32),
            pltpu.HBM((half, dim), BF),
        ],
        compiler_params=params("arbitrary"),
        cost_estimate=cost(8.5),
        name="down",
    )(info, hbm(x1), hbm(g), hbm(g), hbm(w_down), hbm(w_down))


def mid_kernel(
    patches, info_ref, dh_ref, recv_ref, x1_ref, dy_ref, w_ref, gain_ref, dx_ref, da_ref, gs_ref,
    *do_refs,
):
    step = pl.program_id(0)
    fb, width, local = do_refs[0].shape
    hat, rstd = normalise(x1_ref[...])
    dh = dh_ref[...] + recv_ref[...].astype(F32)
    dx = dy_ref[...].astype(F32) + norm_back(dh, hat, rstd, gain_ref[...])
    dx_ref[...] = dx
    da = dx.astype(BF)
    da_ref[...] = da
    sums = jnp.concatenate(
        [jnp.sum(dh * hat, axis=0, keepdims=True), jnp.sum(dh, axis=0, keepdims=True)], axis=0
    )

    @pl.when(step == 0)
    def _():
        gs_ref[...] = sums

    @pl.when(step > 0)
    def _():
        gs_ref[...] += sums

    for j, do_ref in enumerate(do_refs):
        part = nt(da, w_ref[heads_rows(info_ref, j, local), :])
        do_ref[...] = part.astype(BF).reshape(fb, width, local)


def mid_call(info, dh, recv, x1, dy, w_out, gain, frames, patches):
    rows, dim = x1.shape
    width = rows // frames
    local = dim // patches
    fb = frames
    row = pl.BlockSpec((rows, dim), lambda i: (i, 0))
    return pl.pallas_call(
        functools.partial(mid_kernel, patches),
        grid=(1,),
        in_specs=[smem(), row, row, row, row, full(w_out.shape), full(gain.shape)],
        out_specs=[row, row, full((2, dim))]
        + [pl.BlockSpec((fb, width, local), lambda i: (i, 0, 0))] * patches,
        out_shape=[
            pltpu.HBM((rows, dim), F32),
            pltpu.HBM((rows, dim), BF),
            jax.ShapeDtypeStruct((2, dim), F32),
        ]
        + [pltpu.HBM((frames, width, local), BF)] * patches,
        compiler_params=params("arbitrary"),
        cost_estimate=cost(6),
        name="mid",
    )(info, hbm(dh), recv, hbm(x1), hbm(dy), hbm(w_out), gain)


def dwq_kernel(groups, pairs, *refs):
    hs = refs[:groups]
    ds = [refs[groups * (1 + p) : groups * (2 + p)] for p in range(pairs)]
    dw_ref, acc_ref = refs[groups * (1 + pairs) :]
    step = pl.program_id(0)

    @pl.when(step == 0)
    def _():
        acc_ref[...] = jnp.zeros(acc_ref.shape, F32)

    total = None
    for n, h_ref in enumerate(hs):
        fb, rows, dim = h_ref.shape
        d = jnp.concatenate([pair[n][...] for pair in ds], axis=2)
        part = tn(h_ref[...].reshape(fb * rows, dim), d.reshape(fb * rows, -1))
        total = part if total is None else total + part
    acc_ref[...] += total

    @pl.when(step == pl.num_programs(0) - 1)
    def _():
        blocked(dw_ref, acc_ref)


def frame_blocks(a, fb):
    return pl.BlockSpec((fb,) + a.shape[1:], lambda i: (i, 0, 0))


def dwq_call(hs, ds):
    groups, pairs = len(hs), len(ds)
    frames, _, dim = hs[0].shape
    fb = max(1, frames // 2 if frames <= 8 else frames // 8)
    flat = [a for d in ds for a in d]
    return pl.pallas_call(
        functools.partial(dwq_kernel, groups, pairs),
        grid=(frames // fb,),
        in_specs=[frame_blocks(a, fb) for a in (*hs, *flat)],
        out_specs=full((3 * pairs, dim, 128)),
        out_shape=pltpu.HBM((3 * pairs, dim, 128), BF),
        scratch_shapes=[pltpu.VMEM((dim, 384 * pairs), F32)],
        compiler_params=params("arbitrary"),
        cost_estimate=cost(7),
        name="dwq",
    )(*[hbm(a) for a in hs], *flat)


def dh_kernel(groups, pairs, width, *refs):
    ds = [refs[n * groups : (n + 1) * groups] for n in range(pairs)]
    w_ref, even_ref, odd_ref = refs[pairs * groups :]
    j = 0
    for n in range(groups):
        fb, rows, _ = ds[0][n].shape
        d = jnp.concatenate([ds[p][n][...] for p in range(pairs)], axis=2)
        dh = nt(d.reshape(fb * rows, -1), w_ref[...]).astype(BF).reshape(fb, rows, -1)
        for at in range(0, rows, width):
            out = odd_ref if j % 2 else even_ref
            out[j // 2] = dh[:, at : at + width]
            j += 1


def dh_call(ds, w_local, patches):
    pairs, groups = len(ds), len(ds[0])
    frames = ds[0][0].shape[0]
    rows = sum(a.shape[1] for a in ds[0])
    width = rows // patches
    dim = w_local.shape[0]
    fb = max(1, frames // 4 if frames <= 8 else frames // 16)
    shape = (patches // 2, frames, width, dim)
    block = pl.BlockSpec((patches // 2, fb, width, dim), lambda i: (0, i, 0, 0))
    return pl.pallas_call(
        functools.partial(dh_kernel, groups, pairs, width),
        grid=(frames // fb,),
        in_specs=[frame_blocks(a, fb) for d in ds for a in d] + [full(w_local.shape)],
        out_specs=[block, block],
        out_shape=[pltpu.HBM(shape, BF)] * 2,
        compiler_params=params("arbitrary"),
        cost_estimate=cost(5),
        name="dh",
    )(*[a for d in ds for a in d], w_local)


def last_kernel(a_ref, b_ref, x_ref, dx_ref, gain_ref, gt_ref, gs_ref):
    step = pl.program_id(0)
    hat, rstd = normalise(x_ref[...].astype(F32))
    dh = a_ref[...].astype(F32) + b_ref[...].astype(F32)
    gt_ref[...] = (dx_ref[...] + norm_back(dh, hat, rstd, gain_ref[...])).astype(BF)
    sums = jnp.concatenate(
        [jnp.sum(dh * hat, axis=0, keepdims=True), jnp.sum(dh, axis=0, keepdims=True)], axis=0
    )

    @pl.when(step == 0)
    def _():
        gs_ref[...] = sums

    @pl.when(step > 0)
    def _():
        gs_ref[...] += sums


def last_call(a, b, x, dx, gain):
    rows, dim = x.shape
    row = pl.BlockSpec((rows // 2, dim), lambda i: (i, 0))
    return pl.pallas_call(
        last_kernel,
        grid=(2,),
        in_specs=[row, row, row, row, full(gain.shape)],
        out_specs=[row, full((2, dim))],
        out_shape=[
            jax.ShapeDtypeStruct((rows, dim), BF),
            jax.ShapeDtypeStruct((2, dim), F32),
        ],
        compiler_params=params("arbitrary"),
        cost_estimate=cost(3),
        name="last",
    )(a, b, hbm(x), hbm(dx), gain)


class Chain:
    def __init__(self, hops):
        self.hops, self.value, self.got, self.begun, self.done = hops, None, None, False, False
        self.move = None

    def request(self):
        try:
            return self.hops.send(self.got) if self.begun else next(self.hops)
        except StopIteration as stop:
            self.value, self.done = stop.value, True
            return None
        finally:
            self.begun = True


class Move:
    def __init__(self, bit, members, got):
        self.bit, self.members, self.got = bit, members, got

    def settle(self, got):
        start = 0
        for chain, a in self.members:
            chain.move = None
            if len(self.members) == 1:
                chain.got = got
            elif self.bit == "patch":
                chain.got = got[start : start + a.shape[0]]
                start += a.shape[0]
            else:
                n = a.size // 128
                chain.got = got[start : start + n].reshape(a.shape)
                start += n


class Stage:
    def __init__(self, links):
        self.links = links

    def start(self, *chains):
        wanted = {}
        for chain in chains:
            if chain.done or chain.move is not None:
                continue
            request = chain.request()
            if request is not None:
                wanted.setdefault(request[0], []).append((chain, request[1]))
        for bit, members in wanted.items():
            arrays = [a for _, a in members]
            if bit == "patch":
                sent = arrays[0] if len(arrays) == 1 else jnp.concatenate(arrays, axis=0)
                got = lax.all_to_all(sent, "patch", 1, 1, tiled=True)
            elif len(arrays) == 1:
                got = self.links.swap(arrays[0], bit)
            else:
                sent = jnp.concatenate([a.reshape(-1, 128) for a in arrays], axis=0)
                got = self.links.swap(sent, bit)
            move = Move(bit, members, got)
            for chain, _ in members:
                chain.move = move

    def join(self, values, *chains):
        moves = []
        for chain in chains:
            if chain.move is not None and chain.move not in moves:
                moves.append(chain.move)
        held, values = lax.optimization_barrier(([m.got for m in moves], values))
        for move, got in zip(moves, held):
            move.settle(got)
        return values


class Links:
    def __init__(self, batches, patches):
        self.batches, self.patches = batches, patches
        self.patch = lax.axis_index("patch")
        self.batch = lax.axis_index("batch")
        self.bits = {"c": [("p", 1)], "y": [("b", 1)], "x": [], "z": []}
        bit = 2
        while bit < patches:
            self.bits["x"].append(("p", bit))
            bit *= 2
        bit = 2
        while bit < batches:
            self.bits["z"].append(("b", bit))
            bit *= 2

    def swap(self, a, bit):
        axis, step = bit
        step = step if axis == "p" else step * self.patches
        n = self.batches * self.patches
        return lax.ppermute(a, AXES, [(i, i ^ step) for i in range(n)])

    def swap_patch(self, a, bit):
        return self.swap(a, ("p", bit))

    def mine(self, bit):
        axis, step = bit
        return ((self.patch if axis == "p" else self.batch) // step) & 1

    def expand(self, order):
        if not isinstance(order, str):
            return order
        bits = []
        for axis in order:
            one = self.bits[axis.lower()]
            bits += one if axis.islower() else one[::-1]
        return bits

    def hops(self, a, axes, order, back, trade, layout, first, raw):
        if first is not None:
            got = yield first
            a = (a.astype(F32) + got.astype(F32)).astype(BF)
        names = list(self.expand(axes))
        blocks, rows, _ = a.shape
        a = a.reshape((blocks,) + (2,) * len(names) + (rows // 2 ** len(names), 128))
        layout = self.expand(layout)
        for bit in self.expand(order):
            at = names.index(bit) + 1
            names.pop(at - 1)
            got = yield bit, lax.dynamic_index_in_dim(a, 1 - self.mine(bit), at, keepdims=False)
            keep = lax.dynamic_index_in_dim(a, self.mine(bit), at, keepdims=False)
            a = (keep.astype(F32) + got.astype(F32)).astype(BF)
        if trade is not None and trade != "patch":
            bit = ("p", 1)
            size = a.shape[1:]
            pairs = a[:trade].reshape((trade // 2, 2) + size)
            got = yield bit, lax.dynamic_index_in_dim(pairs, 1 - self.mine(bit), 1, keepdims=False)
            own = lax.dynamic_index_in_dim(pairs, self.mine(bit), 1, keepdims=False)
            a = jnp.concatenate([self.join(own, got, bit, 0).reshape((trade,) + size), a[trade:]])
        if trade == "patch":
            a = a.reshape((blocks, self.patches) + a.shape[-2:])
            a = yield "patch", a
            a = a.reshape((blocks * self.patches,) + a.shape[-2:])
        have = []
        for bit in self.expand(back):
            got = yield bit, a
            at = 1 + sum(layout.index(other) < layout.index(bit) for other in have)
            have.append(bit)
            if raw and len(have) == len(self.expand(back)):
                return a, got
            a = self.join(a, got, bit, at)
        return a.reshape(a.shape[0], -1, 128)

    def join(self, a, got, bit, at):
        return jnp.where(
            self.mine(bit) == 0, jnp.stack([a, got], axis=at), jnp.stack([got, a], axis=at)
        )

    def chain(self, a, axes, order, back, trade=None, layout="yz", first=None, raw=False):
        return Chain(self.hops(a, axes, order, back, trade, layout, first, raw))

    def apart(self, a):
        got = {0: a}
        bit = self.patches // 2
        while bit > 1:
            for j in sorted(got):
                got[j | bit] = self.swap_patch(got[j], bit)
            bit //= 2
        return got

    def items(self, a):
        got = self.apart(a)
        for j in sorted(got):
            got[j | 1] = self.swap_patch(got[j], 1)
        return got

    def deal(self, parts):
        return [parts[0]] + [self.swap_patch(parts[j], j) for j in range(1, self.patches)]


def assemble_q_kernel(order, valid, info_ref, mine_ref, got_ref, out):
    own = info_ref[info_ref.shape[0] - 2] == pl.program_id(0)
    pieces = [jnp.where(own, mine_ref[b], got_ref[b])[:, :valid].astype(F32) for b in order]
    out[...] = jnp.concatenate(pieces, axis=1)


def assemble_q(info, pair, order, valid):
    mine, got = (a.reshape(a.shape[0], -1, 128) for a in pair)
    blocks, rows, _ = mine.shape
    return pl.pallas_call(
        functools.partial(assemble_q_kernel, order, valid),
        grid=(2,),
        in_specs=[smem()] + [full(mine.shape)] * 2,
        out_specs=pl.BlockSpec((rows, len(order) * valid), lambda i: (i, 0)),
        out_shape=jax.ShapeDtypeStruct((2 * rows, len(order) * valid), F32),
        compiler_params=params("arbitrary"),
        cost_estimate=cost(2),
        name="assemble_q",
    )(info, mine, got)


def assemble_w_kernel(ups, wos, info_ref, *refs):
    up_ref, wo_ref = refs[4:]
    count = info_ref.shape[0]
    y, z = pl.program_id(0) // 2, pl.program_id(0) % 2
    own_y = info_ref[count - 2] == y
    own_z = info_ref[count - 1] == z

    def block(n, b):
        if n == 0:
            return jnp.where(own_z, refs[0][b, y], refs[1][b, y]).astype(F32)
        return jnp.where(own_y, refs[2][b, z], refs[3][b, z]).astype(F32)

    for ref, order in ((up_ref, ups), (wo_ref, wos)):
        for at, (n, b) in enumerate(order):
            ref[:, at * 128 : (at + 1) * 128] = block(n, b)


def assemble_w(info, first, second, ups, wos):
    arrays = [a.reshape(a.shape[0], 2, -1, 128) for a in (*first, *second)]
    rows = arrays[0].shape[2]
    return pl.pallas_call(
        functools.partial(assemble_w_kernel, ups, wos),
        grid=(4,),
        in_specs=[smem()] + [full(a.shape) for a in arrays],
        out_specs=[
            pl.BlockSpec((rows, len(order) * 128), lambda i: (i, 0)) for order in (ups, wos)
        ],
        out_shape=[
            jax.ShapeDtypeStruct((4 * rows, len(order) * 128), F32) for order in (ups, wos)
        ],
        compiler_params=params("arbitrary"),
        cost_estimate=cost(3),
        name="assemble_w",
    )(info, *arrays)


def pieces_kernel(steps, a_ref, out):
    piece = pl.program_id(0) // steps
    blocks = a_ref.shape[0] // 2

    def put(n):
        for b in range(blocks):
            out[:, b * 128 : (b + 1) * 128] = a_ref[2 * b + n].astype(F32)

    for n in range(2):
        pl.when(piece == n)(functools.partial(put, n))


def pieces_call(a):
    blocks, rows, _ = a.shape
    step = min(rows, 128)
    steps = rows // step
    return pl.pallas_call(
        functools.partial(pieces_kernel, steps),
        grid=(2 * steps,),
        in_specs=[pl.BlockSpec((blocks, step, 128), lambda i: (0, i % steps, 0))],
        out_specs=pl.BlockSpec((step, blocks * 64), lambda i: (i, 0)),
        out_shape=jax.ShapeDtypeStruct((2 * rows, blocks * 64), F32),
        compiler_params=params("arbitrary"),
        cost_estimate=cost(4),
        name="pieces",
    )(a)


def tables(code, times):
    head = 64
    half = head // 6
    band = 2 * half
    dims = jnp.arange(head)
    freq = jnp.power(THETA, -2.0 * (dims % half).astype(F32) / band)
    places = jnp.stack([times, (code // GRID).astype(F32), (code % GRID).astype(F32)], axis=-1)
    which = jnp.minimum(dims // band, 2)
    pick = jnp.where(
        which == 0, places[..., 0:1], jnp.where(which == 1, places[..., 1:2], places[..., 2:3])
    )
    angle = pick * freq
    turned = dims < 3 * band
    cos = jnp.where(turned, jnp.cos(angle), 1.0)
    sin = jnp.where(turned, jnp.sin(angle) * jnp.where(dims % band < half, -1.0, 1.0), 0.0)
    return jnp.concatenate([cos, cos, sin, sin], axis=-1)


def per_device(
    batches, patches, tokens, cotangent, episode_frames, kinds, patch_pos,
    ln1_gain, ln1_shift, w_qkv, w_out, ln2_gain, ln2_shift, w_up, w_down,
):
    tokens = tokens[0]
    frames, width, dim = tokens.shape
    rows = frames * width
    local = dim // patches
    links = Links(batches, patches)
    me = links.patch
    core = me & 1
    gain1, shift1, gain2, shift2 = (
        a.astype(F32).reshape(1, dim) for a in (ln1_gain, ln1_shift, ln2_gain, ln2_shift)
    )
    dy = cotangent.reshape(rows, dim)

    code = jnp.where(kinds[0] == 0, patch_pos[0], 0)
    codes = links.items(code)
    mate = links.swap_patch(tokens, 1)
    dy_mate = links.swap_patch(dy, 1)
    apart = links.apart(tokens)
    ends = jnp.cumsum(episode_frames[0])
    frame_ids = jnp.arange(frames, dtype=jnp.int32)
    starts = jnp.max(
        jnp.where(ends[None, :] <= frame_ids[:, None], ends[None, :], 0), axis=1
    )
    firsts = [links.mine(bits[0])[None] for bits in (links.bits["y"], links.bits["z"])]
    info = jnp.concatenate([me[None], starts, *firsts]).astype(jnp.int32)
    pad = max(128, local)
    pairs = pad // 128
    valid = min(128, local)
    if valid == 128:
        w_local = columns_call(info, w_qkv, pairs)
    else:
        columns = []
        for n in range(3):
            at = n * dim + me * local
            columns.append(lax.dynamic_slice(w_qkv, (jnp.int32(0), at), (dim, valid)))
            columns.append(jnp.zeros((dim, 128 - valid), BF))
        w_local = jnp.concatenate(columns, axis=1)

    members = [[0, 1], list(range(2, patches))]
    css = []
    for group in members:
        place = jnp.concatenate([codes[j] for j in group], axis=1)
        times = jnp.broadcast_to(frame_ids.astype(F32)[:, None], place.shape)
        css.append(tables(place, times))
    near = qkv_call([tokens, mate], css[0], w_local, gain1, shift1)
    dg = pre_call(info, dy, dy_mate, w_down, patches)
    near, dg, apart, css = lax.optimization_barrier((near, dg, apart, css))
    far_items = []
    for j in range(2, patches, 2):
        far_items += [apart[j], links.swap_patch(apart[j], 1)]
    far = qkv_call(far_items, css[1], w_local, gain1, shift1)
    hs, qkvs = [near[0], far[0]], [near[1], far[1]]

    *o_send, o_full, lse = attend_call(info, qkvs, patches)
    o_in = links.deal([a[..., :local] for a in o_send])
    x1, h2, o_own = project_call(info, o_in, tokens, w_out, gain2, shift2)
    h2_mate = links.swap_patch(h2, 1)
    o_mate = links.swap_patch(o_own, 1)
    stage = Stage(links)
    g, du, keep0, send0, keep1, send1, dh_own, dh_mate = ffn_call(
        info, h2, h2_mate, dy, dy_mate, dg, w_up, patches
    )
    inner, outer = links.bits["z"][:1], links.bits["z"][1:]
    ys, xs = links.bits["y"], links.bits["x"]

    def two_pieces(a):
        return a.reshape(a.shape[0] * 2, a.shape[1] // 2, 128)

    def step(held, *chains):
        held = stage.join(held, *chains)
        for chain in chains:
            stage.start(chain)
        return held

    def finish(held, *chains):
        while not all(c.done for c in chains):
            held = step(held, *chains)
        return held

    d1 = links.chain(two_pieces(keep0), xs[::-1] + inner + outer, inner, "", first=(ys[0], two_pieces(send0)))
    d2 = links.chain(two_pieces(keep1), xs[::-1] + ys + outer, ys, "", first=(inner[0], two_pieces(send1)))
    stage.start(d1)
    stage.start(d2)
    dh_recv = links.swap_patch(dh_mate, 1)
    dx1, da, sums2, *d_o = mid_call(
        info, dh_own, dh_recv, x1, dy, w_out, gain2, frames, patches
    )
    da_mate = links.swap_patch(da, 1)
    do_in = links.deal(d_o)
    sides = (o_own, o_mate, da, da_mate)
    dw1 = up_call(info, h2, h2_mate, du, *sides, patches, 0)
    dw2 = up_call(info, h2, h2_mate, du, *sides, patches, 1)
    out_own, out_mate = down_call(info, x1, g, w_down, patches)
    do_in, dw1, dw2, out_own, out_mate = step((do_in, dw1, dw2, out_own, out_mate), d1, d2)
    out_recv = links.swap_patch(out_mate, 1)
    u1 = links.chain(dw1, "Xcyz", xs + inner + ys, "")
    u2 = links.chain(dw2, "Xcyz", ys + xs + inner, "")
    stage.start(u1)
    if pad > local:
        do_in = [jnp.pad(a, ((0, 0), (0, 0), (0, pad - local))) for a in do_in]
    dqkv = attend_back_call(info, qkvs, css, do_in, o_full, lse, patches, 0)
    dqkv, do_in = step((dqkv, do_in), d1, d2)
    dqkv = finish(dqkv, d1, d2)
    dqkvs = [dqkv]
    d = links.chain(
        jnp.concatenate([d1.value, d2.value], axis=0),
        xs[::-1] + outer,
        outer + xs,
        outer[::-1] + inner + ys,
    )
    stage.start(d)
    stage.start(u2)
    for pair in range(1, pairs):
        dqkvs.append(attend_back_call(info, qkvs, css, do_in, o_full, lse, patches, pair))
    dwq = dwq_call(hs, dqkvs)
    even, odd = dh_call(dqkvs, w_local, patches)
    odd, even, dwq = stage.join((odd, even, dwq), u1, d, u2)
    q = links.chain(dwq, "Xcyz", "yz", "zy", "patch", raw=True)
    for chain in (q, u1, d, u2):
        stage.start(chain)
    odd = links.swap_patch(odd, 1)
    odd, even, sums2 = step((odd, even, sums2), u1)
    slots = (even.astype(F32) + odd.astype(F32)).astype(BF)
    bit = patches // 2
    while bit > 2:
        n = slots.shape[0] // 2
        slots = (slots[:n].astype(F32) + links.swap_patch(slots[n:], bit).astype(F32)).astype(BF)
        bit //= 2
    got = links.swap_patch(slots[1], 2)
    sums2 = step(sums2, q)
    sums2 = step(sums2, u2, d)
    sums2 = step(sums2, u1, u2)
    sums2 = finish(sums2, u1, u2)
    w = jnp.concatenate([u1.value, u2.value], axis=0)
    w = w.reshape(2 * w.shape[0], -1, 128)
    w = links.chain(w, outer, outer, outer[::-1], w.shape[0])
    stage.start(w)
    sums2 = step(sums2, q)
    sums2 = step(sums2, d)
    sums2 = step(sums2, w)
    slots, got, sums2 = step((slots, got, sums2), q)
    sums2 = step(sums2, w)
    sums2 = step(sums2, d)
    grad_tokens, sums1 = last_call(
        slots[0].reshape(rows, dim), got.reshape(rows, dim), tokens.reshape(rows, dim), dx1, gain1
    )
    sums = jnp.concatenate([sums1, sums2], axis=0)
    sums = step(sums, q)
    sums = step(sums, w)
    sums = finish(sums, w)
    half = w.value.shape[0] // 2
    wa = links.chain(w.value[:half], [], [], ys + inner, raw=True)
    wb = links.chain(w.value[half:], [], [], inner + ys, raw=True)
    stage.start(wa)
    stage.start(wb)
    sums, out_own, out_recv = step((sums, out_own, out_recv), q)
    out = (out_own + out_recv.astype(F32)).astype(BF)
    sums = sums.reshape(4, patches, local).transpose(1, 0, 2)
    sums = jnp.broadcast_to(sums[None], (batches,) + sums.shape)
    sums = lax.all_to_all(sums.reshape((-1,) + sums.shape[2:]), AXES, 0, 0, tiled=True)
    held = step(grad_tokens, wa, wb)
    held = step(held, q)
    held = step(held, d)
    held, sums = step((held, sums), wa, wb)
    grad_tokens = step(held, q)
    sums = jnp.sum(sums, axis=0)
    grad_tokens = finish(grad_tokens, wa, wb)
    grad_tokens = finish(grad_tokens, q)
    grad_tokens = finish(grad_tokens, d)
    down = pieces_call(d.value)

    nx = patches // 2
    each = dw1.shape[0]
    per = (each - dim // 512) // nx
    ups, wos = [], []
    for owner in range(2):
        for n in range(2):
            wos += [(owner, n * each + nx * per + t) for t in range(dim // 512)]
    for i in range(nx):
        for owner in range(2):
            for n in range(2):
                ups += [(owner, n * each + i * per + t) for t in range(per)]
    up, grad_wo = assemble_w(info, wa.value, wb.value, ups, wos)
    order = []
    for n in range(3):
        for p in range(patches):
            order += [(pair * 3 + n) * patches + p for pair in range(pairs)]
    qkv = assemble_q(info, q.value, order, valid)

    return (
        out.reshape(1, frames, width, dim),
        grad_tokens.reshape(1, frames, width, dim),
        sums[0],
        sums[1],
        qkv,
        grad_wo,
        sums[2],
        sums[3],
        up,
        down,
    )


def solution(mesh):
    placed = (
        P("batch", None, "patch", None),
        P("batch", None, "patch", None),
        P("batch", None),
        P("batch", None, "patch"),
        P("batch", None, "patch"),
    ) + (P(),) * 8
    return jax.shard_map(
        functools.partial(per_device, mesh.shape["batch"], mesh.shape["patch"]),
        mesh=mesh,
        in_specs=placed,
        out_specs=(
            P("batch", None, "patch", None),
            P("batch", None, "patch", None),
            P("patch"),
            P("patch"),
            P("patch", None),
            P("patch", None),
            P("patch"),
            P("patch"),
            P("patch", None),
            P("patch", None),
        ),
        check_vma=False,
    )
```

```python
import functools
import math

import jax
import jax.numpy as jnp
from jax import lax
from jax.experimental import pallas as pl
from jax.experimental.pallas import tpu as pltpu
from jax.sharding import PartitionSpec as P

GRID = 16
EPS = 1e-06
THETA = 10000.0
MASKED = -1e30
LIMIT = 40 * 1024 * 1024
BF = jnp.bfloat16
F32 = jnp.float32
AXES = ("batch", "patch")


def nn(a, b):
    return lax.dot_general(a, b, (((1,), (0,)), ((), ())), preferred_element_type=F32)


def nt(a, b):
    return lax.dot_general(a, b, (((1,), (1,)), ((), ())), preferred_element_type=F32)


def tn(a, b):
    return lax.dot_general(a, b, (((0,), (0,)), ((), ())), preferred_element_type=F32)


def params(*semantics):
    return pltpu.CompilerParams(
        dimension_semantics=semantics, vmem_limit_bytes=LIMIT
    )


def cost(micros):
    return pl.CostEstimate(flops=int(micros * 5e+08), bytes_accessed=1, transcendentals=0)


def full(shape, memory=None):
    zeros = (0,) * len(shape)
    return pl.BlockSpec(shape, lambda *_: zeros)


def blocked(ref, value):
    for n in range(ref.shape[0]):
        ref[n] = value[:, n * 128 : (n + 1) * 128].astype(BF)


def hbm(a):
    return pltpu.with_memory_space_constraint(a, pltpu.HBM)


def smem():
    return pl.BlockSpec(memory_space=pltpu.SMEM)


def normalise(x):
    mean = jnp.mean(x, axis=-1, keepdims=True)
    centred = x - mean
    spread = jnp.mean(centred * centred, axis=-1, keepdims=True)
    rstd = lax.rsqrt(spread + EPS)
    return centred * rstd, rstd


def norm_back(d_h, hat, rstd, gain):
    d_hat = d_h * gain
    first = jnp.mean(d_hat, axis=-1, keepdims=True)
    second = jnp.mean(d_hat * hat, axis=-1, keepdims=True)
    return rstd * (d_hat - first - hat * second)


def partner(value):
    head = 64
    half = head // 6
    width = value.shape[1]
    ahead = jnp.concatenate([value[:, half:], value[:, :half]], axis=1)
    behind = jnp.concatenate([value[:, width - half :], value[:, : width - half]], axis=1)
    lane = lax.broadcasted_iota(jnp.int32, value.shape, 1) % head
    return jnp.where(lane % (2 * half) < half, ahead, behind)


def columns_kernel(info_ref, w_ref, out_ref):
    out_ref[...] = w_ref[...]


def columns_call(info, w_qkv, pairs):
    dim = w_qkv.shape[0]
    blocks = dim // 128

    def at(i, info):
        return (0, (i % 3) * blocks + info[0] * pairs + i // 3)

    return pl.pallas_call(
        columns_kernel,
        grid_spec=pltpu.PrefetchScalarGridSpec(
            num_scalar_prefetch=1,
            grid=(3 * pairs,),
            in_specs=[pl.BlockSpec((dim, 128), at)],
            out_specs=pl.BlockSpec((dim, 128), lambda i, info: (0, i)),
        ),
        out_shape=jax.ShapeDtypeStruct((dim, 384 * pairs), BF),
        compiler_params=params("arbitrary"),
        cost_estimate=cost(2),
        name="columns",
    )(info, hbm(w_qkv))


def qkv_kernel(count, local, *refs):
    tok = refs[:count]
    cs_ref, w_ref, gain_ref, shift_ref = refs[count : count + 4]
    h_ref, qkv_ref = refs[count + 4 :]
    x = jnp.concatenate([t[...] for t in tok], axis=1)
    fb, rows, dim = x.shape
    x = x.reshape(fb * rows, dim).astype(F32)
    hat, _ = normalise(x)
    h = (hat * gain_ref[...] + shift_ref[...]).astype(BF)
    h_ref[...] = h.reshape(fb, rows, dim)
    y = nn(h, w_ref[...])
    cs = cs_ref[...].reshape(fb * rows, 256)
    cos = cs[:, :128]
    sin = cs[:, 128:]
    for at in range(0, 3 * local, 384):
        q = y[:, at : at + 128]
        k = y[:, at + 128 : at + 256]
        q = (q * cos + partner(q) * sin).astype(BF) * BF(0.125)
        k = (k * cos + partner(k) * sin).astype(BF)
        v = y[:, at + 256 : at + 384].astype(BF)
        qkv_ref[:, :, at : at + 128] = q.reshape(fb, rows, 128)
        qkv_ref[:, :, at + 128 : at + 256] = k.reshape(fb, rows, 128)
        qkv_ref[:, :, at + 256 : at + 384] = v.reshape(fb, rows, 128)


def qkv_call(items, cs, w_local, gain, shift):
    count = len(items)
    frames, width, dim = items[0].shape
    local = w_local.shape[1] // 3
    rows = count * width
    fb = max(1, min(frames, 512 // rows))
    while frames % fb:
        fb -= 1
    shapes = [
        pltpu.HBM((frames, rows, dim), BF),
        pltpu.HBM((frames, rows, 3 * local), BF),
    ]
    return pl.pallas_call(
        functools.partial(qkv_kernel, count, local),
        grid=(frames // fb,),
        in_specs=[pl.BlockSpec((fb, width, dim), lambda i: (i, 0, 0))] * count
        + [
            pl.BlockSpec((fb, rows, 256), lambda i: (i, 0, 0)),
            full(w_local.shape),
            full(gain.shape),
            full(shift.shape),
        ],
        out_specs=[
            pl.BlockSpec((fb, rows, dim), lambda i: (i, 0, 0)),
            pl.BlockSpec((fb, rows, 3 * local), lambda i: (i, 0, 0)),
        ],
        out_shape=shapes,
        compiler_params=params("arbitrary"),
        cost_estimate=cost(5.5),
        name="qkv",
    )(*items, cs, w_local, gain, shift)


def lane_halves(shape):
    lane = lax.broadcasted_iota(jnp.int32, shape, 1)
    return lane < 64


def attend_kernel(groups, local, patches, most, info_ref, *refs):
    ins = refs[:groups]
    o_refs = refs[groups : groups + patches]
    of_ref, lse_ref = refs[groups + patches :]
    f = pl.program_id(0)
    begin = info_ref[1 + f]
    rows = sum(r.shape[1] for r in ins)
    low = lane_halves((rows, 128))
    one = jnp.ones((rows, 128), BF)
    zero = jnp.zeros((rows, 128), BF)
    lane = lax.broadcasted_iota(jnp.int32, (rows, 128), 1)

    def part_of(g, pair, n):
        at = pair * 384 + n * 128
        return jnp.concatenate([r[g, :, at : at + 128] for r in ins], axis=0)

    def finish(pair, tops, accs, lses):
        num = jnp.where(low, accs[0], accs[1])
        den = pltpu.roll(jnp.where(low, accs[1], accs[0]), 64, 1)
        of_ref[0, :, pair * 128 : (pair + 1) * 128] = num / den
        logs = jnp.log(jnp.where(low, accs[1], accs[0]))
        lses = jnp.where(lane == 2 * pair + 64, tops[0] + logs, lses)
        return jnp.where(lane == 2 * pair + 1, tops[1] + logs, lses)

    def store(lses):
        even = lane % 2 == 0
        lses = jnp.where(even, pltpu.roll(lses, 64, 1), lses)
        lse_ref[0] = lses.T[:8]

    def whole(count):
        lses = jnp.zeros((rows, 128), F32)
        for pair in range(local // 128):
            q = part_of(f, pair, 0)
            tops, accs = [], []
            for h in range(2):
                qm = jnp.where(low == (h == 0), q, zero)
                scores = [nt(qm, part_of(begin + n, pair, 1)) for n in range(count)]
                top = scores[0]
                for s in scores[1:]:
                    top = jnp.maximum(top, s)
                top = jnp.max(top, axis=1, keepdims=True)
                acc = None
                for n, s in enumerate(scores):
                    v = jnp.where(low == (h == 0), part_of(begin + n, pair, 2), one)
                    part = nn(jnp.exp(s - top).astype(BF), v)
                    acc = part if acc is None else acc + part
                tops.append(top)
                accs.append(acc)
            lses = finish(pair, tops, accs, lses)
        store(lses)

    if most <= 4:
        for count in range(1, most + 1):
            pl.when(f + 1 - begin == count)(functools.partial(whole, count))
    else:
        lses = jnp.zeros((rows, 128), F32)
        for pair in range(local // 128):
            q = part_of(f, pair, 0)

            def body(g, state, pair=pair, q=q):
                new = []
                for h in range(2):
                    top, acc = state[2 * h : 2 * h + 2]
                    qm = jnp.where(low == (h == 0), q, zero)
                    s = nt(qm, part_of(g, pair, 1))
                    new_top = jnp.maximum(top, jnp.max(s, axis=1, keepdims=True))
                    v = jnp.where(low == (h == 0), part_of(g, pair, 2), one)
                    p = jnp.exp(s - new_top).astype(BF)
                    new += [new_top, acc * jnp.exp(top - new_top) + nn(p, v)]
                return tuple(new)

            blank = (jnp.full((rows, 1), MASKED, F32), jnp.zeros((rows, 128), F32))
            state = lax.fori_loop(begin, f + 1, body, blank + blank)
            lses = finish(pair, state[0::2], state[1::2], lses)
        store(lses)

    o = of_ref[0].astype(BF)
    width = rows // patches
    for j in range(patches):
        o_refs[j][0] = o[j * width : (j + 1) * width]


def attend_call(info, qkv, patches):
    groups = len(qkv)
    frames = qkv[0].shape[0]
    local = qkv[0].shape[2] // 3
    rows = sum(a.shape[1] for a in qkv)
    width = rows // patches
    shapes = [jax.ShapeDtypeStruct((frames, width, local), BF)] * patches
    sizes = [(frames, width, local)] * patches + [(frames, rows, local), (frames, 8, rows)]
    shapes += [pltpu.HBM((frames, rows, local), F32), pltpu.HBM((frames, 8, rows), F32)]
    return pl.pallas_call(
        functools.partial(attend_kernel, groups, local, patches, frames // 2),
        grid=(frames,),
        in_specs=[smem()] + [full(a.shape) for a in qkv],
        out_specs=[pl.BlockSpec((1,) + s[1:], lambda i: (i, 0, 0)) for s in sizes],
        out_shape=shapes,
        compiler_params=params("arbitrary"),
        cost_estimate=cost(12.5),
        name="attend",
    )(info, *[hbm(a) for a in qkv])


def attend_back_kernel(groups, pair, patches, info_ref, *refs):
    ins = refs[:groups]
    css = refs[groups : 2 * groups]
    do_refs = refs[2 * groups : 2 * groups + patches]
    refs = refs[2 * groups + patches :]
    of_ref, lse_ref = refs[:2]
    outs = refs[2 : groups + 2]
    dk_ref, dv_ref, dq_ref, kt_ref = refs[groups + 2 :]
    f = pl.program_id(0)
    frames = pl.num_programs(0)
    begin = info_ref[1 + f]

    def part_of(g, n):
        return jnp.concatenate([r[g, :, n * 128 : (n + 1) * 128] for r in ins], axis=0)

    q = part_of(f, 0)
    d_o = jnp.concatenate([r[0] for r in do_refs], axis=0)
    rows = q.shape[0]
    low = lane_halves((rows, 128))
    zero = jnp.zeros((rows, 128), BF)
    turned = (d_o.astype(F32) * of_ref[0]).T
    delta = [jnp.sum(turned[h * 64 : (h + 1) * 64], axis=0, keepdims=True) for h in range(2)]
    lse = lse_ref[0, 2 * pair : 2 * pair + 2]
    dk_ref[f] = jnp.zeros((rows, 128), F32)
    dv_ref[f] = jnp.zeros((rows, 128), F32)
    dq_ref[...] = jnp.zeros((128, rows), F32)
    kt_ref[f] = part_of(f, 1).T
    qm = [jnp.where(low == (h == 0), q, zero) for h in range(2)]
    dom = [jnp.where(low == (h == 0), d_o, zero) for h in range(2)]

    @pl.loop(begin, f + 1)
    def _(g):
        k = part_of(g, 1)
        v = part_of(g, 2)
        scores = [nt(k, qm[h]) for h in range(2)]
        dps = [nt(v, dom[h]) for h in range(2)]
        dk = dv = None
        for h in range(2):
            p = jnp.exp(scores[h] - lse[h : h + 1])
            ds = (p * (dps[h] - delta[h])).astype(BF)
            dq_ref[h * 64 : (h + 1) * 64] += nn(kt_ref[g, h * 64 : (h + 1) * 64], ds)
            part_k = nn(ds, qm[h])
            part_v = nn(p.astype(BF), dom[h])
            dk = part_k if dk is None else dk + part_k
            dv = part_v if dv is None else dv + part_v
        dk_ref[g] += dk
        dv_ref[g] += dv

    def turn_back(t, value):
        cs = jnp.concatenate([r[t] for r in css], axis=0)
        return (value * cs[:, :128] - partner(value) * cs[:, 128:]).astype(BF)

    def put(t, n, value):
        start = 0
        for out in outs:
            count = out.shape[1]
            out[t, :, n * 128 : (n + 1) * 128] = value[start : start + count]
            start += count

    put(f, 0, turn_back(f, dq_ref[...].T * 0.125))

    @pl.when(f == frames - 1)
    def _():
        @pl.loop(0, frames)
        def _(t):
            put(t, 1, turn_back(t, dk_ref[t]))
            put(t, 2, dv_ref[t].astype(BF))


def attend_back_call(info, qkv, cs, d_o, o_full, lse, patches, pair):
    groups = len(qkv)
    frames = qkv[0].shape[0]
    rows = sum(a.shape[1] for a in qkv)
    width = rows // patches
    shapes = [jax.ShapeDtypeStruct((frames, a.shape[1], 384), BF) for a in qkv]
    return pl.pallas_call(
        functools.partial(attend_back_kernel, groups, pair, patches),
        grid=(frames,),
        in_specs=[smem()]
        + [pl.BlockSpec(a.shape[:2] + (384,), lambda i: (0, 0, pair)) for a in qkv]
        + [full(a.shape) for a in cs]
        + [pl.BlockSpec((1, width, 128), lambda i: (i, 0, pair))] * patches
        + [
            pl.BlockSpec((1, rows, 128), lambda i: (i, 0, pair)),
            pl.BlockSpec((1, 8, rows), lambda i: (i, 0, 0)),
        ],
        out_specs=[full(s.shape) for s in shapes],
        out_shape=shapes,
        scratch_shapes=[
            pltpu.VMEM((frames, rows, 128), F32),
            pltpu.VMEM((frames, rows, 128), F32),
            pltpu.VMEM((128, rows), F32),
            pltpu.VMEM((frames, 128, rows), BF),
        ],
        compiler_params=params("arbitrary"),
        cost_estimate=cost(15),
        name="attend_back",
    )(info, *[hbm(a) for a in (*qkv, *cs)], *d_o, hbm(o_full), hbm(lse))


def heads_rows(info_ref, j, local):
    return pl.ds(pl.multiple_of((info_ref[0] ^ j) * local, local), local)


def project_kernel(patches, info_ref, *refs):
    o_refs = refs[:patches]
    x_ref, w_ref, gain_ref, shift_ref, x1_ref, h_ref, o_ref, kept_ref = refs[patches:]
    fb, width, local = o_refs[0].shape
    rows = fb * width
    for j, ref in enumerate(o_refs):
        kept_ref[j] = ref[...].reshape(rows, local)
    o = jnp.concatenate([kept_ref[info_ref[0] ^ p] for p in range(patches)], axis=1)
    o_ref[...] = o
    acc = x_ref[...].astype(F32).reshape(rows, -1) + nn(o, w_ref[...])
    x1_ref[...] = acc
    hat, _ = normalise(acc)
    h_ref[...] = (hat * gain_ref[...] + shift_ref[...]).astype(BF)


def project_call(info, o_in, tokens, w_out, gain, shift):
    patches = len(o_in)
    frames, width, local = o_in[0].shape
    dim = w_out.shape[0]
    fb = frames
    rows = frames * width
    return pl.pallas_call(
        functools.partial(project_kernel, patches),
        grid=(1,),
        in_specs=[smem()]
        + [pl.BlockSpec((fb, width, local), lambda i: (i, 0, 0))] * patches
        + [
            pl.BlockSpec((fb, width, dim), lambda i: (i, 0, 0)),
            full(w_out.shape),
            full(gain.shape),
            full(shift.shape),
        ],
        out_specs=[
            pl.BlockSpec((rows, dim), lambda i: (i, 0)),
            pl.BlockSpec((rows, dim), lambda i: (i, 0)),
            pl.BlockSpec((rows, dim), lambda i: (i, 0)),
        ],
        out_shape=[
            pltpu.HBM((rows, dim), F32),
            jax.ShapeDtypeStruct((rows, dim), BF),
            jax.ShapeDtypeStruct((rows, dim), BF),
        ],
        scratch_shapes=[pltpu.VMEM((patches, rows, local), BF)],
        compiler_params=params("arbitrary"),
        cost_estimate=cost(3.7),
        name="project",
    )(info, *o_in, tokens, w_out, gain, shift)


def tile_at(piece, steps):
    return lambda i, info: ((i % steps) * 2 + (info[0] & 1)) * 2 + (
        i // steps if piece is None else piece
    )


def pre_kernel(info_ref, dy_own, dy_mate, down_ref, dg_ref):
    half = dy_own.shape[0]
    dg_ref[:half] = nt(dy_own[...], down_ref[...]).astype(BF)
    dg_ref[half:] = nt(dy_mate[...], down_ref[...]).astype(BF)


def pre_call(info, dy_own, dy_mate, w_down, patches):
    half, dim = dy_own.shape
    hidden = w_down.shape[0]
    tile, steps = hidden // patches // 2, patches // 2
    at = tile_at(None, steps)
    return pl.pallas_call(
        pre_kernel,
        grid_spec=pltpu.PrefetchScalarGridSpec(
            num_scalar_prefetch=1,
            grid=(2 * steps,),
            in_specs=[full((half, dim))] * 2
            + [pl.BlockSpec((tile, dim), lambda i, info: (at(i, info), 0))],
            out_specs=pl.BlockSpec((2 * half, tile), lambda i, info: (0, i)),
        ),
        out_shape=pltpu.HBM((2 * half, hidden // 2), BF),
        compiler_params=params("arbitrary"),
        cost_estimate=cost(8.5),
        name="pre",
    )(info, dy_own, dy_mate, w_down)


def ffn_kernel(
    info_ref, h_own, h_mate, dy_own, dy_mate, dg_ref, up_ref,
    g_ref, du_ref, keep0, send0, keep1, send1, dh_own, dh_mate, acc_ref,
):
    step = pl.program_id(0)
    half = h_own.shape[0]

    @pl.when(step == 0)
    def _():
        acc_ref[...] = jnp.zeros(acc_ref.shape, F32)

    w_up = up_ref[...]
    chunk = half // 2
    for n in range(4):
        h_ref = (h_own, h_mate)[n // 2]
        here = slice((n % 2) * chunk, (n % 2 + 1) * chunk)
        rows = slice(n * chunk, (n + 1) * chunk)
        u = nn(h_ref[here], w_up)
        cdf = 0.5 + 0.5 * lax.erf(u * math.sqrt(0.5))
        pdf = jnp.exp(u * u * -0.5) * (1.0 / math.sqrt(2.0 * math.pi))
        g = (u * cdf).astype(BF)
        du = (dg_ref[rows].astype(F32) * (cdf + u * pdf)).astype(BF)
        g_ref[rows] = g
        du_ref[rows] = du
        acc_ref[rows] += nt(du, w_up)
    total = tn(g_ref[:half], dy_own[...]) + tn(g_ref[half:], dy_mate[...])
    middle = total.shape[1] // 2
    part = total.shape[0] // 2
    for n, (keep_ref, send_ref) in enumerate(((keep0, send0), (keep1, send1))):
        value = total[:, n * middle : (n + 1) * middle]
        if n == 0:
            low, high = value[:part], value[part:]
        else:
            some = part // 2
            low = jnp.concatenate([value[:some], value[part : part + some]], axis=0)
            high = jnp.concatenate([value[some:part], value[part + some :]], axis=0)
        first = info_ref[info_ref.shape[0] - 2 + n] == 0
        blocked(keep_ref, jnp.where(first, low, high))
        blocked(send_ref, jnp.where(first, high, low))

    @pl.when(step == pl.num_programs(0) - 1)
    def _():
        dh_own[...] = acc_ref[:half]
        dh_mate[...] = acc_ref[half:].astype(BF)


def ffn_call(info, h_own, h_mate, dy_own, dy_mate, dg, w_up, patches):
    half, dim = h_own.shape
    hidden = w_up.shape[1]
    tile, steps = hidden // patches // 2, patches // 2
    at = tile_at(None, steps)
    column = pl.BlockSpec((2 * half, tile), lambda i, info: (0, i))
    return pl.pallas_call(
        ffn_kernel,
        grid_spec=pltpu.PrefetchScalarGridSpec(
            num_scalar_prefetch=1,
            grid=(2 * steps,),
            in_specs=[full((half, dim))] * 4
            + [column, pl.BlockSpec((dim, tile), lambda i, info: (0, at(i, info)))],
            out_specs=[
                column,
                column,
            ]
            + [pl.BlockSpec((dim // 256, tile // 2, 128), lambda i, info: (0, i, 0))] * 4
            + [
                full((half, dim)),
                full((half, dim)),
            ],
            scratch_shapes=[pltpu.VMEM((2 * half, dim), F32)],
        ),
        out_shape=[
            pltpu.HBM((2 * half, hidden // 2), BF),
            pltpu.HBM((2 * half, hidden // 2), BF),
        ]
        + [pltpu.HBM((dim // 256, hidden // 4, 128), BF)] * 4
        + [
            pltpu.HBM((half, dim), F32),
            jax.ShapeDtypeStruct((half, dim), BF),
        ],
        compiler_params=params("arbitrary"),
        cost_estimate=cost(25),
        name="ffn",
    )(info, h_own, h_mate, hbm(dy_own), hbm(dy_mate), hbm(dg), hbm(w_up))


def up_kernel(steps, tile, h_own, h_mate, du_ref, o_own, o_mate, da_own, da_mate, dw_ref):
    half = h_own.shape[0]
    step = pl.program_id(0)
    count = tile // 128

    def put(at, value):
        for n in range(value.shape[1] // 128):
            dw_ref[at + n] = value[:, n * 128 : (n + 1) * 128].astype(BF)

    @pl.when(step < steps)
    def _():
        value = tn(h_own[...], du_ref[:half]) + tn(h_mate[...], du_ref[half:])
        put(step * count, value)

    @pl.when(step == steps)
    def _():
        put(steps * count, tn(o_own[...], da_own[...]) + tn(o_mate[...], da_mate[...]))


def up_call(info, h_own, h_mate, du, o_own, o_mate, da_own, da_mate, patches, piece):
    half, dim = h_own.shape
    columns = du.shape[1] // 2
    steps = patches // 2
    tile = columns // steps
    shape = (columns // 128 + dim // 512, dim, 128)
    quarter = pl.BlockSpec((half, dim // 4), lambda i, info: (0, (info[0] & 1) * 2 + piece))

    def kernel(info_ref, *refs):
        up_kernel(steps, tile, *refs)

    return pl.pallas_call(
        kernel,
        grid_spec=pltpu.PrefetchScalarGridSpec(
            num_scalar_prefetch=1,
            grid=(steps + 1,),
            in_specs=[full((half, dim))] * 2
            + [
                pl.BlockSpec(
                    (2 * half, tile),
                    lambda i, info: (0, piece * steps + jnp.minimum(i, steps - 1)),
                )
            ]
            + [full((half, dim))] * 2
            + [quarter] * 2,
            out_specs=full(shape),
        ),
        out_shape=jax.ShapeDtypeStruct(shape, BF),
        compiler_params=params("arbitrary"),
        cost_estimate=cost(6),
        name="up",
    )(info, hbm(h_own), hbm(h_mate), hbm(du), hbm(o_own), hbm(o_mate), hbm(da_own), hbm(da_mate))


def down_kernel(info_ref, x1_ref, g0_ref, g1_ref, down0_ref, down1_ref, own_ref, mate_ref, acc_ref):
    step = pl.program_id(0)
    half = x1_ref.shape[0]

    @pl.when(step == 0)
    def _():
        acc_ref[:half] = x1_ref[...]
        acc_ref[half:] = jnp.zeros_like(x1_ref)

    for n in range(2):
        rows = slice(n * half, (n + 1) * half)
        acc_ref[rows] += nn(g0_ref[rows], down0_ref[...]) + nn(g1_ref[rows], down1_ref[...])

    @pl.when(step == pl.num_programs(0) - 1)
    def _():
        own_ref[...] = acc_ref[:half]
        mate_ref[...] = acc_ref[half:].astype(BF)


def down_call(info, x1, g, w_down, patches):
    half, dim = x1.shape
    hidden = w_down.shape[0]
    tile, steps = hidden // patches // 2, patches // 2
    first, second = tile_at(0, steps), tile_at(1, steps)
    return pl.pallas_call(
        down_kernel,
        grid_spec=pltpu.PrefetchScalarGridSpec(
            num_scalar_prefetch=1,
            grid=(steps,),
            in_specs=[
                full((half, dim)),
                pl.BlockSpec((2 * half, tile), lambda i, info: (0, i)),
                pl.BlockSpec((2 * half, tile), lambda i, info: (0, steps + i)),
                pl.BlockSpec((tile, dim), lambda i, info: (first(i, info), 0)),
                pl.BlockSpec((tile, dim), lambda i, info: (second(i, info), 0)),
            ],
            out_specs=[full((half, dim)), full((half, dim))],
            scratch_shapes=[pltpu.VMEM((2 * half, dim), F32)],
        ),
        out_shape=[
            pltpu.HBM((half, dim), F32),
            pltpu.HBM((half, dim), BF),
        ],
        compiler_params=params("arbitrary"),
        cost_estimate=cost(8.5),
        name="down",
    )(info, hbm(x1), hbm(g), hbm(g), hbm(w_down), hbm(w_down))


def mid_kernel(
    patches, info_ref, dh_ref, recv_ref, x1_ref, dy_ref, w_ref, gain_ref, dx_ref, da_ref, gs_ref,
    *do_refs,
):
    step = pl.program_id(0)
    fb, width, local = do_refs[0].shape
    hat, rstd = normalise(x1_ref[...])
    dh = dh_ref[...] + recv_ref[...].astype(F32)
    dx = dy_ref[...].astype(F32) + norm_back(dh, hat, rstd, gain_ref[...])
    dx_ref[...] = dx
    da = dx.astype(BF)
    da_ref[...] = da
    sums = jnp.concatenate(
        [jnp.sum(dh * hat, axis=0, keepdims=True), jnp.sum(dh, axis=0, keepdims=True)], axis=0
    )

    @pl.when(step == 0)
    def _():
        gs_ref[...] = sums

    @pl.when(step > 0)
    def _():
        gs_ref[...] += sums

    for j, do_ref in enumerate(do_refs):
        part = nt(da, w_ref[heads_rows(info_ref, j, local), :])
        do_ref[...] = part.astype(BF).reshape(fb, width, local)


def mid_call(info, dh, recv, x1, dy, w_out, gain, frames, patches):
    rows, dim = x1.shape
    width = rows // frames
    local = dim // patches
    fb = frames
    row = pl.BlockSpec((rows, dim), lambda i: (i, 0))
    return pl.pallas_call(
        functools.partial(mid_kernel, patches),
        grid=(1,),
        in_specs=[smem(), row, row, row, row, full(w_out.shape), full(gain.shape)],
        out_specs=[row, row, full((2, dim))]
        + [pl.BlockSpec((fb, width, local), lambda i: (i, 0, 0))] * patches,
        out_shape=[
            pltpu.HBM((rows, dim), F32),
            pltpu.HBM((rows, dim), BF),
            jax.ShapeDtypeStruct((2, dim), F32),
        ]
        + [pltpu.HBM((frames, width, local), BF)] * patches,
        compiler_params=params("arbitrary"),
        cost_estimate=cost(6),
        name="mid",
    )(info, hbm(dh), recv, hbm(x1), hbm(dy), hbm(w_out), gain)


def dwq_kernel(groups, pairs, *refs):
    hs = refs[:groups]
    ds = [refs[groups * (1 + p) : groups * (2 + p)] for p in range(pairs)]
    dw_ref, acc_ref = refs[groups * (1 + pairs) :]
    step = pl.program_id(0)

    @pl.when(step == 0)
    def _():
        acc_ref[...] = jnp.zeros(acc_ref.shape, F32)

    total = None
    for n, h_ref in enumerate(hs):
        fb, rows, dim = h_ref.shape
        d = jnp.concatenate([pair[n][...] for pair in ds], axis=2)
        part = tn(h_ref[...].reshape(fb * rows, dim), d.reshape(fb * rows, -1))
        total = part if total is None else total + part
    acc_ref[...] += total

    @pl.when(step == pl.num_programs(0) - 1)
    def _():
        blocked(dw_ref, acc_ref)


def frame_blocks(a, fb):
    return pl.BlockSpec((fb,) + a.shape[1:], lambda i: (i, 0, 0))


def dwq_call(hs, ds):
    groups, pairs = len(hs), len(ds)
    frames, _, dim = hs[0].shape
    fb = max(1, frames // 2 if frames <= 8 else frames // 8)
    flat = [a for d in ds for a in d]
    return pl.pallas_call(
        functools.partial(dwq_kernel, groups, pairs),
        grid=(frames // fb,),
        in_specs=[frame_blocks(a, fb) for a in (*hs, *flat)],
        out_specs=full((3 * pairs, dim, 128)),
        out_shape=pltpu.HBM((3 * pairs, dim, 128), BF),
        scratch_shapes=[pltpu.VMEM((dim, 384 * pairs), F32)],
        compiler_params=params("arbitrary"),
        cost_estimate=cost(7),
        name="dwq",
    )(*[hbm(a) for a in hs], *flat)


def dh_kernel(groups, pairs, width, *refs):
    ds = [refs[n * groups : (n + 1) * groups] for n in range(pairs)]
    w_ref, even_ref, odd_ref = refs[pairs * groups :]
    j = 0
    for n in range(groups):
        fb, rows, _ = ds[0][n].shape
        d = jnp.concatenate([ds[p][n][...] for p in range(pairs)], axis=2)
        dh = nt(d.reshape(fb * rows, -1), w_ref[...]).astype(BF).reshape(fb, rows, -1)
        for at in range(0, rows, width):
            out = odd_ref if j % 2 else even_ref
            out[j // 2] = dh[:, at : at + width]
            j += 1


def dh_call(ds, w_local, patches):
    pairs, groups = len(ds), len(ds[0])
    frames = ds[0][0].shape[0]
    rows = sum(a.shape[1] for a in ds[0])
    width = rows // patches
    dim = w_local.shape[0]
    fb = max(1, frames // 4 if frames <= 8 else frames // 16)
    shape = (patches // 2, frames, width, dim)
    block = pl.BlockSpec((patches // 2, fb, width, dim), lambda i: (0, i, 0, 0))
    return pl.pallas_call(
        functools.partial(dh_kernel, groups, pairs, width),
        grid=(frames // fb,),
        in_specs=[frame_blocks(a, fb) for d in ds for a in d] + [full(w_local.shape)],
        out_specs=[block, block],
        out_shape=[pltpu.HBM(shape, BF)] * 2,
        compiler_params=params("arbitrary"),
        cost_estimate=cost(5),
        name="dh",
    )(*[a for d in ds for a in d], w_local)


def last_kernel(a_ref, b_ref, x_ref, dx_ref, gain_ref, gt_ref, gs_ref):
    step = pl.program_id(0)
    hat, rstd = normalise(x_ref[...].astype(F32))
    dh = a_ref[...].astype(F32) + b_ref[...].astype(F32)
    gt_ref[...] = (dx_ref[...] + norm_back(dh, hat, rstd, gain_ref[...])).astype(BF)
    sums = jnp.concatenate(
        [jnp.sum(dh * hat, axis=0, keepdims=True), jnp.sum(dh, axis=0, keepdims=True)], axis=0
    )

    @pl.when(step == 0)
    def _():
        gs_ref[...] = sums

    @pl.when(step > 0)
    def _():
        gs_ref[...] += sums


def last_call(a, b, x, dx, gain):
    rows, dim = x.shape
    row = pl.BlockSpec((rows // 2, dim), lambda i: (i, 0))
    return pl.pallas_call(
        last_kernel,
        grid=(2,),
        in_specs=[row, row, row, row, full(gain.shape)],
        out_specs=[row, full((2, dim))],
        out_shape=[
            jax.ShapeDtypeStruct((rows, dim), BF),
            jax.ShapeDtypeStruct((2, dim), F32),
        ],
        compiler_params=params("arbitrary"),
        cost_estimate=cost(3),
        name="last",
    )(a, b, hbm(x), hbm(dx), gain)


class Chain:
    def __init__(self, hops):
        self.hops, self.value, self.got, self.begun, self.done = hops, None, None, False, False
        self.move = None

    def request(self):
        try:
            return self.hops.send(self.got) if self.begun else next(self.hops)
        except StopIteration as stop:
            self.value, self.done = stop.value, True
            return None
        finally:
            self.begun = True


class Move:
    def __init__(self, bit, members, got):
        self.bit, self.members, self.got = bit, members, got

    def settle(self, got):
        start = 0
        for chain, a in self.members:
            chain.move = None
            if len(self.members) == 1:
                chain.got = got
            elif self.bit == "patch":
                chain.got = got[start : start + a.shape[0]]
                start += a.shape[0]
            else:
                n = a.size // 128
                chain.got = got[start : start + n].reshape(a.shape)
                start += n


class Stage:
    def __init__(self, links):
        self.links = links

    def start(self, *chains):
        wanted = {}
        for chain in chains:
            if chain.done or chain.move is not None:
                continue
            request = chain.request()
            if request is not None:
                wanted.setdefault(request[0], []).append((chain, request[1]))
        for bit, members in wanted.items():
            arrays = [a for _, a in members]
            if bit == "patch":
                sent = arrays[0] if len(arrays) == 1 else jnp.concatenate(arrays, axis=0)
                got = lax.all_to_all(sent, "patch", 1, 1, tiled=True)
            elif len(arrays) == 1:
                got = self.links.swap(arrays[0], bit)
            else:
                sent = jnp.concatenate([a.reshape(-1, 128) for a in arrays], axis=0)
                got = self.links.swap(sent, bit)
            move = Move(bit, members, got)
            for chain, _ in members:
                chain.move = move

    def join(self, values, *chains):
        moves = []
        for chain in chains:
            if chain.move is not None and chain.move not in moves:
                moves.append(chain.move)
        held, values = lax.optimization_barrier(([m.got for m in moves], values))
        for move, got in zip(moves, held):
            move.settle(got)
        return values


class Links:
    def __init__(self, batches, patches):
        self.batches, self.patches = batches, patches
        self.patch = lax.axis_index("patch")
        self.batch = lax.axis_index("batch")
        self.bits = {"c": [("p", 1)], "y": [("b", 1)], "x": [], "z": []}
        bit = 2
        while bit < patches:
            self.bits["x"].append(("p", bit))
            bit *= 2
        bit = 2
        while bit < batches:
            self.bits["z"].append(("b", bit))
            bit *= 2

    def swap(self, a, bit):
        axis, step = bit
        step = step if axis == "p" else step * self.patches
        n = self.batches * self.patches
        return lax.ppermute(a, AXES, [(i, i ^ step) for i in range(n)])

    def swap_patch(self, a, bit):
        return self.swap(a, ("p", bit))

    def mine(self, bit):
        axis, step = bit
        return ((self.patch if axis == "p" else self.batch) // step) & 1

    def expand(self, order):
        if not isinstance(order, str):
            return order
        bits = []
        for axis in order:
            one = self.bits[axis.lower()]
            bits += one if axis.islower() else one[::-1]
        return bits

    def hops(self, a, axes, order, back, trade, layout, first, raw):
        if first is not None:
            got = yield first
            a = (a.astype(F32) + got.astype(F32)).astype(BF)
        names = list(self.expand(axes))
        blocks, rows, _ = a.shape
        a = a.reshape((blocks,) + (2,) * len(names) + (rows // 2 ** len(names), 128))
        layout = self.expand(layout)
        for bit in self.expand(order):
            at = names.index(bit) + 1
            names.pop(at - 1)
            got = yield bit, lax.dynamic_index_in_dim(a, 1 - self.mine(bit), at, keepdims=False)
            keep = lax.dynamic_index_in_dim(a, self.mine(bit), at, keepdims=False)
            a = (keep.astype(F32) + got.astype(F32)).astype(BF)
        if trade is not None and trade != "patch":
            bit = ("p", 1)
            size = a.shape[1:]
            pairs = a[:trade].reshape((trade // 2, 2) + size)
            got = yield bit, lax.dynamic_index_in_dim(pairs, 1 - self.mine(bit), 1, keepdims=False)
            own = lax.dynamic_index_in_dim(pairs, self.mine(bit), 1, keepdims=False)
            a = jnp.concatenate([self.join(own, got, bit, 0).reshape((trade,) + size), a[trade:]])
        if trade == "patch":
            a = a.reshape((blocks, self.patches) + a.shape[-2:])
            a = yield "patch", a
            a = a.reshape((blocks * self.patches,) + a.shape[-2:])
        have = []
        for bit in self.expand(back):
            got = yield bit, a
            at = 1 + sum(layout.index(other) < layout.index(bit) for other in have)
            have.append(bit)
            if raw and len(have) == len(self.expand(back)):
                return a, got
            a = self.join(a, got, bit, at)
        return a.reshape(a.shape[0], -1, 128)

    def join(self, a, got, bit, at):
        return jnp.where(
            self.mine(bit) == 0, jnp.stack([a, got], axis=at), jnp.stack([got, a], axis=at)
        )

    def chain(self, a, axes, order, back, trade=None, layout="yz", first=None, raw=False):
        return Chain(self.hops(a, axes, order, back, trade, layout, first, raw))

    def apart(self, a):
        got = {0: a}
        bit = self.patches // 2
        while bit > 1:
            for j in sorted(got):
                got[j | bit] = self.swap_patch(got[j], bit)
            bit //= 2
        return got

    def items(self, a):
        got = self.apart(a)
        for j in sorted(got):
            got[j | 1] = self.swap_patch(got[j], 1)
        return got

    def deal(self, parts):
        return [parts[0]] + [self.swap_patch(parts[j], j) for j in range(1, self.patches)]


def assemble_q_kernel(order, valid, info_ref, mine_ref, got_ref, out):
    own = info_ref[info_ref.shape[0] - 2] == pl.program_id(0)
    pieces = [jnp.where(own, mine_ref[b], got_ref[b])[:, :valid].astype(F32) for b in order]
    out[...] = jnp.concatenate(pieces, axis=1)


def assemble_q(info, pair, order, valid):
    mine, got = (a.reshape(a.shape[0], -1, 128) for a in pair)
    blocks, rows, _ = mine.shape
    return pl.pallas_call(
        functools.partial(assemble_q_kernel, order, valid),
        grid=(2,),
        in_specs=[smem()] + [full(mine.shape)] * 2,
        out_specs=pl.BlockSpec((rows, len(order) * valid), lambda i: (i, 0)),
        out_shape=jax.ShapeDtypeStruct((2 * rows, len(order) * valid), F32),
        compiler_params=params("arbitrary"),
        cost_estimate=cost(2),
        name="assemble_q",
    )(info, mine, got)


def assemble_w_kernel(ups, wos, info_ref, *refs):
    up_ref, wo_ref = refs[4:]
    count = info_ref.shape[0]
    y, z = pl.program_id(0) // 2, pl.program_id(0) % 2
    own_y = info_ref[count - 2] == y
    own_z = info_ref[count - 1] == z

    def block(n, b):
        if n == 0:
            return jnp.where(own_z, refs[0][b, y], refs[1][b, y]).astype(F32)
        return jnp.where(own_y, refs[2][b, z], refs[3][b, z]).astype(F32)

    for ref, order in ((up_ref, ups), (wo_ref, wos)):
        for at, (n, b) in enumerate(order):
            ref[:, at * 128 : (at + 1) * 128] = block(n, b)


def assemble_w(info, first, second, ups, wos):
    arrays = [a.reshape(a.shape[0], 2, -1, 128) for a in (*first, *second)]
    rows = arrays[0].shape[2]
    return pl.pallas_call(
        functools.partial(assemble_w_kernel, ups, wos),
        grid=(4,),
        in_specs=[smem()] + [full(a.shape) for a in arrays],
        out_specs=[
            pl.BlockSpec((rows, len(order) * 128), lambda i: (i, 0)) for order in (ups, wos)
        ],
        out_shape=[
            jax.ShapeDtypeStruct((4 * rows, len(order) * 128), F32) for order in (ups, wos)
        ],
        compiler_params=params("arbitrary"),
        cost_estimate=cost(3),
        name="assemble_w",
    )(info, *arrays)


def pieces_kernel(steps, a_ref, out):
    piece = pl.program_id(0) // steps
    blocks = a_ref.shape[0] // 2

    def put(n):
        for b in range(blocks):
            out[:, b * 128 : (b + 1) * 128] = a_ref[2 * b + n].astype(F32)

    for n in range(2):
        pl.when(piece == n)(functools.partial(put, n))


def pieces_call(a):
    blocks, rows, _ = a.shape
    step = min(rows, 128)
    steps = rows // step
    return pl.pallas_call(
        functools.partial(pieces_kernel, steps),
        grid=(2 * steps,),
        in_specs=[pl.BlockSpec((blocks, step, 128), lambda i: (0, i % steps, 0))],
        out_specs=pl.BlockSpec((step, blocks * 64), lambda i: (i, 0)),
        out_shape=jax.ShapeDtypeStruct((2 * rows, blocks * 64), F32),
        compiler_params=params("arbitrary"),
        cost_estimate=cost(4),
        name="pieces",
    )(a)


def tables(code, times):
    head = 64
    half = head // 6
    band = 2 * half
    dims = jnp.arange(head)
    freq = jnp.power(THETA, -2.0 * (dims % half).astype(F32) / band)
    places = jnp.stack([times, (code // GRID).astype(F32), (code % GRID).astype(F32)], axis=-1)
    which = jnp.minimum(dims // band, 2)
    pick = jnp.where(
        which == 0, places[..., 0:1], jnp.where(which == 1, places[..., 1:2], places[..., 2:3])
    )
    angle = pick * freq
    turned = dims < 3 * band
    cos = jnp.where(turned, jnp.cos(angle), 1.0)
    sin = jnp.where(turned, jnp.sin(angle) * jnp.where(dims % band < half, -1.0, 1.0), 0.0)
    return jnp.concatenate([cos, cos, sin, sin], axis=-1)


def per_device(
    batches, patches, tokens, cotangent, episode_frames, kinds, patch_pos,
    ln1_gain, ln1_shift, w_qkv, w_out, ln2_gain, ln2_shift, w_up, w_down,
):
    tokens = tokens[0]
    frames, width, dim = tokens.shape
    rows = frames * width
    local = dim // patches
    links = Links(batches, patches)
    me = links.patch
    core = me & 1
    gain1, shift1, gain2, shift2 = (
        a.astype(F32).reshape(1, dim) for a in (ln1_gain, ln1_shift, ln2_gain, ln2_shift)
    )
    dy = cotangent.reshape(rows, dim)

    code = jnp.where(kinds[0] == 0, patch_pos[0], 0)
    codes = links.items(code)
    mate = links.swap_patch(tokens, 1)
    dy_mate = links.swap_patch(dy, 1)
    apart = links.apart(tokens)
    ends = jnp.cumsum(episode_frames[0])
    frame_ids = jnp.arange(frames, dtype=jnp.int32)
    starts = jnp.max(
        jnp.where(ends[None, :] <= frame_ids[:, None], ends[None, :], 0), axis=1
    )
    firsts = [links.mine(bits[0])[None] for bits in (links.bits["y"], links.bits["z"])]
    info = jnp.concatenate([me[None], starts, *firsts]).astype(jnp.int32)
    pad = max(128, local)
    pairs = pad // 128
    valid = min(128, local)
    if valid == 128:
        w_local = columns_call(info, w_qkv, pairs)
    else:
        columns = []
        for n in range(3):
            at = n * dim + me * local
            columns.append(lax.dynamic_slice(w_qkv, (jnp.int32(0), at), (dim, valid)))
            columns.append(jnp.zeros((dim, 128 - valid), BF))
        w_local = jnp.concatenate(columns, axis=1)

    members = [[0, 1], list(range(2, patches))]
    css = []
    for group in members:
        place = jnp.concatenate([codes[j] for j in group], axis=1)
        times = jnp.broadcast_to(frame_ids.astype(F32)[:, None], place.shape)
        css.append(tables(place, times))
    near = qkv_call([tokens, mate], css[0], w_local, gain1, shift1)
    dg = pre_call(info, dy, dy_mate, w_down, patches)
    near, dg, apart, css = lax.optimization_barrier((near, dg, apart, css))
    far_items = []
    for j in range(2, patches, 2):
        far_items += [apart[j], links.swap_patch(apart[j], 1)]
    far = qkv_call(far_items, css[1], w_local, gain1, shift1)
    hs, qkvs = [near[0], far[0]], [near[1], far[1]]

    *o_send, o_full, lse = attend_call(info, qkvs, patches)
    o_in = links.deal([a[..., :local] for a in o_send])
    x1, h2, o_own = project_call(info, o_in, tokens, w_out, gain2, shift2)
    h2_mate = links.swap_patch(h2, 1)
    o_mate = links.swap_patch(o_own, 1)
    stage = Stage(links)
    g, du, keep0, send0, keep1, send1, dh_own, dh_mate = ffn_call(
        info, h2, h2_mate, dy, dy_mate, dg, w_up, patches
    )
    inner, outer = links.bits["z"][:1], links.bits["z"][1:]
    ys, xs = links.bits["y"], links.bits["x"]

    def two_pieces(a):
        return a.reshape(a.shape[0] * 2, a.shape[1] // 2, 128)

    def step(held, *chains):
        held = stage.join(held, *chains)
        for chain in chains:
            stage.start(chain)
        return held

    def finish(held, *chains):
        while not all(c.done for c in chains):
            held = step(held, *chains)
        return held

    d1 = links.chain(two_pieces(keep0), xs[::-1] + inner + outer, inner, "", first=(ys[0], two_pieces(send0)))
    d2 = links.chain(two_pieces(keep1), xs[::-1] + ys + outer, ys, "", first=(inner[0], two_pieces(send1)))
    stage.start(d1)
    stage.start(d2)
    dh_recv = links.swap_patch(dh_mate, 1)
    dx1, da, sums2, *d_o = mid_call(
        info, dh_own, dh_recv, x1, dy, w_out, gain2, frames, patches
    )
    da_mate = links.swap_patch(da, 1)
    do_in = links.deal(d_o)
    sides = (o_own, o_mate, da, da_mate)
    dw1 = up_call(info, h2, h2_mate, du, *sides, patches, 0)
    dw2 = up_call(info, h2, h2_mate, du, *sides, patches, 1)
    out_own, out_mate = down_call(info, x1, g, w_down, patches)
    do_in, dw1, dw2, out_own, out_mate = step((do_in, dw1, dw2, out_own, out_mate), d1, d2)
    out_recv = links.swap_patch(out_mate, 1)
    u1 = links.chain(dw1, "Xcyz", xs + inner + ys, "")
    u2 = links.chain(dw2, "Xcyz", ys + xs + inner, "")
    stage.start(u1)
    if pad > local:
        do_in = [jnp.pad(a, ((0, 0), (0, 0), (0, pad - local))) for a in do_in]
    dqkv = attend_back_call(info, qkvs, css, do_in, o_full, lse, patches, 0)
    dqkv, do_in = step((dqkv, do_in), d1, d2)
    dqkv = finish(dqkv, d1, d2)
    dqkvs = [dqkv]
    d = links.chain(
        jnp.concatenate([d1.value, d2.value], axis=0),
        xs[::-1] + outer,
        xs + outer,
        outer[::-1] + inner + ys,
    )
    stage.start(d)
    stage.start(u2)
    for pair in range(1, pairs):
        dqkvs.append(attend_back_call(info, qkvs, css, do_in, o_full, lse, patches, pair))
    dwq = dwq_call(hs, dqkvs)
    even, odd = dh_call(dqkvs, w_local, patches)
    odd, even, dwq = stage.join((odd, even, dwq), u1, d, u2)
    q = links.chain(dwq, "Xcyz", "yz", "zy", "patch", raw=True)
    for chain in (q, u1, d, u2):
        stage.start(chain)
    odd = links.swap_patch(odd, 1)
    odd, even, sums2 = step((odd, even, sums2), u1)
    slots = (even.astype(F32) + odd.astype(F32)).astype(BF)
    bit = patches // 2
    while bit > 2:
        n = slots.shape[0] // 2
        slots = (slots[:n].astype(F32) + links.swap_patch(slots[n:], bit).astype(F32)).astype(BF)
        bit //= 2
    got = links.swap_patch(slots[1], 2)
    sums2 = step(sums2, q)
    sums2 = step(sums2, u2, d)
    sums2 = step(sums2, u1, u2)
    sums2 = finish(sums2, u1, u2)
    w = jnp.concatenate([u1.value, u2.value], axis=0)
    w = w.reshape(2 * w.shape[0], -1, 128)
    w = links.chain(w, outer, outer, outer[::-1], w.shape[0])
    stage.start(w)
    sums2 = step(sums2, q)
    sums2 = step(sums2, d)
    sums2 = step(sums2, w)
    slots, got, sums2 = step((slots, got, sums2), q)
    sums2 = step(sums2, w)
    sums2 = step(sums2, d)
    grad_tokens, sums1 = last_call(
        slots[0].reshape(rows, dim), got.reshape(rows, dim), tokens.reshape(rows, dim), dx1, gain1
    )
    sums = jnp.concatenate([sums1, sums2], axis=0)
    sums = step(sums, q)
    sums = step(sums, w)
    sums = finish(sums, w)
    half = w.value.shape[0] // 2
    wa = links.chain(w.value[:half], [], [], ys + inner, raw=True)
    wb = links.chain(w.value[half:], [], [], inner + ys, raw=True)
    stage.start(wa)
    stage.start(wb)
    sums, out_own, out_recv = step((sums, out_own, out_recv), q)
    out = (out_own + out_recv.astype(F32)).astype(BF)
    sums = sums.reshape(4, patches, local).transpose(1, 0, 2)
    sums = jnp.broadcast_to(sums[None], (batches,) + sums.shape)
    sums = lax.all_to_all(sums.reshape((-1,) + sums.shape[2:]), AXES, 0, 0, tiled=True)
    held = step(grad_tokens, wa, wb)
    held = step(held, q)
    held = step(held, d)
    held, sums = step((held, sums), wa, wb)
    grad_tokens = step(held, q)
    sums = jnp.sum(sums, axis=0)
    grad_tokens = finish(grad_tokens, wa, wb)
    grad_tokens = finish(grad_tokens, q)
    grad_tokens = finish(grad_tokens, d)
    down = pieces_call(d.value)

    nx = patches // 2
    each = dw1.shape[0]
    per = (each - dim // 512) // nx
    ups, wos = [], []
    for owner in range(2):
        for n in range(2):
            wos += [(owner, n * each + nx * per + t) for t in range(dim // 512)]
    for i in range(nx):
        for owner in range(2):
            for n in range(2):
                ups += [(owner, n * each + i * per + t) for t in range(per)]
    up, grad_wo = assemble_w(info, wa.value, wb.value, ups, wos)
    order = []
    for n in range(3):
        for p in range(patches):
            order += [(pair * 3 + n) * patches + p for pair in range(pairs)]
    qkv = assemble_q(info, q.value, order, valid)

    return (
        out.reshape(1, frames, width, dim),
        grad_tokens.reshape(1, frames, width, dim),
        sums[0],
        sums[1],
        qkv,
        grad_wo,
        sums[2],
        sums[3],
        up,
        down,
    )


def solution(mesh):
    placed = (
        P("batch", None, "patch", None),
        P("batch", None, "patch", None),
        P("batch", None),
        P("batch", None, "patch"),
        P("batch", None, "patch"),
    ) + (P(),) * 8
    return jax.shard_map(
        functools.partial(per_device, mesh.shape["batch"], mesh.shape["patch"]),
        mesh=mesh,
        in_specs=placed,
        out_specs=(
            P("batch", None, "patch", None),
            P("batch", None, "patch", None),
            P("patch"),
            P("patch"),
            P("patch", None),
            P("patch", None),
            P("patch"),
            P("patch"),
            P("patch", None),
            P("patch", None),
        ),
        check_vma=False,
    )
```
